32 devices in a mesh: pair: 16 (over z, y, core), proj: 2 (over x).
Axes of the slice: x: 2, y: 2, z: 4, core: 2. Of those that a mesh axis runs over, the one named last changes fastest.
Arguments:
- val_orbitals: bfloat16 [128, 24576], P(('pair', 'proj')), may hold values from -6 to 6
- cond_orbitals: bfloat16 [512, 24576], P(('pair', 'proj')), may hold values from -6 to 6
- val_energy: float32 [128], P(('pair', 'proj')), may hold values from -1 to -0.25
- cond_energy: float32 [512], P(('pair', 'proj')), may hold values from 0.25 to 16
- val_slot: int32 [2048], P(('pair', 'proj')), may hold values from 0 to 3
- cond_slot: int32 [2048], P(('pair', 'proj')), may hold values from 0 to 15
- eigenvectors: bfloat16 [24576, 2048], P('proj', 'pair'), may hold values from -0.0390625 to 0.0390625
- frequencies: float32 [4], replicated, may hold values from 0.5 to 16
Outputs:
- chi_sub: float32 [2048, 4, 2048], P('pair', None, 'proj')
The draws below stay inside these ranges and needn't reach their ends.
All inputs are finite; a program needn't handle non-finite values.
Results may differ from the reference program's by a relative error of at most 0.0045.
Values may be sent and summed in bfloat16 or wider, within the bound.
No kernel may reach another device: no remote copies, remote signals or barrier semaphores. Data moves between devices by JAX's collectives and lax.ppermute only.
A program may use at most 192 MiB of HBM per device.

```python
import math
import jax
import jax.numpy as jnp
from jax import lax

NG = 24576
NS = 2048
NF = 4
PD = 64
V_DEV = 4
C_DEV = 16
PAIRS = 2048
NV = 128
NC = 512
N_PAIR = 16
N_PROJ = 2


def draw_cond_energy(key, part):
    key = jax.random.fold_in(key, 5)
    uniform_part = jax.random.uniform(key, (NC,), jnp.float32, 0.0, 1.0)
    return 0.25 * jnp.power(64.0, uniform_part)


def draw_frequencies(key, part):
    key = jax.random.fold_in(key, 11)
    jitter = jax.random.uniform(key, (NF,), jnp.float32, 0.0, 0.25)
    places = jnp.arange(NF, dtype=jnp.float32)
    exponent = -1.0 + 4.75 * places / (NF - 1) + jitter
    return jnp.power(2.0, exponent)


def set_ends(drawn, key, low, largest):
    index_at = [jax.random.randint(jax.random.fold_in(key, axis), (), 0, length) for axis, length in enumerate(drawn.shape)]
    widest = drawn.shape.index(max(drawn.shape))
    neighbour = index_at[:widest] + [(index_at[widest] + 1) % drawn.shape[widest]] + index_at[widest + 1:]
    return drawn.at[tuple(index_at)].set(low).at[tuple(neighbour)].set(largest)


def level_of(stream_key, dims, pieces, smallest, largest):
    def one(axis_at, parts):
        steps = jax.random.uniform(jax.random.fold_in(jax.random.fold_in(stream_key, 6), axis_at), (parts,), jnp.float32, smallest / len(pieces), largest / len(pieces))
        return jnp.repeat(jnp.exp(steps), dims[axis_at] // parts).reshape((-1,) + (1,) * (len(dims) - axis_at - 1))

    level = one(*pieces[0])
    for cut in pieces[1:]:
        level = level * one(*cut)
    return level


def gaussian(key, shape, scale, reach, cuts=(), held_as=jnp.bfloat16):
    drawn = scale * jax.random.normal(key, shape, jnp.float32)
    if cuts:
        drawn = drawn * level_of(key, shape, cuts, -0.22, 0.18)
    return jnp.clip(drawn, -reach, reach).astype(held_as)


def setup_inputs(seed: int = 0) -> dict:
    arg_keys = jax.random.split(jax.random.key(seed), 9)
    return {
        "val_orbitals": gaussian(arg_keys[0], (NV, NG), 1.0, 6.0, ((0, 32),)),
        "cond_orbitals": gaussian(arg_keys[1], (NC, NG), 1.0, 6.0, ((0, 32),)),
        "val_energy": jnp.clip(-1.0 + 0.75 * jax.random.uniform(arg_keys[2], (NV,), jnp.float32) ** level_of(arg_keys[2], (NV,), ((0, 32),), -0.2, 0.2), -1.0, -0.25),
        "cond_energy": draw_cond_energy(jax.random.fold_in(arg_keys[8], 71), 0),
        "val_slot": set_ends(jax.random.randint(arg_keys[4], (PAIRS,), 0, V_DEV), jax.random.fold_in(arg_keys[4], 1), 0, V_DEV - 1).astype(jnp.int32),
        "cond_slot": set_ends(jax.random.randint(arg_keys[5], (PAIRS,), 0, C_DEV), jax.random.fold_in(arg_keys[5], 1), 0, C_DEV - 1).astype(jnp.int32),
        "eigenvectors": gaussian(arg_keys[6], (NG, NS), NG ** -0.5, 0.0390625, ((0, 2), (1, 16))),
        "frequencies": draw_frequencies(jax.random.fold_in(arg_keys[8], 71), 0),
    }


def reference(val_orbitals, cond_orbitals, val_energy, cond_energy, val_slot, cond_slot, eigenvectors, frequencies):
    blocks = N_PAIR * N_PROJ
    val_blocks = val_orbitals.reshape(blocks, V_DEV, NG)
    cond_blocks = cond_orbitals.reshape(blocks, C_DEV, NG)
    val_levels = val_energy.reshape(blocks, V_DEV)
    cond_levels = cond_energy.reshape(blocks, C_DEV)
    val_index = val_slot.reshape(blocks, PD)
    cond_index = cond_slot.reshape(blocks, PD)

    def one_block(pair_entries):
        valence_orbital_rows, conduction_orbital_rows, valence_energies, conduction_energies, valence_choice_index, conduction_choice_index = pair_entries
        valence_row_block = jnp.take(valence_orbital_rows, valence_choice_index, axis=0).astype(jnp.float32)
        crows = jnp.take(conduction_orbital_rows, conduction_choice_index, axis=0).astype(jnp.float32)
        density = (valence_row_block * crows).astype(jnp.bfloat16)
        coeffs = jnp.dot(density, eigenvectors, preferred_element_type=jnp.float32).astype(jnp.bfloat16)
        energy_difference = jnp.take(conduction_energies, conduction_choice_index) - jnp.take(valence_energies, valence_choice_index)
        weights = (4.0 * energy_difference[:, None] / (energy_difference[:, None] ** 2 + frequencies[None, :] ** 2)).astype(jnp.bfloat16)
        return (coeffs, weights)
    coeffs, weights = lax.map(one_block, (val_blocks, cond_blocks, val_levels, cond_levels, val_index, cond_index))
    group_rows = PD * N_PROJ
    coeffs = coeffs.reshape(N_PAIR, group_rows, NS)
    weights = weights.reshape(N_PAIR, group_rows, NF)

    def accumulate(total, pair_entries):
        cblock, wblock = pair_entries
        weighted = (cblock.astype(jnp.float32)[:, None, :] * wblock.astype(jnp.float32)[:, :, None]).astype(jnp.bfloat16)
        weighted = weighted.reshape(group_rows, NF * NS)
        return (total + lax.dot_general(cblock, weighted, (((0,), (0,)), ((), ())), preferred_element_type=jnp.float32), None)
    total, unused = lax.scan(accumulate, jnp.zeros((NS, NF * NS), jnp.float32), (coeffs, weights))
    factor = -1.0 / math.sqrt(PAIRS)
    return (total * factor).reshape(NS, NF, NS)
```

```python
import math

import jax
import jax.numpy as jnp
from jax import lax
from jax.sharding import PartitionSpec as P

LANES = 128


def local(
    val_orbitals,
    cond_orbitals,
    val_energy,
    cond_energy,
    val_slot,
    cond_slot,
    eigenvectors,
    frequencies,
):
    val_count, n_grid = val_orbitals.shape
    cond_count = cond_orbitals.shape[0]
    per_dev = val_slot.shape[0]
    n_freq = frequencies.shape[0]
    n_proj = lax.axis_size("proj")
    n_pair = lax.axis_size("pair")
    x = lax.axis_index("proj")
    part = n_grid // n_proj
    segs = cond_count // val_count
    seg = part // segs
    combos = val_count * cond_count
    columns = eigenvectors.shape[1]
    fold = n_pair // n_proj

    gap = cond_energy[:, None] - val_energy[None, :]
    weights = (
        4.0 * gap[:, :, None] / (gap[:, :, None] ** 2 + frequencies[None, None, :] ** 2)
    ).astype(jnp.bfloat16)
    chosen = (cond_slot[:, None, None] == jnp.arange(cond_count, dtype=jnp.int32)[None, :, None]) & (
        val_slot[:, None, None] == jnp.arange(val_count, dtype=jnp.int32)[None, None, :]
    )
    counts = jnp.sum(chosen.astype(jnp.float32), axis=0).astype(jnp.bfloat16)
    extra = jnp.concatenate([weights, counts[:, :, None]], axis=2).reshape(
        cond_count, val_count * (n_freq + 1)
    )
    extra = jnp.pad(extra, ((0, 0), (0, LANES - extra.shape[1])))

    def packed(place):
        cond_part = lax.dynamic_slice_in_dim(cond_orbitals, place * part, part, 1)
        val_part = lax.dynamic_slice_in_dim(val_orbitals, place * part, part, 1)
        val_part = val_part.reshape(val_count, segs, seg).transpose(1, 0, 2)
        return jnp.concatenate([cond_part, val_part.reshape(cond_count, seg), extra], axis=1)

    pieces = [packed(x)]
    for k in range(1, n_proj):
        to_send = packed((x + k) % n_proj)
        pieces.append(
            lax.ppermute(to_send, "proj", [(s, (s + k) % n_proj) for s in range(n_proj)])
        )
    eig = eigenvectors.reshape(segs, seg, columns)
    running = None
    scales = []
    for k in range(n_proj):
        got = lax.all_gather(pieces[k], "pair", axis=0, tiled=True)
        got = got.reshape(n_pair, cond_count, part + seg + LANES)
        cond_rows = got[:, :, :part].reshape(n_pair, cond_count, segs, seg)
        val_rows = got[:, :, part : part + seg].reshape(n_pair, segs, val_count, seg)
        density = (
            cond_rows.astype(jnp.float32)[:, None]
            * val_rows.transpose(0, 2, 1, 3).astype(jnp.float32)[:, :, None]
        ).astype(jnp.bfloat16)
        sums = lax.dot_general(
            density.reshape(n_pair * combos, part),
            eigenvectors,
            (((1,), (0,)), ((), ())),
            preferred_element_type=jnp.float32,
        )
        if running is not None:
            sums = sums + running
        if k < n_proj - 1:
            running = lax.ppermute(
                sums, "proj", [(s, (s + 1) % n_proj) for s in range(n_proj)]
            )
        scales.append(got[:, :, part + seg : part + seg + val_count * (n_freq + 1)])
    coeffs = sums.astype(jnp.bfloat16)

    perm = []
    for j in range(n_pair):
        for s in range(n_proj):
            source = j * n_proj + s
            perm.append((source, (j % fold + fold * s) * n_proj + j // fold))
    share = lax.ppermute(coeffs, ("pair", "proj"), perm)
    right = lax.all_gather(share, "pair", axis=0, tiled=True)
    right = right.reshape(n_proj, fold, n_pair * combos, columns)

    own = [coeffs]
    for k in range(1, n_proj):
        own.append(
            lax.ppermute(coeffs, "proj", [(s, (s + k) % n_proj) for s in range(n_proj)])
        )
    factor = -1.0 / math.sqrt(per_dev * n_pair * n_proj)
    total = None
    left, rights = [], []
    for k in range(n_proj):
        place = (x - k + n_proj) % n_proj
        rows = own[k].astype(jnp.float32).reshape(n_pair, val_count, cond_count, columns)
        scale = scales[(k - 1) % n_proj].astype(jnp.float32)
        scale = scale.reshape(n_pair, cond_count, val_count, n_freq + 1).transpose(0, 2, 1, 3)
        scale = scale[..., :n_freq] * scale[..., n_freq:]
        weighted = (rows[..., None] * scale[:, :, :, None, :]).astype(jnp.bfloat16)
        left.append(weighted.reshape(n_pair * combos, columns * n_freq))
        rights.append(lax.dynamic_index_in_dim(right, place, 0, keepdims=False))
    left = jnp.concatenate(left, axis=0)
    rights = jnp.concatenate(rights, axis=1)
    chi = lax.dot_general(
        left, rights, (((0,), (1,)), ((), ())), preferred_element_type=jnp.float32
    )
    return (chi * factor).reshape(columns, n_freq, fold * columns)


def solution(mesh):
    return jax.shard_map(
        local,
        mesh=mesh,
        in_specs=(
            P(("pair", "proj"), None),
            P(("pair", "proj"), None),
            P(("pair", "proj")),
            P(("pair", "proj")),
            P(("pair", "proj")),
            P(("pair", "proj")),
            P("proj", "pair"),
            P(),
        ),
        out_specs=P("pair", None, "proj"),
        check_vma=False,
    )
```

```python
import functools
import math

import jax
import jax.numpy as jnp
from jax import lax
from jax.experimental import pallas as pl
from jax.experimental.pallas import tpu as pltpu
from jax.sharding import PartitionSpec as P

LANES = 128

def project_kernel(segs, val_count, cond_count, with_running, *refs):
    conds = refs[:segs]
    val = refs[segs]
    eigs = refs[segs + 1 : 2 * segs + 1]
    rest = refs[2 * segs + 1 :]
    running = rest[0] if with_running else None
    out, density, total = rest[-3:]
    blocks = val.shape[0] // cond_count
    combos = val_count * cond_count

    @pl.when(pl.program_id(0) == 0)
    def _():
        if with_running:
            total[...] = running[...]
        else:
            total[...] = jnp.zeros_like(total)

    for k in range(segs):

        @pl.loop(0, blocks)
        def _(j):
            rows = pl.ds(pl.multiple_of(j * cond_count, cond_count), cond_count)
            c = conds[k][rows, :].astype(jnp.float32)
            vals = val[rows, :].astype(jnp.float32)
            for v in range(val_count):
                at = k * val_count + v
                product = (c * vals[at : at + 1, :]).astype(jnp.bfloat16)
                start = pl.multiple_of(j * combos + v * cond_count, cond_count)
                density[pl.ds(start, cond_count), :] = product

        total[...] += jnp.dot(density[...], eigs[k][...], preferred_element_type=jnp.float32)

    @pl.when(pl.program_id(0) == pl.num_programs(0) - 1)
    def _():
        out[...] = total[...].astype(out.dtype)


def project(packed_rows, eigenvectors, running, val_count, cond_count, out_type):
    part, columns = eigenvectors.shape
    segs = cond_count // val_count
    seg = part // segs
    rows = packed_rows.shape[0]
    width = math.gcd(seg, 768)
    steps = seg // width
    out_rows = rows * val_count
    in_specs = (
        [pl.BlockSpec((rows, width), functools.partial(lambda k, i: (0, k * steps + i), k)) for k in range(segs)]
        + [pl.BlockSpec((rows, width), lambda i: (0, segs * steps + i))]
        + [pl.BlockSpec((width, columns), functools.partial(lambda k, i: (k * steps + i, 0), k)) for k in range(segs)]
    )
    operands = [packed_rows] * (segs + 1) + [eigenvectors] * segs
    if running is not None:
        in_specs.append(pl.BlockSpec((out_rows, columns), lambda i: (0, 0)))
        operands.append(running)
    return pl.pallas_call(
        functools.partial(project_kernel, segs, val_count, cond_count, running is not None),
        out_shape=jax.ShapeDtypeStruct((out_rows, columns), out_type),
        grid=(steps,),
        in_specs=in_specs,
        out_specs=pl.BlockSpec((out_rows, columns), lambda i: (0, 0)),
        scratch_shapes=[
            pltpu.VMEM((out_rows, width), jnp.bfloat16),
            pltpu.VMEM((out_rows, columns), jnp.float32),
        ],
        compiler_params=pltpu.CompilerParams(vmem_limit_bytes=40 * 1024 * 1024),
        cost_estimate=pl.CostEstimate(
            flops=2 * out_rows * part * columns,
            bytes_accessed=2 * (packed_rows.size + eigenvectors.size),
            transcendentals=0,
        ),
        name="project",
    )(*operands)


def chi_kernel(count, val_count, cond_count, n_freq, factor, order, *refs):
    lefts = refs[:count]
    scales = refs[count : 2 * count]
    rights = refs[2 * count : 4 * count]
    out, weighted = refs[4 * count :]
    rows, columns = lefts[0].shape
    combos = val_count * cond_count
    stride = n_freq + 1

    @pl.when(pl.program_id(0) == 0)
    def _():
        for k in range(count):

            @pl.loop(0, rows // combos)
            def _(j):
                at = pl.multiple_of(j * cond_count, cond_count)
                scale = scales[k][pl.ds(at, cond_count), :].astype(jnp.float32)
                for v in range(val_count):
                    start = pl.multiple_of(j * combos + v * cond_count, cond_count)
                    coeffs = lefts[k][pl.ds(start, cond_count), :].astype(jnp.float32)
                    number = scale[:, v * stride + n_freq : v * stride + n_freq + 1]
                    for f in range(n_freq):
                        factor_f = scale[:, v * stride + f : v * stride + f + 1] * number
                        weighted[pl.ds(k * rows + start, cond_count), f * columns : (f + 1) * columns] = (
                            coeffs * factor_f
                        ).astype(jnp.bfloat16)

    right = jnp.concatenate(
        [jnp.concatenate([rights[2 * k][0], rights[2 * k + 1][0]], axis=1) for k in range(count)], axis=0
    )
    for f in range(n_freq):
        chi = lax.dot_general(
            weighted[:, f * columns : (f + 1) * columns],
            right,
            (((0,), (0,)), ((), ())),
            preferred_element_type=jnp.float32,
        )
        out[:, f, :] = chi * factor


def make_chi(lefts, scales, right, order, fold, val_count, cond_count, n_freq, factor):
    count = len(lefts)
    rows, columns = lefts[0].shape
    whole = lambda shape: pl.BlockSpec(shape, lambda i, order: tuple(0 for _ in shape))
    right_specs = []
    for k in range(count):
        for half in range(2):
            right_specs.append(
                pl.BlockSpec(
                    (1, rows, columns),
                    functools.partial(lambda k, half, i, order: (order[k] * fold + 2 * i + half, 0, 0), k, half),
                )
            )
    return pl.pallas_call(
        functools.partial(chi_kernel, count, val_count, cond_count, n_freq, factor),
        out_shape=jax.ShapeDtypeStruct((columns, n_freq, fold * columns), jnp.float32),
        grid_spec=pltpu.PrefetchScalarGridSpec(
            num_scalar_prefetch=1,
            grid=(fold // 2,),
            in_specs=[whole(a.shape) for a in lefts] + [whole(a.shape) for a in scales] + right_specs,
            out_specs=pl.BlockSpec((columns, n_freq, 2 * columns), lambda i, order: (0, 0, i)),
            scratch_shapes=[pltpu.VMEM((count * rows, n_freq * columns), jnp.bfloat16)],
        ),
        compiler_params=pltpu.CompilerParams(vmem_limit_bytes=40 * 1024 * 1024),
        cost_estimate=pl.CostEstimate(
            flops=2 * count * rows * columns * n_freq * fold * columns,
            bytes_accessed=2 * right.size + 4 * columns * n_freq * fold * columns,
            transcendentals=0,
        ),
        name="chi",
    )(order, *lefts, *scales, *([right] * (2 * count)))


def local(
    val_orbitals,
    cond_orbitals,
    val_energy,
    cond_energy,
    val_slot,
    cond_slot,
    eigenvectors,
    frequencies,
):
    val_count, n_grid = val_orbitals.shape
    cond_count = cond_orbitals.shape[0]
    per_dev = val_slot.shape[0]
    n_freq = frequencies.shape[0]
    n_proj = lax.axis_size("proj")
    n_pair = lax.axis_size("pair")
    x = lax.axis_index("proj")
    part = n_grid // n_proj
    segs = cond_count // val_count
    seg = part // segs
    combos = val_count * cond_count
    columns = eigenvectors.shape[1]
    fold = n_pair // n_proj

    gap = cond_energy[:, None] - val_energy[None, :]
    weights = (
        4.0 * gap[:, :, None] / (gap[:, :, None] ** 2 + frequencies[None, None, :] ** 2)
    ).astype(jnp.bfloat16)
    chosen = (cond_slot[:, None, None] == jnp.arange(cond_count, dtype=jnp.int32)[None, :, None]) & (
        val_slot[:, None, None] == jnp.arange(val_count, dtype=jnp.int32)[None, None, :]
    )
    counts = jnp.sum(chosen.astype(jnp.float32), axis=0).astype(jnp.bfloat16)
    extra = jnp.concatenate([weights, counts[:, :, None]], axis=2).reshape(
        cond_count, val_count * (n_freq + 1)
    )
    extra = jnp.pad(extra, ((0, 0), (0, LANES - extra.shape[1])))

    def packed(place):
        cond_part = lax.dynamic_slice_in_dim(cond_orbitals, place * part, part, 1)
        val_part = lax.dynamic_slice_in_dim(val_orbitals, place * part, part, 1)
        val_part = val_part.reshape(val_count, segs, seg).transpose(1, 0, 2)
        return jnp.concatenate([cond_part, val_part.reshape(cond_count, seg), extra], axis=1)

    pieces = [packed(x)]
    for k in range(1, n_proj):
        to_send = packed((x + k) % n_proj)
        pieces.append(
            lax.ppermute(to_send, "proj", [(s, (s + k) % n_proj) for s in range(n_proj)])
        )
    running = None
    scales = []
    for k in range(n_proj):
        got = lax.all_gather(pieces[k], "pair", axis=0, tiled=True)
        last = k == n_proj - 1
        sums = project(
            got,
            eigenvectors,
            running,
            val_count,
            cond_count,
            jnp.bfloat16 if last else jnp.float32,
        )
        if k < n_proj - 1:
            running = lax.ppermute(
                sums, "proj", [(s, (s + 1) % n_proj) for s in range(n_proj)]
            )
        scales.append(got[:, part + seg :])
    coeffs = sums

    perm = []
    for j in range(n_pair):
        for s in range(n_proj):
            source = j * n_proj + s
            perm.append((source, (j % fold + fold * s) * n_proj + j // fold))
    share = lax.ppermute(coeffs, ("pair", "proj"), perm)
    right = lax.all_gather(share, "pair", axis=0, tiled=True)
    right = right.reshape(n_pair, n_pair * combos, columns)

    own = [coeffs]
    for k in range(1, n_proj):
        own.append(
            lax.ppermute(coeffs, "proj", [(s, (s + k) % n_proj) for s in range(n_proj)])
        )
    factor = -1.0 / math.sqrt(per_dev * n_pair * n_proj)
    order = (x - jnp.arange(n_proj, dtype=jnp.int32)) % n_proj
    scales = [scales[(k - 1) % n_proj] for k in range(n_proj)]
    if columns % LANES == 0:
        return make_chi(own, scales, right, order, fold, val_count, cond_count, n_freq, factor)
    left = []
    for k in range(n_proj):
        rows = own[k].astype(jnp.float32).reshape(n_pair, val_count, cond_count, columns)
        scale = scales[k][:, : val_count * (n_freq + 1)].astype(jnp.float32)
        scale = scale.reshape(n_pair, cond_count, val_count, n_freq + 1).transpose(0, 2, 1, 3)
        scale = scale[..., :n_freq] * scale[..., n_freq:]
        weighted = (rows[..., None] * scale[:, :, :, None, :]).astype(jnp.bfloat16)
        left.append(weighted.reshape(n_pair * combos, columns * n_freq))
    left = jnp.concatenate(left, axis=0)
    right = jnp.take(right.reshape(n_proj, fold, n_pair * combos, columns), order, axis=0)
    right = right.transpose(1, 0, 2, 3).reshape(fold, n_proj * n_pair * combos, columns)
    chi = lax.dot_general(
        left, right, (((0,), (1,)), ((), ())), preferred_element_type=jnp.float32
    )
    return (chi * factor).reshape(columns, n_freq, fold * columns)


def solution(mesh):
    return jax.shard_map(
        local,
        mesh=mesh,
        in_specs=(
            P(("pair", "proj"), None),
            P(("pair", "proj"), None),
            P(("pair", "proj")),
            P(("pair", "proj")),
            P(("pair", "proj")),
            P(("pair", "proj")),
            P("proj", "pair"),
            P(),
        ),
        out_specs=P("pair", None, "proj"),
        check_vma=False,
    )
```

```python
import functools
import math

import jax
import jax.numpy as jnp
from jax import lax
from jax.experimental import pallas as pl
from jax.experimental.pallas import tpu as pltpu
from jax.sharding import Mesh
from jax.sharding import PartitionSpec as P

LANES = 128
AXES = ("z", "y", "c", "x")


def project_kernel(segs, val_count, cond_count, *refs):
    conds = refs[:segs]
    val = refs[segs]
    eigs = refs[segs + 1 : 2 * segs + 1]
    out, density, total = refs[2 * segs + 1 :]
    blocks = val.shape[0] // cond_count
    combos = val_count * cond_count
    groups, _, columns = out.shape

    for k in range(segs):

        @pl.loop(0, blocks)
        def _(j):
            rows = pl.ds(pl.multiple_of(j * cond_count, cond_count), cond_count)
            c = conds[k][rows, :].astype(jnp.float32)
            vals = val[rows, :].astype(jnp.float32)
            for v in range(val_count):
                at = k * val_count + v
                product = (c * vals[at : at + 1, :]).astype(jnp.bfloat16)
                start = pl.multiple_of(j * combos + v * cond_count, cond_count)
                density[pl.ds(start, cond_count), :] = product

        eig = jnp.concatenate([eigs[k][q] for q in range(groups)], axis=1)
        sums = jnp.dot(density[...], eig, preferred_element_type=jnp.float32)
        if k == 0:

            @pl.when(pl.program_id(0) == 0)
            def _():
                total[...] = sums

            @pl.when(pl.program_id(0) > 0)
            def _():
                total[...] += sums
        else:
            total[...] += sums

    @pl.when(pl.program_id(0) == pl.num_programs(0) - 1)
    def _():
        for q in range(groups):
            out[q] = total[:, q * columns : (q + 1) * columns].astype(out.dtype)


def project(unit, eigs, val_count, cond_count):
    groups, part, columns = eigs.shape
    segs = cond_count // val_count
    seg = part // segs
    rows = unit.shape[0]
    out_rows = rows * val_count
    if seg % LANES or columns % LANES:
        blocks = rows // cond_count
        cond = unit[:, :part].reshape(blocks, 1, cond_count, segs, seg)
        val = unit[:, part : part + seg].reshape(blocks, segs, val_count, seg)
        val = val.transpose(0, 2, 1, 3)[:, :, None]
        density = (cond.astype(jnp.float32) * val.astype(jnp.float32)).astype(jnp.bfloat16)
        sums = jnp.einsum(
            "pg,qgs->qps", density.reshape(out_rows, part), eigs, preferred_element_type=jnp.float32
        )
        return sums.astype(jnp.bfloat16)
    width = math.gcd(seg, 384)
    steps = seg // width
    in_specs = (
        [
            pl.BlockSpec((rows, width), functools.partial(lambda k, i: (0, k * steps + i), k))
            for k in range(segs)
        ]
        + [pl.BlockSpec((rows, width), lambda i: (0, segs * steps + i))]
        + [
            pl.BlockSpec(
                (groups, width, columns), functools.partial(lambda k, i: (0, k * steps + i, 0), k)
            )
            for k in range(segs)
        ]
    )
    return pl.pallas_call(
        functools.partial(project_kernel, segs, val_count, cond_count),
        out_shape=jax.ShapeDtypeStruct((groups, out_rows, columns), jnp.bfloat16),
        grid=(steps,),
        in_specs=in_specs,
        out_specs=pl.BlockSpec((groups, out_rows, columns), lambda i: (0, 0, 0)),
        scratch_shapes=[
            pltpu.VMEM((out_rows, width), jnp.bfloat16),
            pltpu.VMEM((out_rows, groups * columns), jnp.float32),
        ],
        compiler_params=pltpu.CompilerParams(vmem_limit_bytes=32 * 1024 * 1024),
        cost_estimate=pl.CostEstimate(
            flops=2 * out_rows * part * groups * columns,
            bytes_accessed=2 * (unit.size + eigs.size),
            transcendentals=0,
        ),
        name="project",
    )(*([unit] * (segs + 1)), *([eigs] * segs))


def chi_kernel(slots, parts, val_count, cond_count, n_freq, factor, place, *refs):
    lefts = refs[0]
    scales = refs[1 : 1 + slots]
    rights = refs[1 + slots : 1 + slots + 2 * parts]
    out, weighted = refs[1 + slots + 2 * parts :]
    rows, columns = lefts.shape[2:]
    combos = val_count * cond_count
    blocks = rows // combos
    stride = n_freq + 1

    @pl.when(pl.program_id(0) == 0)
    def _():
        for k in range(slots):
            for h in range(parts):
                base = (k * parts + h) * rows

                @pl.loop(0, blocks)
                def _(j):
                    at = pl.multiple_of((h * blocks + j) * cond_count, cond_count)
                    scale = scales[k][pl.ds(at, cond_count), :].astype(jnp.float32)
                    for v in range(val_count):
                        start = pl.multiple_of(j * combos + v * cond_count, cond_count)
                        coeffs = lefts[h, k, pl.ds(start, cond_count), :].astype(jnp.float32)
                        number = scale[:, v * stride + n_freq : v * stride + n_freq + 1]
                        for f in range(n_freq):
                            one = scale[:, v * stride + f : v * stride + f + 1] * number
                            weighted[
                                pl.ds(base + start, cond_count), f * columns : (f + 1) * columns
                            ] = (coeffs * one).astype(jnp.bfloat16)

    shift = place[pl.program_id(0)]
    pieces = []
    for k in range(slots):
        for h in range(parts):
            at = lax.bitwise_xor(shift, k)
            pieces.append(
                jnp.concatenate([rights[2 * h][0, at], rights[2 * h + 1][0, at]], axis=1)
            )
    right = jnp.concatenate(pieces, axis=0)
    for f in range(n_freq):
        chi = lax.dot_general(
            weighted[:, f * columns : (f + 1) * columns],
            right,
            (((0,), (0,)), ((), ())),
            preferred_element_type=jnp.float32,
        )
        out[:, f, :] = chi * factor


def make_chi(lefts, units, right, place, val_count, cond_count, n_freq, factor):
    parts, slots, rows, columns = lefts.shape
    members = right.shape[0]
    tiles = members // (2 * parts)
    unit_rows, unit_width = units[0].shape
    last = unit_width // LANES - 1
    right_specs = [
        pl.BlockSpec(
            (1, slots, rows, columns),
            functools.partial(lambda h, c, i, place: (h * tiles * 2 + i * 2 + c, 0, 0, 0), h, c),
        )
        for h in range(parts)
        for c in range(2)
    ]
    return pl.pallas_call(
        functools.partial(chi_kernel, slots, parts, val_count, cond_count, n_freq, factor),
        out_shape=jax.ShapeDtypeStruct((columns, n_freq, tiles * 2 * columns), jnp.float32),
        grid_spec=pltpu.PrefetchScalarGridSpec(
            num_scalar_prefetch=1,
            grid=(tiles,),
            in_specs=[pl.BlockSpec(lefts.shape, lambda i, place: (0, 0, 0, 0))]
            + [pl.BlockSpec((unit_rows, LANES), lambda i, place: (0, last))] * slots
            + right_specs,
            out_specs=pl.BlockSpec((columns, n_freq, 2 * columns), lambda i, place: (0, 0, i)),
            scratch_shapes=[pltpu.VMEM((slots * parts * rows, n_freq * columns), jnp.bfloat16)],
        ),
        compiler_params=pltpu.CompilerParams(vmem_limit_bytes=32 * 1024 * 1024),
        cost_estimate=pl.CostEstimate(
            flops=2 * slots * parts * rows * columns * n_freq * tiles * 2 * columns,
            bytes_accessed=2 * right.size + 4 * columns * n_freq * tiles * 2 * columns,
            transcendentals=0,
        ),
        name="chi",
    )(place, lefts, *units, *([right] * (2 * parts)))


def local(
    shape,
    val_orbitals,
    cond_orbitals,
    val_energy,
    cond_energy,
    val_slot,
    cond_slot,
    eigenvectors,
    frequencies,
):
    nz, ny, nc, nx = shape
    val_count, n_grid = val_orbitals.shape
    cond_count = cond_orbitals.shape[0]
    per_dev = val_slot.shape[0]
    n_freq = frequencies.shape[0]
    z = lax.axis_index("z")
    x = lax.axis_index("x")
    group = ny * nc
    n_parts = group * nx
    part = n_grid // n_parts
    segs = cond_count // val_count
    seg = part // segs
    combos = val_count * cond_count
    columns = eigenvectors.shape[1]
    zfold = nz // nx

    def along_z(array, pairs):
        return lax.ppermute(array, "z", pairs)

    gap = cond_energy[:, None] - val_energy[None, :]
    weights = (
        4.0 * gap[:, :, None] / (gap[:, :, None] ** 2 + frequencies[None, None, :] ** 2)
    ).astype(jnp.bfloat16)
    chosen = (cond_slot[:, None, None] == jnp.arange(cond_count, dtype=jnp.int32)[None, :, None]) & (
        val_slot[:, None, None] == jnp.arange(val_count, dtype=jnp.int32)[None, None, :]
    )
    counts = jnp.sum(chosen.astype(jnp.float32), axis=0).astype(jnp.bfloat16)
    extra = jnp.concatenate([weights, counts[:, :, None]], axis=2).reshape(
        cond_count, val_count * (n_freq + 1)
    )
    extra = jnp.pad(extra, ((0, 0), (0, LANES - extra.shape[1])))

    cond_parts = cond_orbitals.reshape(cond_count, nx, group, part).transpose(2, 1, 0, 3)
    val_parts = val_orbitals.reshape(val_count, nx, group, segs, seg).transpose(2, 1, 3, 0, 4)
    packed = jnp.concatenate(
        [
            cond_parts.reshape(n_parts, cond_count, part),
            val_parts.reshape(n_parts, cond_count, seg),
            jnp.broadcast_to(extra, (n_parts,) + extra.shape),
        ],
        axis=2,
    )
    unit = lax.all_to_all(packed, ("y", "c", "x"), 0, 0, tiled=True)
    unit = unit.reshape(n_parts * cond_count, part + seg + LANES)
    eigs = lax.all_to_all(
        eigenvectors.reshape(group, part, columns), ("y", "c"), 0, 0, tiled=True
    )

    if nz == 4:
        inner = (z == 1) | (z == 2)
        near = along_z(unit, [(0, 1), (1, 0), (2, 3), (3, 2)])
        middle = along_z(unit, [(1, 2), (2, 1)])
        across = along_z(near, [(1, 2), (2, 1)])
        outward = along_z(middle, [(1, 0), (2, 3)])
        far = along_z(across, [(1, 0), (2, 3)])
        units = [unit, near, jnp.where(inner, across, outward), jnp.where(inner, middle, far)]
    else:
        every = lax.all_gather(unit, "z", axis=0)
        units = [
            lax.dynamic_index_in_dim(every, lax.bitwise_xor(z, k), 0, keepdims=False)
            for k in range(nz)
        ]

    own = []
    for k in range(nz):
        sums = project(units[k], eigs, val_count, cond_count)
        sums = sums.reshape(n_parts, -1, columns)
        sums = lax.all_to_all(sums, ("y", "c", "x"), 0, 0, tiled=True)
        own.append(jnp.sum(sums.astype(jnp.float32), axis=0).astype(jnp.bfloat16))
    own = jnp.stack(own)

    lefts = lax.all_gather(own, "x", axis=0)
    perm = []
    for s in range(nz):
        for q in range(group):
            for t in range(nx):
                perm.append(
                    (
                        (s * group + q) * nx + t,
                        ((s % zfold + zfold * t) * group + q) * nx + s // zfold,
                    )
                )
    share = lax.ppermute(own, AXES, perm)
    right = lax.all_gather(share, ("z", "y", "c"), axis=0)
    source = x * zfold + jnp.arange(zfold, dtype=jnp.int32)
    place = lax.bitwise_xor(jnp.broadcast_to(z, source.shape).astype(jnp.int32), source)
    factor = -1.0 / math.sqrt(per_dev * nz * n_parts)
    if columns % LANES == 0:
        return make_chi(
            lefts, units, right, jnp.repeat(place, ny), val_count, cond_count, n_freq, factor
        )
    rows = own.shape[1]
    total = 0.0
    for k in range(nz):
        scale = units[k][:, part + seg : part + seg + val_count * (n_freq + 1)].astype(jnp.float32)
        scale = scale.reshape(n_parts, cond_count, val_count, n_freq + 1).transpose(0, 2, 1, 3)
        scale = scale.reshape(nx, rows, n_freq + 1)
        scale = scale[..., :n_freq] * scale[..., n_freq:]
        weighted = (lefts[:, k, :, :, None].astype(jnp.float32) * scale[:, :, None, :]).astype(
            jnp.bfloat16
        )
        weighted = weighted.reshape(nx * rows, columns * n_freq)
        for low in range(zfold):
            at = lax.bitwise_xor(place[low], k)
            piece = lax.dynamic_index_in_dim(right, at, 1, keepdims=False)
            piece = piece.reshape(nx, zfold, group, rows, columns)[:, low]
            piece = piece.transpose(0, 2, 1, 3).reshape(nx * rows, group * columns)
            chi = lax.dot_general(
                weighted, piece, (((0,), (0,)), ((), ())), preferred_element_type=jnp.float32
            )
            chi = jnp.pad(chi, ((0, 0), (low * group * columns, (zfold - 1 - low) * group * columns)))
            total = total + chi
    return (total * factor).reshape(columns, n_freq, zfold * group * columns)


def solution(mesh):
    n_pair = mesh.shape["pair"]
    n_proj = mesh.shape["proj"]
    shape = (n_pair // 4, 2, 2, n_proj)
    grid = Mesh(mesh.devices.reshape(shape), AXES)
    return jax.shard_map(
        functools.partial(local, shape),
        mesh=grid,
        in_specs=(
            P(AXES, None),
            P(AXES, None),
            P(AXES),
            P(AXES),
            P(AXES),
            P(AXES),
            P("x", ("z", "y", "c")),
            P(),
        ),
        out_specs=P(("z", "y", "c"), None, "x"),
        check_vma=False,
    )
```

```python
import functools
import math

import jax
import jax.numpy as jnp
from jax import lax
from jax.experimental import pallas as pl
from jax.experimental.pallas import tpu as pltpu
from jax.sharding import Mesh
from jax.sharding import PartitionSpec as P

LANES = 128
AXES = ("z", "y", "c", "x")


def project_kernel(segs, val_count, cond_count, *refs):
    conds = refs[:segs]
    val = refs[segs]
    eigs = refs[segs + 1 : 2 * segs + 1]
    out, density, total = refs[2 * segs + 1 :]
    blocks = val.shape[0] // cond_count
    groups, _, columns = out.shape

    for k in range(segs):

        @pl.loop(0, blocks)
        def _(j):
            rows = pl.ds(pl.multiple_of(j * cond_count, cond_count), cond_count)
            c = conds[k][rows, :].astype(jnp.float32)
            vals = val[rows, :].astype(jnp.float32)
            for v in range(val_count):
                at = k * val_count + v
                product = (c * vals[at : at + 1, :]).astype(jnp.bfloat16)
                start = pl.multiple_of(v * val.shape[0] + j * cond_count, cond_count)
                density[pl.ds(start, cond_count), :] = product

        eig = jnp.concatenate([eigs[k][q] for q in range(groups)], axis=1)
        sums = jnp.dot(density[...], eig, preferred_element_type=jnp.float32)
        if k == 0:

            @pl.when(pl.program_id(0) == 0)
            def _():
                total[...] = sums

            @pl.when(pl.program_id(0) > 0)
            def _():
                total[...] += sums
        else:
            total[...] += sums

    @pl.when(pl.program_id(0) == pl.num_programs(0) - 1)
    def _():
        for q in range(groups):
            out[q] = total[:, q * columns : (q + 1) * columns].astype(out.dtype)


def project(unit, eigs, val_count, cond_count, out_type):
    groups, part, columns = eigs.shape
    segs = cond_count // val_count
    seg = part // segs
    rows = unit.shape[0]
    out_rows = rows * val_count
    if seg % LANES or columns % LANES:
        blocks = rows // cond_count
        cond = unit[:, :part].reshape(1, blocks, cond_count, segs, seg)
        val = unit[:, part:].reshape(blocks, segs, val_count, seg)
        val = val.transpose(2, 0, 1, 3)[:, :, None]
        density = (cond.astype(jnp.float32) * val.astype(jnp.float32)).astype(jnp.bfloat16)
        sums = jnp.einsum(
            "pg,qgs->qps", density.reshape(out_rows, part), eigs, preferred_element_type=jnp.float32
        )
        return sums.astype(out_type)
    width = math.gcd(seg, 384)
    steps = seg // width
    in_specs = (
        [
            pl.BlockSpec((rows, width), functools.partial(lambda k, i: (0, k * steps + i), k))
            for k in range(segs)
        ]
        + [pl.BlockSpec((rows, width), lambda i: (0, segs * steps + i))]
        + [
            pl.BlockSpec(
                (groups, width, columns), functools.partial(lambda k, i: (0, k * steps + i, 0), k)
            )
            for k in range(segs)
        ]
    )
    return pl.pallas_call(
        functools.partial(project_kernel, segs, val_count, cond_count),
        out_shape=jax.ShapeDtypeStruct((groups, out_rows, columns), out_type),
        grid=(steps,),
        in_specs=in_specs,
        out_specs=pl.BlockSpec((groups, out_rows, columns), lambda i: (0, 0, 0)),
        scratch_shapes=[
            pltpu.VMEM((out_rows, width), jnp.bfloat16),
            pltpu.VMEM((out_rows, groups * columns), jnp.float32),
        ],
        compiler_params=pltpu.CompilerParams(vmem_limit_bytes=32 * 1024 * 1024),
        cost_estimate=pl.CostEstimate(
            flops=2 * out_rows * part * groups * columns,
            bytes_accessed=2 * (unit.size + eigs.size),
            transcendentals=0,
        ),
        name="project",
    )(*([unit] * (segs + 1)), *([eigs] * segs))


def weigh_kernel(early, late, n_freq, scalars, *refs):
    own_a, mate_a, own_b, mate_b = refs[:4]
    scales = refs[4 : 4 + early + late]
    out = refs[-1]
    rows, columns = own_b.shape[1:]
    stride = n_freq + 1
    width = scales[0].shape[0]
    mine = scalars[0]
    for k in range(early + late):
        scale = scales[k][...].astype(jnp.float32).T
        own = (own_a[k] if k < early else own_b[k - early]).astype(jnp.float32).T
        mate = (mate_a[k] if k < early else mate_b[k - early]).astype(jnp.float32).T
        for h in range(2):
            coeffs = jnp.where(mine == h, own, mate)
            for at in range(0, rows, width):
                v = (h * rows + at) // width
                number = scale[v * stride + n_freq : v * stride + n_freq + 1, :]
                for f in range(n_freq):
                    one = scale[v * stride + f : v * stride + f + 1, :] * number
                    out[k, f * columns : (f + 1) * columns, h * rows + at : h * rows + at + width] = (
                        coeffs[:, at : at + width] * one
                    ).astype(jnp.bfloat16)


def weigh(own_a, mate_a, own_b, mate_b, scales, scalars, n_freq):
    early, rows, columns = own_a.shape
    late = own_b.shape[0]
    width = scales.shape[1]
    whole = lambda shape: pl.BlockSpec(shape, lambda i, scalars: tuple(0 for _ in shape))
    shape = (early + late, n_freq * columns, 2 * rows)
    return pl.pallas_call(
        functools.partial(weigh_kernel, early, late, n_freq),
        out_shape=jax.ShapeDtypeStruct(shape, jnp.bfloat16),
        grid_spec=pltpu.PrefetchScalarGridSpec(
            num_scalar_prefetch=1,
            grid=(1,),
            in_specs=[whole(a.shape) for a in (own_a, mate_a, own_b, mate_b)]
            + [
                pl.BlockSpec(
                    (None, width, LANES),
                    functools.partial(lambda k, i, scalars: (scalars[1 + k], 0, 0), k),
                )
                for k in range(early + late)
            ],
            out_specs=whole(shape),
        ),
        compiler_params=pltpu.CompilerParams(vmem_limit_bytes=24 * 1024 * 1024),
        cost_estimate=pl.CostEstimate(
            flops=2 * math.prod(shape), bytes_accessed=3 * math.prod(shape), transcendentals=0
        ),
        name="weigh",
    )(scalars, own_a, mate_a, own_b, mate_b, *([scales] * (early + late)))


def chi_kernel(early, late, n_freq, factor, place, *refs):
    weighted = refs[0]
    rights_a = refs[1:5]
    rights_b = refs[5:9]
    out = refs[9]
    columns = out.shape[0]
    shift = place[pl.program_id(0)]
    left, right = [], []
    for r in range(early + late):
        left.append(weighted[lax.bitwise_xor(shift, r)])
        for h in range(2):
            pair = [
                rights_a[2 * h + c][0, r] if r < early else rights_b[2 * h + c][0, r - early] for c in range(2)
            ]
            right.append(jnp.concatenate(pair, axis=1))
    chi = jnp.dot(
        jnp.concatenate(left, axis=1),
        jnp.concatenate(right, axis=0),
        preferred_element_type=jnp.float32,
    )
    for f in range(n_freq):
        out[:, f, :] = chi[f * columns : (f + 1) * columns, :] * factor


def make_chi(weighted, right_a, right_b, place, n_freq, factor):
    members, early, rows, columns = right_a.shape
    tiles = members // 4
    late = right_b.shape[1]

    def right_specs(slots):
        return [
            pl.BlockSpec(
                (1, slots, rows, columns),
                functools.partial(lambda h, c, i, place: (h * tiles * 2 + i * 2 + c, 0, 0, 0), h, c),
            )
            for h in range(2)
            for c in range(2)
        ]

    return pl.pallas_call(
        functools.partial(chi_kernel, early, late, n_freq, factor),
        out_shape=jax.ShapeDtypeStruct((columns, n_freq, tiles * 2 * columns), jnp.float32),
        grid_spec=pltpu.PrefetchScalarGridSpec(
            num_scalar_prefetch=1,
            grid=(tiles,),
            in_specs=[pl.BlockSpec(weighted.shape, lambda i, place: (0, 0, 0))]
            + right_specs(early)
            + right_specs(late),
            out_specs=pl.BlockSpec((columns, n_freq, 2 * columns), lambda i, place: (0, 0, i)),
        ),
        compiler_params=pltpu.CompilerParams(vmem_limit_bytes=32 * 1024 * 1024),
        cost_estimate=pl.CostEstimate(
            flops=2 * weighted.size * tiles * 2 * columns,
            bytes_accessed=2 * (right_a.size + right_b.size) + 4 * columns * n_freq * tiles * 2 * columns,
            transcendentals=0,
        ),
        name="chi",
    )(place, weighted, *([right_a] * 4), *([right_b] * 4))


def local(
    shape,
    val_orbitals,
    cond_orbitals,
    val_energy,
    cond_energy,
    val_slot,
    cond_slot,
    eigenvectors,
    frequencies,
):
    nz, ny, nc, nx = shape
    val_count, n_grid = val_orbitals.shape
    cond_count = cond_orbitals.shape[0]
    per_dev = val_slot.shape[0]
    n_freq = frequencies.shape[0]
    z = lax.axis_index("z")
    x = lax.axis_index("x")
    group = ny * nc
    n_parts = group * nx
    part = n_grid // n_parts
    segs = cond_count // val_count
    seg = part // segs
    columns = eigenvectors.shape[1]
    zfold = nz // nx

    def along_z(array, pairs):
        return lax.ppermute(array, "z", pairs)

    gap = cond_energy[:, None] - val_energy[None, :]
    weights = (
        4.0 * gap[:, :, None] / (gap[:, :, None] ** 2 + frequencies[None, None, :] ** 2)
    ).astype(jnp.bfloat16)
    chosen = (cond_slot[:, None, None] == jnp.arange(cond_count, dtype=jnp.int32)[None, :, None]) & (
        val_slot[:, None, None] == jnp.arange(val_count, dtype=jnp.int32)[None, None, :]
    )
    counts = jnp.sum(chosen.astype(jnp.float32), axis=0).astype(jnp.bfloat16)
    extra = jnp.concatenate([weights, counts[:, :, None]], axis=2).reshape(
        cond_count, val_count * (n_freq + 1)
    )
    extra = jnp.pad(extra, ((0, 0), (0, LANES - extra.shape[1])))
    scales = lax.all_gather(extra, AXES, axis=0).reshape(nz, n_parts * cond_count, LANES)

    cond_parts = cond_orbitals.reshape(cond_count, nx, group, part).transpose(2, 1, 0, 3)
    val_parts = val_orbitals.reshape(val_count, nx, group, segs, seg).transpose(2, 1, 3, 0, 4)
    packed = jnp.concatenate(
        [cond_parts.reshape(n_parts, cond_count, part), val_parts.reshape(n_parts, cond_count, seg)],
        axis=2,
    )
    unit = lax.all_to_all(packed, ("y", "c", "x"), 0, 0, tiled=True)
    unit = unit.reshape(n_parts * cond_count, part + seg)
    eigs = lax.all_to_all(
        eigenvectors.reshape(group, part, columns), ("y", "c"), 0, 0, tiled=True
    )

    if nz == 4:
        inner = (z == 1) | (z == 2)
        near = along_z(unit, [(0, 1), (1, 0), (2, 3), (3, 2)])
        middle = along_z(unit, [(1, 2), (2, 1)])
        across = along_z(near, [(1, 2), (2, 1)])
        outward = along_z(middle, [(1, 0), (2, 3)])
        far = along_z(across, [(1, 0), (2, 3)])
        units = [unit, near, jnp.where(inner, across, outward), jnp.where(inner, middle, far)]
    else:
        every = lax.all_gather(unit, "z", axis=0)
        units = [
            lax.dynamic_index_in_dim(every, lax.bitwise_xor(z, k), 0, keepdims=False)
            for k in range(nz)
        ]

    planes = lax.bitwise_xor(z.astype(jnp.int32), jnp.arange(nz, dtype=jnp.int32))
    source = x.astype(jnp.int32) * zfold + jnp.arange(zfold, dtype=jnp.int32)
    place = lax.bitwise_xor(jnp.broadcast_to(z.astype(jnp.int32), source.shape), source)
    factor = -1.0 / math.sqrt(per_dev * nz * n_parts)
    perm = []
    for s in range(nz):
        for q in range(group):
            for t in range(nx):
                perm.append(
                    (
                        (s * group + q) * nx + t,
                        ((s % zfold + zfold * t) * group + q) * nx + s // zfold,
                    )
                )

    def coefficients(k, sent_type):
        sums = project(units[k], eigs, val_count, cond_count, sent_type)
        sums = sums.reshape(n_parts, -1, columns)
        sums = lax.all_to_all(sums, ("y", "c", "x"), 0, 0, tiled=True)
        return jnp.sum(sums.astype(jnp.float32), axis=0).astype(jnp.bfloat16)

    def swapped(own):
        return lax.ppermute(own, AXES, perm)

    def gathered(share):
        return lax.all_gather(share, ("z", "y", "c"), axis=0)

    if columns % LANES == 0 and nx == 2 and nz == 4:
        units[1], scales = lax.optimization_barrier((units[1], scales))
        own_a = jnp.stack([coefficients(k, jnp.float32) for k in range(2)])
        share_a = swapped(own_a)
        right_a = gathered(share_a)
        units[2], _ = lax.optimization_barrier((units[2], share_a))
        own_b = jnp.stack([coefficients(2, jnp.float32), coefficients(3, jnp.bfloat16)])
        share_b, _ = lax.optimization_barrier((swapped(own_b), right_a))
        right_b = gathered(share_b)
        mate_a = lax.ppermute(own_a, "x", [(0, 1), (1, 0)])
        mate_b = lax.ppermute(own_b, "x", [(0, 1), (1, 0)])
        scalars = jnp.concatenate([x.astype(jnp.int32)[None], planes])
        weighted = weigh(own_a, mate_a, own_b, mate_b, scales, scalars, n_freq)
        return make_chi(weighted, right_a, right_b, jnp.repeat(place, ny), n_freq, factor)
    own = jnp.stack([coefficients(k, jnp.float32) for k in range(nz)])
    right = gathered(swapped(own))
    lefts = lax.all_gather(own, "x", axis=0)
    rows = own.shape[1]
    total = 0.0
    for k in range(nz):
        scale = lax.dynamic_index_in_dim(scales, planes[k], 0, keepdims=False)
        scale = scale[:, : val_count * (n_freq + 1)].astype(jnp.float32)
        scale = scale.reshape(n_parts * cond_count, val_count, n_freq + 1).transpose(1, 0, 2)
        scale = scale.reshape(nx, rows, n_freq + 1)
        scale = scale[..., :n_freq] * scale[..., n_freq:]
        weighted = (lefts[:, k, :, :, None].astype(jnp.float32) * scale[:, :, None, :]).astype(
            jnp.bfloat16
        )
        weighted = weighted.reshape(nx * rows, columns * n_freq)
        for low in range(zfold):
            at = lax.bitwise_xor(place[low], k)
            piece = lax.dynamic_index_in_dim(right, at, 1, keepdims=False)
            piece = piece.reshape(nx, zfold, group, rows, columns)[:, low]
            piece = piece.transpose(0, 2, 1, 3).reshape(nx * rows, group * columns)
            chi = lax.dot_general(
                weighted, piece, (((0,), (0,)), ((), ())), preferred_element_type=jnp.float32
            )
            chi = jnp.pad(chi, ((0, 0), (low * group * columns, (zfold - 1 - low) * group * columns)))
            total = total + chi
    return (total * factor).reshape(columns, n_freq, zfold * group * columns)


def solution(mesh):
    n_pair = mesh.shape["pair"]
    n_proj = mesh.shape["proj"]
    shape = (n_pair // 4, 2, 2, n_proj)
    grid = Mesh(mesh.devices.reshape(shape), AXES)
    return jax.shard_map(
        functools.partial(local, shape),
        mesh=grid,
        in_specs=(
            P(AXES, None),
            P(AXES, None),
            P(AXES),
            P(AXES),
            P(AXES),
            P(AXES),
            P("x", ("z", "y", "c")),
            P(),
        ),
        out_specs=P(("z", "y", "c"), None, "x"),
        check_vma=False,
    )
```

```python
import functools
import math

import jax
import jax.numpy as jnp
from jax import lax
from jax.experimental import pallas as pl
from jax.experimental.pallas import tpu as pltpu
from jax.sharding import Mesh
from jax.sharding import PartitionSpec as P

LANES = 128
AXES = ("z", "y", "c", "x")


def pack_kernel(nx, part, seg, val_energy, cond_energy, val_slot, cond_slot, frequencies, *refs):
    conds = refs[:nx]
    vals = refs[nx : 2 * nx]
    out, extra = refs[2 * nx :]
    val_count = val_energy.shape[0]
    cond_count = cond_energy.shape[0]
    n_freq = frequencies.shape[0]
    stride = n_freq + 1

    @pl.when(pl.program_id(0) == 0)
    def _():
        row = lax.broadcasted_iota(jnp.int32, (cond_count, LANES), 0)
        lane = lax.broadcasted_iota(jnp.int32, (cond_count, LANES), 1)
        cond_level = jnp.zeros((cond_count, LANES), jnp.float32)
        for c in range(cond_count):
            cond_level = jnp.where(row == c, cond_energy[c], cond_level)
        val_level = jnp.zeros((cond_count, LANES), jnp.float32)
        freq = jnp.zeros((cond_count, LANES), jnp.float32)
        is_count = lane < 0
        for v in range(val_count):
            for f in range(stride):
                here = lane == v * stride + f
                val_level = jnp.where(here, val_energy[v], val_level)
                if f < n_freq:
                    freq = jnp.where(here, frequencies[f], freq)
                else:
                    is_count = is_count | here
        gap = cond_level - val_level
        weight = 4.0 * gap / (gap * gap + freq * freq)

        def add(p, number):
            here = (row == cond_slot[p]) & (lane == val_slot[p] * stride + n_freq)
            return number + jnp.where(here, 1.0, 0.0)

        number = lax.fori_loop(0, val_slot.shape[0], add, jnp.zeros((cond_count, LANES), jnp.float32))
        used = lane < val_count * stride
        extra[...] = jnp.where(used, jnp.where(is_count, number, weight), 0.0).astype(jnp.bfloat16)

    for t in range(nx):
        out[t, :, :part] = conds[t][...]
        val = vals[t][...].astype(jnp.float32)
        pieces = [val[:, k * seg : (k + 1) * seg] for k in range(part // seg)]
        out[t, :, part : part + seg] = jnp.concatenate(pieces, axis=0).astype(jnp.bfloat16)
        out[t, :, part + seg :] = extra[...]


def pack(val_orbitals, cond_orbitals, val_energy, cond_energy, val_slot, cond_slot, frequencies, nx, group):
    val_count, n_grid = val_orbitals.shape
    cond_count = cond_orbitals.shape[0]
    n_freq = frequencies.shape[0]
    n_parts = group * nx
    part = n_grid // n_parts
    segs = cond_count // val_count
    seg = part // segs
    width = part + seg + LANES
    if seg % LANES == 0:
        smem = pl.BlockSpec(memory_space=pltpu.SMEM)
        piece = lambda rows: [
            pl.BlockSpec((rows, part), functools.partial(lambda t, i: (0, t * group + i), t))
            for t in range(nx)
        ]
        return pl.pallas_call(
            functools.partial(pack_kernel, nx, part, seg),
            out_shape=jax.ShapeDtypeStruct((n_parts, cond_count, width), jnp.bfloat16),
            grid=(group,),
            in_specs=[smem] * 5 + piece(cond_count) + piece(val_count),
            out_specs=pl.BlockSpec((nx, cond_count, width), lambda i: (i, 0, 0)),
            scratch_shapes=[pltpu.VMEM((cond_count, LANES), jnp.bfloat16)],
            name="pack",
        )(
            val_energy,
            cond_energy,
            val_slot,
            cond_slot,
            frequencies,
            *([cond_orbitals] * nx),
            *([val_orbitals] * nx),
        )
    gap = cond_energy[:, None] - val_energy[None, :]
    weights = (
        4.0 * gap[:, :, None] / (gap[:, :, None] ** 2 + frequencies[None, None, :] ** 2)
    ).astype(jnp.bfloat16)
    chosen = (cond_slot[:, None, None] == jnp.arange(cond_count, dtype=jnp.int32)[None, :, None]) & (
        val_slot[:, None, None] == jnp.arange(val_count, dtype=jnp.int32)[None, None, :]
    )
    counts = jnp.sum(chosen.astype(jnp.float32), axis=0).astype(jnp.bfloat16)
    extra = jnp.concatenate([weights, counts[:, :, None]], axis=2).reshape(
        cond_count, val_count * (n_freq + 1)
    )
    extra = jnp.pad(extra, ((0, 0), (0, LANES - extra.shape[1])))
    cond_parts = cond_orbitals.reshape(cond_count, nx, group, part).transpose(2, 1, 0, 3)
    val_parts = val_orbitals.reshape(val_count, nx, group, segs, seg).transpose(2, 1, 3, 0, 4)
    return jnp.concatenate(
        [
            cond_parts.reshape(n_parts, cond_count, part),
            val_parts.reshape(n_parts, cond_count, seg),
            jnp.broadcast_to(extra, (n_parts,) + extra.shape),
        ],
        axis=2,
    )


def project_kernel(segs, val_count, cond_count, *refs):
    conds = refs[:segs]
    val = refs[segs]
    eigs = refs[segs + 1 : 2 * segs + 1]
    out, density, total = refs[2 * segs + 1 :]
    blocks = val.shape[0] // cond_count
    groups, _, columns = out.shape

    for k in range(segs):

        @pl.loop(0, blocks)
        def _(j):
            rows = pl.ds(pl.multiple_of(j * cond_count, cond_count), cond_count)
            c = conds[k][rows, :].astype(jnp.float32)
            vals = val[rows, :].astype(jnp.float32)
            for v in range(val_count):
                at = k * val_count + v
                product = (c * vals[at : at + 1, :]).astype(jnp.bfloat16)
                start = pl.multiple_of(v * val.shape[0] + j * cond_count, cond_count)
                density[pl.ds(start, cond_count), :] = product

        eig = jnp.concatenate([eigs[k][q] for q in range(groups)], axis=1)
        sums = jnp.dot(density[...], eig, preferred_element_type=jnp.float32)
        if k == 0:

            @pl.when(pl.program_id(0) == 0)
            def _():
                total[...] = sums

            @pl.when(pl.program_id(0) > 0)
            def _():
                total[...] += sums
        else:
            total[...] += sums

    @pl.when(pl.program_id(0) == pl.num_programs(0) - 1)
    def _():
        for q in range(groups):
            out[q] = total[:, q * columns : (q + 1) * columns].astype(out.dtype)


def project(unit, eigs, val_count, cond_count, out_type):
    groups, part, columns = eigs.shape
    segs = cond_count // val_count
    seg = part // segs
    rows = unit.shape[0]
    out_rows = rows * val_count
    if seg % LANES or columns % LANES:
        blocks = rows // cond_count
        cond = unit[:, :part].reshape(1, blocks, cond_count, segs, seg)
        val = unit[:, part : part + seg].reshape(blocks, segs, val_count, seg)
        val = val.transpose(2, 0, 1, 3)[:, :, None]
        density = (cond.astype(jnp.float32) * val.astype(jnp.float32)).astype(jnp.bfloat16)
        sums = jnp.einsum(
            "pg,qgs->qps", density.reshape(out_rows, part), eigs, preferred_element_type=jnp.float32
        )
        return sums.astype(out_type)
    width = math.gcd(seg, 384)
    steps = seg // width
    in_specs = (
        [
            pl.BlockSpec((rows, width), functools.partial(lambda k, i: (0, k * steps + i), k))
            for k in range(segs)
        ]
        + [pl.BlockSpec((rows, width), lambda i: (0, segs * steps + i))]
        + [
            pl.BlockSpec(
                (groups, width, columns), functools.partial(lambda k, i: (0, k * steps + i, 0), k)
            )
            for k in range(segs)
        ]
    )
    return pl.pallas_call(
        functools.partial(project_kernel, segs, val_count, cond_count),
        out_shape=jax.ShapeDtypeStruct((groups, out_rows, columns), out_type),
        grid=(steps,),
        in_specs=in_specs,
        out_specs=pl.BlockSpec((groups, out_rows, columns), lambda i: (0, 0, 0)),
        scratch_shapes=[
            pltpu.VMEM((out_rows, width), jnp.bfloat16),
            pltpu.VMEM((out_rows, groups * columns), jnp.float32),
        ],
        compiler_params=pltpu.CompilerParams(vmem_limit_bytes=32 * 1024 * 1024),
        cost_estimate=pl.CostEstimate(
            flops=2 * out_rows * part * groups * columns,
            bytes_accessed=2 * (unit.size + eigs.size),
            transcendentals=0,
        ),
        name="project",
    )(*([unit] * (segs + 1)), *([eigs] * segs))


def weigh_kernel(early, late, n_freq, scalars, *refs):
    own_a, mate_a, own_b, mate_b = refs[:4]
    scales = refs[4 : 4 + early + late]
    out = refs[-1]
    rows, columns = own_b.shape[1:]
    stride = n_freq + 1
    width = scales[0].shape[0]
    mine = scalars[0]
    for k in range(early + late):
        scale = scales[k][...].astype(jnp.float32).T
        own = (own_a[k] if k < early else own_b[k - early]).astype(jnp.float32).T
        mate = (mate_a[k] if k < early else mate_b[k - early]).astype(jnp.float32).T
        for h in range(2):
            coeffs = jnp.where(mine == h, own, mate)
            for at in range(0, rows, width):
                v = (h * rows + at) // width
                number = scale[v * stride + n_freq : v * stride + n_freq + 1, :]
                for f in range(n_freq):
                    one = scale[v * stride + f : v * stride + f + 1, :] * number
                    out[k, f * columns : (f + 1) * columns, h * rows + at : h * rows + at + width] = (
                        coeffs[:, at : at + width] * one
                    ).astype(jnp.bfloat16)


def weigh(own_a, mate_a, own_b, mate_b, units, scalars, n_freq):
    early, rows, columns = own_a.shape
    late = own_b.shape[0]
    width = units[0].shape[0]
    last = units[0].shape[1] // LANES - 1
    whole = lambda shape: pl.BlockSpec(shape, lambda i, scalars: tuple(0 for _ in shape))
    shape = (early + late, n_freq * columns, 2 * rows)
    return pl.pallas_call(
        functools.partial(weigh_kernel, early, late, n_freq),
        out_shape=jax.ShapeDtypeStruct(shape, jnp.bfloat16),
        grid_spec=pltpu.PrefetchScalarGridSpec(
            num_scalar_prefetch=1,
            grid=(1,),
            in_specs=[whole(a.shape) for a in (own_a, mate_a, own_b, mate_b)]
            + [pl.BlockSpec((width, LANES), lambda i, scalars: (0, last))] * (early + late),
            out_specs=whole(shape),
        ),
        compiler_params=pltpu.CompilerParams(vmem_limit_bytes=24 * 1024 * 1024),
        cost_estimate=pl.CostEstimate(
            flops=2 * math.prod(shape), bytes_accessed=3 * math.prod(shape), transcendentals=0
        ),
        name="weigh",
    )(scalars, own_a, mate_a, own_b, mate_b, *units)


def chi_kernel(early, n_freq, factor, scalars, *refs):
    weighted = refs[0]
    rights_a = refs[1:5]
    rights_b = refs[5:9]
    out = refs[9]
    columns = out.shape[0]
    shift = lax.bitwise_xor(scalars[0], scalars[3] + pl.program_id(0) // 2)
    left, right = [], []
    for r in range(early + 1):
        left.append(weighted[lax.bitwise_xor(shift, r)])
        for h in range(2):
            pair = [rights_a[2 * h + c][0, r] if r < early else rights_b[2 * h + c][0] for c in range(2)]
            right.append(jnp.concatenate(pair, axis=1))
    chi = jnp.dot(
        jnp.concatenate(left, axis=1),
        jnp.concatenate(right, axis=0),
        preferred_element_type=jnp.float32,
    )
    for f in range(n_freq):
        out[:, f, :] = chi[f * columns : (f + 1) * columns, :] * factor


def make_chi(weighted, right_a, right_b, scalars, n_freq, factor):
    members, early, rows, columns = right_a.shape
    tiles = members // 4

    def near(h, c, i, scalars):
        z = lax.bitwise_xor(scalars[0], h * 2 + i // 2)
        y = lax.bitwise_xor(scalars[1], lax.rem(i, 2))
        core = lax.bitwise_xor(scalars[2], c)
        return ((core * 2 + y) * 4 + z, 0, 0)

    places = [(h, c) for h in range(2) for c in range(2)]
    return pl.pallas_call(
        functools.partial(chi_kernel, early, n_freq, factor),
        out_shape=jax.ShapeDtypeStruct((columns, n_freq, tiles * 2 * columns), jnp.float32),
        grid_spec=pltpu.PrefetchScalarGridSpec(
            num_scalar_prefetch=1,
            grid=(tiles,),
            in_specs=[pl.BlockSpec(weighted.shape, lambda i, scalars: (0, 0, 0))]
            + [
                pl.BlockSpec(
                    (1, early, rows, columns),
                    functools.partial(
                        lambda h, c, i, scalars: (h * tiles * 2 + i * 2 + c, 0, 0, 0), h, c
                    ),
                )
                for h, c in places
            ]
            + [pl.BlockSpec((1, rows, columns), functools.partial(near, h, c)) for h, c in places],
            out_specs=pl.BlockSpec((columns, n_freq, 2 * columns), lambda i, scalars: (0, 0, i)),
        ),
        compiler_params=pltpu.CompilerParams(vmem_limit_bytes=32 * 1024 * 1024),
        cost_estimate=pl.CostEstimate(
            flops=2 * weighted.size * tiles * 2 * columns,
            bytes_accessed=2 * (right_a.size + right_b.size) + 4 * columns * n_freq * tiles * 2 * columns,
            transcendentals=0,
        ),
        name="chi",
    )(scalars, weighted, *([right_a] * 4), *([right_b] * 4))


def local(
    shape,
    val_orbitals,
    cond_orbitals,
    val_energy,
    cond_energy,
    val_slot,
    cond_slot,
    eigenvectors,
    frequencies,
):
    nz, ny, nc, nx = shape
    val_count, n_grid = val_orbitals.shape
    cond_count = cond_orbitals.shape[0]
    per_dev = val_slot.shape[0]
    n_freq = frequencies.shape[0]
    z = lax.axis_index("z")
    x = lax.axis_index("x")
    group = ny * nc
    n_parts = group * nx
    part = n_grid // n_parts
    segs = cond_count // val_count
    seg = part // segs
    columns = eigenvectors.shape[1]
    zfold = nz // nx

    def along_z(array, pairs):
        return lax.ppermute(array, "z", pairs)

    packed = pack(
        val_orbitals, cond_orbitals, val_energy, cond_energy, val_slot, cond_slot, frequencies, nx, group
    )
    unit = lax.all_to_all(packed, ("y", "c", "x"), 0, 0, tiled=True)
    unit = unit.reshape(n_parts * cond_count, part + seg + LANES)
    eigs = lax.all_to_all(
        eigenvectors.reshape(group, part, columns), ("y", "c"), 0, 0, tiled=True
    )

    if nz == 4:
        inner = (z == 1) | (z == 2)
        near = along_z(unit, [(0, 1), (1, 0), (2, 3), (3, 2)])
        middle = along_z(unit, [(1, 2), (2, 1)])
        across = along_z(near, [(1, 2), (2, 1)])
        outward = along_z(middle, [(1, 0), (2, 3)])
        far = along_z(across, [(1, 0), (2, 3)])
        units = [unit, near, jnp.where(inner, across, outward), jnp.where(inner, middle, far)]
    else:
        every = lax.all_gather(unit, "z", axis=0)
        units = [
            lax.dynamic_index_in_dim(every, lax.bitwise_xor(z, k), 0, keepdims=False)
            for k in range(nz)
        ]

    source = x.astype(jnp.int32) * zfold + jnp.arange(zfold, dtype=jnp.int32)
    place = lax.bitwise_xor(jnp.broadcast_to(z.astype(jnp.int32), source.shape), source)
    factor = -1.0 / math.sqrt(per_dev * nz * n_parts)
    perm = []
    for s in range(nz):
        for q in range(group):
            for t in range(nx):
                perm.append(
                    (
                        (s * group + q) * nx + t,
                        ((s % zfold + zfold * t) * group + q) * nx + s // zfold,
                    )
                )

    def coefficients(k, sent_type):
        sums = project(units[k], eigs, val_count, cond_count, sent_type)
        sums = sums.reshape(n_parts, -1, columns)
        sums = lax.all_to_all(sums, ("y", "c", "x"), 0, 0, tiled=True)
        return jnp.sum(sums.astype(jnp.float32), axis=0).astype(jnp.bfloat16)

    def swapped(own):
        return lax.ppermute(own, AXES, perm)

    def gathered(share):
        return lax.all_gather(share, ("z", "y", "c"), axis=0)

    if columns % LANES == 0 and seg % LANES == 0 and nx == 2 and nz == 4:
        flip = [(0, 1), (1, 0)]
        own_a = jnp.stack([coefficients(k, jnp.float32) for k in range(nz - 1)])
        share_a = swapped(own_a)
        right_a = gathered(share_a)
        units[-1], _ = lax.optimization_barrier((units[-1], own_a))
        own_b = coefficients(nz - 1, jnp.bfloat16)
        share_b = swapped(own_b)
        held = jnp.stack(
            [share_b] + [along_z(share_b, [(t, t ^ k) for t in range(nz)]) for k in range(1, nz)]
        )
        held = jnp.concatenate([held, lax.ppermute(held, "y", flip)])
        right_b = jnp.concatenate([held, lax.ppermute(held, "c", flip)])
        mate_a = lax.ppermute(own_a, "x", flip)
        mate_b = lax.ppermute(own_b, "x", flip)
        weighted = weigh(
            own_a, mate_a, own_b[None], mate_b[None], units, x.astype(jnp.int32)[None], n_freq
        )
        scalars = jnp.stack([z, lax.axis_index("y"), lax.axis_index("c"), x * zfold]).astype(jnp.int32)
        return make_chi(weighted, right_a, right_b, scalars, n_freq, factor)
    own = jnp.stack([coefficients(k, jnp.float32) for k in range(nz)])
    right = gathered(swapped(own))
    lefts = lax.all_gather(own, "x", axis=0)
    rows = own.shape[1]
    total = 0.0
    for k in range(nz):
        scale = units[k][:, part + seg : part + seg + val_count * (n_freq + 1)].astype(jnp.float32)
        scale = scale.reshape(n_parts * cond_count, val_count, n_freq + 1).transpose(1, 0, 2)
        scale = scale.reshape(nx, rows, n_freq + 1)
        scale = scale[..., :n_freq] * scale[..., n_freq:]
        weighted = (lefts[:, k, :, :, None].astype(jnp.float32) * scale[:, :, None, :]).astype(
            jnp.bfloat16
        )
        weighted = weighted.reshape(nx * rows, columns * n_freq)
        for low in range(zfold):
            at = lax.bitwise_xor(place[low], k)
            piece = lax.dynamic_index_in_dim(right, at, 1, keepdims=False)
            piece = piece.reshape(nx, zfold, group, rows, columns)[:, low]
            piece = piece.transpose(0, 2, 1, 3).reshape(nx * rows, group * columns)
            chi = lax.dot_general(
                weighted, piece, (((0,), (0,)), ((), ())), preferred_element_type=jnp.float32
            )
            chi = jnp.pad(chi, ((0, 0), (low * group * columns, (zfold - 1 - low) * group * columns)))
            total = total + chi
    return (total * factor).reshape(columns, n_freq, zfold * group * columns)


def solution(mesh):
    n_pair = mesh.shape["pair"]
    n_proj = mesh.shape["proj"]
    shape = (n_pair // 4, 2, 2, n_proj)
    grid = Mesh(mesh.devices.reshape(shape), AXES)
    return jax.shard_map(
        functools.partial(local, shape),
        mesh=grid,
        in_specs=(
            P(AXES, None),
            P(AXES, None),
            P(AXES),
            P(AXES),
            P(AXES),
            P(AXES),
            P("x", ("z", "y", "c")),
            P(),
        ),
        out_specs=P(("z", "y", "c"), None, "x"),
        check_vma=False,
    )
```

```python
import functools
import math

import jax
import jax.numpy as jnp
from jax import lax
from jax.experimental import pallas as pl
from jax.experimental.pallas import tpu as pltpu
from jax.sharding import Mesh
from jax.sharding import PartitionSpec as P

LANES = 128
AXES = ("z", "y", "c", "x")


def pack_kernel(nx, part, seg, val_energy, cond_energy, val_slot, cond_slot, frequencies, *refs):
    conds = refs[:nx]
    vals = refs[nx : 2 * nx]
    out, extra = refs[2 * nx :]
    val_count = val_energy.shape[0]
    cond_count = cond_energy.shape[0]
    n_freq = frequencies.shape[0]
    stride = n_freq + 1

    @pl.when(pl.program_id(0) == 0)
    def _():
        row = lax.broadcasted_iota(jnp.int32, (cond_count, LANES), 0)
        lane = lax.broadcasted_iota(jnp.int32, (cond_count, LANES), 1)
        cond_level = jnp.zeros((cond_count, LANES), jnp.float32)
        for c in range(cond_count):
            cond_level = jnp.where(row == c, cond_energy[c], cond_level)
        val_level = jnp.zeros((cond_count, LANES), jnp.float32)
        freq = jnp.zeros((cond_count, LANES), jnp.float32)
        is_count = lane < 0
        for v in range(val_count):
            for f in range(stride):
                here = lane == v * stride + f
                val_level = jnp.where(here, val_energy[v], val_level)
                if f < n_freq:
                    freq = jnp.where(here, frequencies[f], freq)
                else:
                    is_count = is_count | here
        gap = cond_level - val_level
        weight = 4.0 * gap / (gap * gap + freq * freq)

        def add(p, number):
            here = (row == cond_slot[p]) & (lane == val_slot[p] * stride + n_freq)
            return number + jnp.where(here, 1.0, 0.0)

        number = lax.fori_loop(0, val_slot.shape[0], add, jnp.zeros((cond_count, LANES), jnp.float32))
        used = lane < val_count * stride
        extra[...] = jnp.where(used, jnp.where(is_count, number, weight), 0.0).astype(jnp.bfloat16)

    for t in range(nx):
        out[t, :, :part] = conds[t][...]
        val = vals[t][...].astype(jnp.float32)
        pieces = [val[:, k * seg : (k + 1) * seg] for k in range(part // seg)]
        out[t, :, part : part + seg] = jnp.concatenate(pieces, axis=0).astype(jnp.bfloat16)
        out[t, :, part + seg :] = extra[...]


def pack(val_orbitals, cond_orbitals, val_energy, cond_energy, val_slot, cond_slot, frequencies, nx, group):
    val_count, n_grid = val_orbitals.shape
    cond_count = cond_orbitals.shape[0]
    n_freq = frequencies.shape[0]
    n_parts = group * nx
    part = n_grid // n_parts
    segs = cond_count // val_count
    seg = part // segs
    width = part + seg + LANES
    if seg % LANES == 0:
        smem = pl.BlockSpec(memory_space=pltpu.SMEM)
        piece = lambda rows: [
            pl.BlockSpec((rows, part), functools.partial(lambda t, i: (0, t * group + i), t))
            for t in range(nx)
        ]
        return pl.pallas_call(
            functools.partial(pack_kernel, nx, part, seg),
            out_shape=jax.ShapeDtypeStruct((n_parts, cond_count, width), jnp.bfloat16),
            grid=(group,),
            in_specs=[smem] * 5 + piece(cond_count) + piece(val_count),
            out_specs=pl.BlockSpec((nx, cond_count, width), lambda i: (i, 0, 0)),
            scratch_shapes=[pltpu.VMEM((cond_count, LANES), jnp.bfloat16)],
            name="pack",
        )(
            val_energy,
            cond_energy,
            val_slot,
            cond_slot,
            frequencies,
            *([cond_orbitals] * nx),
            *([val_orbitals] * nx),
        )
    gap = cond_energy[:, None] - val_energy[None, :]
    weights = (
        4.0 * gap[:, :, None] / (gap[:, :, None] ** 2 + frequencies[None, None, :] ** 2)
    ).astype(jnp.bfloat16)
    chosen = (cond_slot[:, None, None] == jnp.arange(cond_count, dtype=jnp.int32)[None, :, None]) & (
        val_slot[:, None, None] == jnp.arange(val_count, dtype=jnp.int32)[None, None, :]
    )
    counts = jnp.sum(chosen.astype(jnp.float32), axis=0).astype(jnp.bfloat16)
    extra = jnp.concatenate([weights, counts[:, :, None]], axis=2).reshape(
        cond_count, val_count * (n_freq + 1)
    )
    extra = jnp.pad(extra, ((0, 0), (0, LANES - extra.shape[1])))
    cond_parts = cond_orbitals.reshape(cond_count, nx, group, part).transpose(2, 1, 0, 3)
    val_parts = val_orbitals.reshape(val_count, nx, group, segs, seg).transpose(2, 1, 3, 0, 4)
    return jnp.concatenate(
        [
            cond_parts.reshape(n_parts, cond_count, part),
            val_parts.reshape(n_parts, cond_count, seg),
            jnp.broadcast_to(extra, (n_parts,) + extra.shape),
        ],
        axis=2,
    )


def project_kernel(segs, val_count, cond_count, place, *refs):
    conds = refs[:segs]
    val = refs[segs]
    eigs = refs[segs + 1 : 5 * segs + 1]
    keep, send, density, total = refs[5 * segs + 1 :]
    rows = val.shape[0]
    blocks = rows // cond_count
    columns = keep.shape[-1]
    half = keep.shape[-2]
    turn = place[0] * 2

    for k in range(segs):

        @pl.loop(0, blocks)
        def _(j):
            at = pl.ds(pl.multiple_of(j * cond_count, cond_count), cond_count)
            c = conds[k][at, :].astype(jnp.float32)
            vals = val[at, :].astype(jnp.float32)
            for v in range(val_count):
                row = k * val_count + v
                product = (c * vals[row : row + 1, :]).astype(jnp.bfloat16)
                start = lax.bitwise_xor(v, turn) * rows + j * cond_count
                density[pl.ds(pl.multiple_of(start, cond_count), cond_count), :] = product

        eig = jnp.concatenate([eigs[4 * k + q][...] for q in range(4)], axis=1)
        sums = jnp.dot(density[...], eig, preferred_element_type=jnp.float32)
        if k == 0:

            @pl.when(pl.program_id(0) == 0)
            def _():
                total[...] = sums

            @pl.when(pl.program_id(0) > 0)
            def _():
                total[...] += sums
        else:
            total[...] += sums

    @pl.when(pl.program_id(0) == pl.num_programs(0) - 1)
    def _():
        for q in range(4):
            out = send if q % 2 else keep
            for h in range(2):
                out[q // 2, h] = total[h * half : (h + 1) * half, q * columns : (q + 1) * columns]


def project(unit, eigs, place, val_count, cond_count):
    part, columns = eigs[0].shape
    segs = cond_count // val_count
    seg = part // segs
    rows = unit.shape[0]
    half = rows * val_count // 2
    width = math.gcd(seg, 384)
    steps = seg // width
    in_specs = (
        [
            pl.BlockSpec((rows, width), functools.partial(lambda k, i, place: (0, k * steps + i), k))
            for k in range(segs)
        ]
        + [pl.BlockSpec((rows, width), lambda i, place: (0, segs * steps + i))]
        + [
            pl.BlockSpec((width, columns), functools.partial(lambda k, i, place: (k * steps + i, 0), k))
            for k in range(segs)
            for q in range(4)
        ]
    )
    shape = (2, 2, half, columns)
    out = jax.ShapeDtypeStruct(shape, jnp.float32)
    out_spec = pl.BlockSpec(shape, lambda i, place: (0, 0, 0, 0))
    return pl.pallas_call(
        functools.partial(project_kernel, segs, val_count, cond_count),
        out_shape=[out, out],
        grid_spec=pltpu.PrefetchScalarGridSpec(
            num_scalar_prefetch=1,
            grid=(steps,),
            in_specs=in_specs,
            out_specs=[out_spec, out_spec],
            scratch_shapes=[
                pltpu.VMEM((2 * half, width), jnp.bfloat16),
                pltpu.VMEM((2 * half, 4 * columns), jnp.float32),
            ],
        ),
        compiler_params=pltpu.CompilerParams(vmem_limit_bytes=32 * 1024 * 1024),
        cost_estimate=pl.CostEstimate(
            flops=16 * half * part * columns,
            bytes_accessed=2 * (unit.size + 4 * part * columns),
            transcendentals=0,
        ),
        name="project",
    )(place, *([unit] * (segs + 1)), *(list(eigs) * segs))


def weigh_kernel(slots, n_freq, place, *refs):
    owns = refs[:slots]
    mates = refs[slots : 2 * slots]
    scales = refs[2 * slots : 3 * slots]
    out = refs[-1]
    rows, columns = owns[0].shape
    stride = n_freq + 1
    width = scales[0].shape[0]
    mine = place[0]
    for k in range(slots):
        scale = scales[k][...].astype(jnp.float32).T
        own = owns[k][...].astype(jnp.float32).T
        mate = mates[k][...].astype(jnp.float32).T
        for h in range(2):
            coeffs = jnp.where(mine == h, own, mate)
            for at in range(0, rows, width):
                v = (h * rows + at) // width
                number = scale[v * stride + n_freq : v * stride + n_freq + 1, :]
                for f in range(n_freq):
                    one = scale[v * stride + f : v * stride + f + 1, :] * number
                    out[k, f * columns : (f + 1) * columns, h * rows + at : h * rows + at + width] = (
                        coeffs[:, at : at + width] * one
                    ).astype(jnp.bfloat16)


def weigh(owns, mates, units, place, n_freq):
    slots = len(owns)
    rows, columns = owns[0].shape
    width = units[0].shape[0]
    last = units[0].shape[1] // LANES - 1
    shape = (slots, n_freq * columns, 2 * rows)
    return pl.pallas_call(
        functools.partial(weigh_kernel, slots, n_freq),
        out_shape=jax.ShapeDtypeStruct(shape, jnp.bfloat16),
        grid_spec=pltpu.PrefetchScalarGridSpec(
            num_scalar_prefetch=1,
            grid=(1,),
            in_specs=[pl.BlockSpec((rows, columns), lambda i, place: (0, 0))] * (2 * slots)
            + [pl.BlockSpec((width, LANES), lambda i, place: (0, last))] * slots,
            out_specs=pl.BlockSpec(shape, lambda i, place: (0, 0, 0)),
        ),
        compiler_params=pltpu.CompilerParams(vmem_limit_bytes=24 * 1024 * 1024),
        cost_estimate=pl.CostEstimate(
            flops=2 * math.prod(shape), bytes_accessed=3 * math.prod(shape), transcendentals=0
        ),
        name="weigh",
    )(place, *owns, *mates, *units)


def chi_kernel(early, late, n_freq, factor, scalars, *refs):
    weighted = refs[0]
    rights_a = refs[1:5]
    rights_b = refs[5 : 5 + 4 * late]
    out = refs[5 + 4 * late]
    columns = out.shape[0]
    core = scalars[2]
    shift = lax.bitwise_xor(scalars[0], scalars[3] + pl.program_id(0) // 2)
    left, right = [], []
    for r in range(early + late):
        left.append(weighted[lax.bitwise_xor(shift, r)])
        for h in range(2):
            if r < early:
                pair = [rights_a[2 * h + c][0, r] for c in range(2)]
            else:
                at = 4 * (r - early) + 2 * h
                own, mate = rights_b[at][0], rights_b[at + 1][0]
                pair = [jnp.where(core == c, own, mate) for c in range(2)]
            right.append(jnp.concatenate(pair, axis=1))
    chi = jnp.dot(
        jnp.concatenate(left, axis=1),
        jnp.concatenate(right, axis=0),
        preferred_element_type=jnp.float32,
    )
    for f in range(n_freq):
        out[:, f, :] = chi[f * columns : (f + 1) * columns, :] * factor


def make_chi(weighted, right_a, rights_b, scalars, n_freq, factor):
    members, early, rows, columns = right_a.shape
    tiles = members // 4
    late = len(rights_b)

    def near(h, i, scalars):
        z = lax.bitwise_xor(scalars[0], h * 2 + i // 2)
        y = lax.bitwise_xor(scalars[1], lax.rem(i, 2))
        return (y * 4 + z, 0, 0)

    return pl.pallas_call(
        functools.partial(chi_kernel, early, late, n_freq, factor),
        out_shape=jax.ShapeDtypeStruct((columns, n_freq, tiles * 2 * columns), jnp.float32),
        grid_spec=pltpu.PrefetchScalarGridSpec(
            num_scalar_prefetch=1,
            grid=(tiles,),
            in_specs=[pl.BlockSpec(weighted.shape, lambda i, scalars: (0, 0, 0))]
            + [
                pl.BlockSpec(
                    (1, early, rows, columns),
                    functools.partial(
                        lambda h, c, i, scalars: (h * tiles * 2 + i * 2 + c, 0, 0, 0), h, c
                    ),
                )
                for h in range(2)
                for c in range(2)
            ]
            + [
                pl.BlockSpec((1, rows, columns), functools.partial(near, h))
                for r in range(late)
                for h in range(2)
                for c in range(2)
            ],
            out_specs=pl.BlockSpec((columns, n_freq, 2 * columns), lambda i, scalars: (0, 0, i)),
        ),
        compiler_params=pltpu.CompilerParams(vmem_limit_bytes=32 * 1024 * 1024),
        cost_estimate=pl.CostEstimate(
            flops=2 * weighted.size * tiles * 2 * columns,
            bytes_accessed=2 * (early + late) * members * rows * columns
            + 4 * columns * n_freq * tiles * 2 * columns,
            transcendentals=0,
        ),
        name="chi",
    )(scalars, weighted, *([right_a] * 4), *[a for pair in rights_b for a in pair * 2])


def fast(shape, unit, eigenvectors, part, val_count, cond_count, n_freq, factor):
    nz, ny, nc, nx = shape
    z, y, c, x = [lax.axis_index(name).astype(jnp.int32) for name in AXES]
    columns = eigenvectors.shape[1]
    places = [(i, j, k, t) for i in range(nz) for j in range(ny) for k in range(nc) for t in range(nx)]
    number = {place: at for at, place in enumerate(places)}

    def send(array, target):
        pairs = [(number[place], target(*place)) for place in places]
        return lax.ppermute(
            array, AXES, [(source, number[to]) for source, to in pairs if to is not None]
        )

    def along_z(array, moves):
        moves = dict(moves)
        return send(array, lambda i, j, k, t: (moves[i], j, k, t) if i in moves else None)

    here = y * nc + c
    eigs = []
    for k in range(ny * nc):
        at = lax.bitwise_xor(here, k) * part
        rows = lax.dynamic_slice_in_dim(eigenvectors, at, part, 0)
        eigs.append(
            send(rows, functools.partial(lambda q, i, j, k, t: (i, j ^ (q // 2), k ^ (q % 2), t), k))
            if k
            else rows
        )

    inner = (z == 1) | (z == 2)
    near = along_z(unit, [(0, 1), (1, 0), (2, 3), (3, 2)])
    middle = along_z(unit, [(1, 2), (2, 1)])
    across = along_z(near, [(1, 2), (2, 1)])
    outward = along_z(middle, [(1, 0), (2, 3)])
    far = along_z(across, [(1, 0), (2, 3)])
    units = [unit, near, jnp.where(inner, across, outward), jnp.where(inner, middle, far)]

    place = x[None]

    def coefficients(unit):
        keep, away = project(unit, eigs, place, val_count, cond_count)
        sums = keep + send(away, lambda i, j, k, t: (i, j, 1 - k, t))
        total = sums[0, 0] + send(sums[0, 1], lambda i, j, k, t: (i, j, k, 1 - t))
        total = total + send(sums[1, 0], lambda i, j, k, t: (i, 1 - j, k, t))
        total = total + send(sums[1, 1], lambda i, j, k, t: (i, 1 - j, k, 1 - t))
        return total.astype(jnp.bfloat16)

    def mate(own):
        return send(own, lambda i, j, k, t: (i, j, k, 1 - t))

    def share(own, m):
        return send(own, lambda i, j, k, t: ((2 * t + i % 2) ^ m, j, k, i // 2))

    def spread(own):
        held = jnp.stack([share(own, m) for m in range(nz)])
        held = jnp.concatenate([held, send(held, lambda i, j, k, t: (i, 1 - j, k, t))])
        return held, send(held, lambda i, j, k, t: (i, j, 1 - k, t))

    owns = [coefficients(units[k]) for k in range(2)]
    share_a = share(jnp.stack(owns), 0)
    right_a = lax.all_gather(share_a, ("z", "y", "c"), axis=0)
    mates = [mate(own) for own in owns]
    units[3], _ = lax.optimization_barrier((units[3], (share_a, mates)))
    rights_b = []
    for k in range(2, nz):
        own = coefficients(units[k])
        rights_b.append(spread(own))
        owns.append(own)
        mates.append(mate(own))
    weighted = weigh(owns, mates, units, place, n_freq)
    scalars = jnp.stack([z, y, c, 2 * x])
    return make_chi(weighted, right_a, rights_b, scalars, n_freq, factor)


def plain(shape, unit, eigenvectors, part, val_count, cond_count, n_freq, factor):
    nz, ny, nc, nx = shape
    z = lax.axis_index("z").astype(jnp.int32)
    x = lax.axis_index("x").astype(jnp.int32)
    group = ny * nc
    n_parts = group * nx
    segs = cond_count // val_count
    seg = part // segs
    columns = eigenvectors.shape[1]
    zfold = nz // nx
    eigs = lax.all_to_all(
        eigenvectors.reshape(group, part, columns), ("y", "c"), 0, 0, tiled=True
    )
    every = lax.all_gather(unit, "z", axis=0)

    def coefficients(unit):
        cond = unit[:, :part].reshape(1, n_parts, cond_count, segs, seg)
        val = unit[:, part : part + seg].reshape(n_parts, segs, val_count, seg)
        val = val.transpose(2, 0, 1, 3)[:, :, None]
        density = (cond.astype(jnp.float32) * val.astype(jnp.float32)).astype(jnp.bfloat16)
        sums = jnp.einsum(
            "pg,qgs->qps", density.reshape(-1, part), eigs, preferred_element_type=jnp.float32
        )
        sums = sums.reshape(n_parts, -1, columns)
        sums = lax.all_to_all(sums, ("y", "c", "x"), 0, 0, tiled=True)
        return jnp.sum(sums, axis=0).astype(jnp.bfloat16)

    own = jnp.stack([coefficients(every[k]) for k in range(nz)])
    lefts = lax.all_gather(own, "x", axis=0)
    perm = []
    for s in range(nz):
        for q in range(group):
            for t in range(nx):
                target = ((s % zfold + zfold * t) * group + q) * nx + s // zfold
                perm.append(((s * group + q) * nx + t, target))
    share = lax.ppermute(own, AXES, perm)
    right = lax.all_gather(share, ("z", "y", "c"), axis=0)
    rows = own.shape[1]
    total = 0.0
    for k in range(nz):
        scale = every[k][:, part + seg : part + seg + val_count * (n_freq + 1)].astype(jnp.float32)
        scale = scale.reshape(n_parts * cond_count, val_count, n_freq + 1).transpose(1, 0, 2)
        scale = scale.reshape(nx, rows, n_freq + 1)
        scale = scale[..., :n_freq] * scale[..., n_freq:]
        weighted = (lefts[:, k, :, :, None].astype(jnp.float32) * scale[:, :, None, :]).astype(
            jnp.bfloat16
        )
        weighted = weighted.reshape(nx * rows, columns * n_freq)
        piece = right[:, k].reshape(nx, zfold * group, rows, columns)
        piece = piece.transpose(0, 2, 1, 3).reshape(nx * rows, zfold * group * columns)
        total = total + lax.dot_general(
            weighted, piece, (((0,), (0,)), ((), ())), preferred_element_type=jnp.float32
        )
    return (total * factor).reshape(columns, n_freq, zfold * group * columns)


def local(
    shape,
    val_orbitals,
    cond_orbitals,
    val_energy,
    cond_energy,
    val_slot,
    cond_slot,
    eigenvectors,
    frequencies,
):
    nz, ny, nc, nx = shape
    val_count, n_grid = val_orbitals.shape
    cond_count = cond_orbitals.shape[0]
    n_parts = ny * nc * nx
    part = n_grid // n_parts
    seg = part * val_count // cond_count
    columns = eigenvectors.shape[1]
    factor = -1.0 / math.sqrt(val_slot.shape[0] * nz * n_parts)
    packed = pack(
        val_orbitals,
        cond_orbitals,
        val_energy,
        cond_energy,
        val_slot,
        cond_slot,
        frequencies,
        nx,
        ny * nc,
    )
    unit = lax.all_to_all(packed, ("y", "c", "x"), 0, 0, tiled=True)
    unit = unit.reshape(n_parts * cond_count, part + seg + LANES)
    on_tiles = columns % LANES == 0 and seg % LANES == 0
    run = fast if on_tiles and nx == 2 and nz == 4 and val_count == 4 else plain
    return run(
        shape, unit, eigenvectors, part, val_count, cond_count, frequencies.shape[0], factor
    )


def solution(mesh):
    n_pair = mesh.shape["pair"]
    n_proj = mesh.shape["proj"]
    shape = (n_pair // 4, 2, 2, n_proj)
    grid = Mesh(mesh.devices.reshape(shape), AXES)
    return jax.shard_map(
        functools.partial(local, shape),
        mesh=grid,
        in_specs=(
            P(AXES, None),
            P(AXES, None),
            P(AXES),
            P(AXES),
            P(AXES),
            P(AXES),
            P("x", ("z", "y", "c")),
            P(),
        ),
        out_specs=P(("z", "y", "c"), None, "x"),
        check_vma=False,
    )
```

```python
import functools
import math

import jax
import jax.numpy as jnp
from jax import lax
from jax.experimental import pallas as pl
from jax.experimental.pallas import tpu as pltpu
from jax.sharding import Mesh
from jax.sharding import PartitionSpec as P

LANES = 128
AXES = ("z", "y", "c", "x")


def pack_kernel(nx, part, seg, val_energy, cond_energy, val_slot, cond_slot, frequencies, *refs):
    conds = refs[:nx]
    vals = refs[nx : 2 * nx]
    out, extra = refs[2 * nx :]
    val_count = val_energy.shape[0]
    cond_count = cond_energy.shape[0]
    n_freq = frequencies.shape[0]
    stride = n_freq + 1

    @pl.when(pl.program_id(0) == 0)
    def _():
        row = lax.broadcasted_iota(jnp.int32, (cond_count, LANES), 0)
        lane = lax.broadcasted_iota(jnp.int32, (cond_count, LANES), 1)
        cond_level = jnp.zeros((cond_count, LANES), jnp.float32)
        for c in range(cond_count):
            cond_level = jnp.where(row == c, cond_energy[c], cond_level)
        val_level = jnp.zeros((cond_count, LANES), jnp.float32)
        freq = jnp.zeros((cond_count, LANES), jnp.float32)
        is_count = lane < 0
        for v in range(val_count):
            for f in range(stride):
                here = lane == v * stride + f
                val_level = jnp.where(here, val_energy[v], val_level)
                if f < n_freq:
                    freq = jnp.where(here, frequencies[f], freq)
                else:
                    is_count = is_count | here
        gap = cond_level - val_level
        weight = 4.0 * gap / (gap * gap + freq * freq)

        def add(p, number):
            here = (row == cond_slot[p]) & (lane == val_slot[p] * stride + n_freq)
            return number + jnp.where(here, 1.0, 0.0)

        number = lax.fori_loop(0, val_slot.shape[0], add, jnp.zeros((cond_count, LANES), jnp.float32))
        used = lane < val_count * stride
        extra[...] = jnp.where(used, jnp.where(is_count, number, weight), 0.0).astype(jnp.bfloat16)

    for t in range(nx):
        out[t, :, :part] = conds[t][...]
        val = vals[t][...].astype(jnp.float32)
        pieces = [val[:, k * seg : (k + 1) * seg] for k in range(part // seg)]
        out[t, :, part : part + seg] = jnp.concatenate(pieces, axis=0).astype(jnp.bfloat16)
        out[t, :, part + seg :] = extra[...]


def pack(val_orbitals, cond_orbitals, val_energy, cond_energy, val_slot, cond_slot, frequencies, nx, group):
    val_count, n_grid = val_orbitals.shape
    cond_count = cond_orbitals.shape[0]
    n_freq = frequencies.shape[0]
    n_parts = group * nx
    part = n_grid // n_parts
    segs = cond_count // val_count
    seg = part // segs
    width = part + seg + LANES
    if seg % LANES == 0:
        smem = pl.BlockSpec(memory_space=pltpu.SMEM)
        piece = lambda rows: [
            pl.BlockSpec((rows, part), functools.partial(lambda t, i: (0, t * group + i), t))
            for t in range(nx)
        ]
        return pl.pallas_call(
            functools.partial(pack_kernel, nx, part, seg),
            out_shape=jax.ShapeDtypeStruct((n_parts, cond_count, width), jnp.bfloat16),
            grid=(group,),
            in_specs=[smem] * 5 + piece(cond_count) + piece(val_count),
            out_specs=pl.BlockSpec((nx, cond_count, width), lambda i: (i, 0, 0)),
            scratch_shapes=[pltpu.VMEM((cond_count, LANES), jnp.bfloat16)],
            name="pack",
        )(
            val_energy,
            cond_energy,
            val_slot,
            cond_slot,
            frequencies,
            *([cond_orbitals] * nx),
            *([val_orbitals] * nx),
        )
    gap = cond_energy[:, None] - val_energy[None, :]
    weights = (
        4.0 * gap[:, :, None] / (gap[:, :, None] ** 2 + frequencies[None, None, :] ** 2)
    ).astype(jnp.bfloat16)
    chosen = (cond_slot[:, None, None] == jnp.arange(cond_count, dtype=jnp.int32)[None, :, None]) & (
        val_slot[:, None, None] == jnp.arange(val_count, dtype=jnp.int32)[None, None, :]
    )
    counts = jnp.sum(chosen.astype(jnp.float32), axis=0).astype(jnp.bfloat16)
    extra = jnp.concatenate([weights, counts[:, :, None]], axis=2).reshape(
        cond_count, val_count * (n_freq + 1)
    )
    extra = jnp.pad(extra, ((0, 0), (0, LANES - extra.shape[1])))
    cond_parts = cond_orbitals.reshape(cond_count, nx, group, part).transpose(2, 1, 0, 3)
    val_parts = val_orbitals.reshape(val_count, nx, group, segs, seg).transpose(2, 1, 3, 0, 4)
    return jnp.concatenate(
        [
            cond_parts.reshape(n_parts, cond_count, part),
            val_parts.reshape(n_parts, cond_count, seg),
            jnp.broadcast_to(extra, (n_parts,) + extra.shape),
        ],
        axis=2,
    )


def project_kernel(segs, val_count, cond_count, place, *refs):
    conds = refs[:segs]
    val = refs[segs]
    eigs = refs[segs + 1 : 5 * segs + 1]
    keep, send, density, total = refs[5 * segs + 1 :]
    rows = val.shape[0]
    blocks = rows // cond_count
    columns = keep.shape[-1]
    half = keep.shape[-2]
    turn = place[0] * 2

    for k in range(segs):

        @pl.loop(0, blocks)
        def _(j):
            at = pl.ds(pl.multiple_of(j * cond_count, cond_count), cond_count)
            c = conds[k][at, :].astype(jnp.float32)
            vals = val[at, :].astype(jnp.float32)
            for v in range(val_count):
                row = k * val_count + v
                product = (c * vals[row : row + 1, :]).astype(jnp.bfloat16)
                start = lax.bitwise_xor(v, turn) * rows + j * cond_count
                density[pl.ds(pl.multiple_of(start, cond_count), cond_count), :] = product

        eig = jnp.concatenate([eigs[4 * k + q][...] for q in range(4)], axis=1)
        sums = jnp.dot(density[...], eig, preferred_element_type=jnp.float32)
        if k == 0:

            @pl.when(pl.program_id(0) == 0)
            def _():
                total[...] = sums

            @pl.when(pl.program_id(0) > 0)
            def _():
                total[...] += sums
        else:
            total[...] += sums

    @pl.when(pl.program_id(0) == pl.num_programs(0) - 1)
    def _():
        for q in range(4):
            out = send if q % 2 else keep
            for h in range(2):
                out[q // 2, h] = total[h * half : (h + 1) * half, q * columns : (q + 1) * columns]


def project(unit, eigs, place, val_count, cond_count):
    part, columns = eigs[0].shape
    segs = cond_count // val_count
    seg = part // segs
    rows = unit.shape[0]
    half = rows * val_count // 2
    width = math.gcd(seg, 384)
    steps = seg // width
    in_specs = (
        [
            pl.BlockSpec((rows, width), functools.partial(lambda k, i, place: (0, k * steps + i), k))
            for k in range(segs)
        ]
        + [pl.BlockSpec((rows, width), lambda i, place: (0, segs * steps + i))]
        + [
            pl.BlockSpec((width, columns), functools.partial(lambda k, i, place: (k * steps + i, 0), k))
            for k in range(segs)
            for q in range(4)
        ]
    )
    shape = (2, 2, half, columns)
    out = jax.ShapeDtypeStruct(shape, jnp.float32)
    out_spec = pl.BlockSpec(shape, lambda i, place: (0, 0, 0, 0))
    return pl.pallas_call(
        functools.partial(project_kernel, segs, val_count, cond_count),
        out_shape=[out, out],
        grid_spec=pltpu.PrefetchScalarGridSpec(
            num_scalar_prefetch=1,
            grid=(steps,),
            in_specs=in_specs,
            out_specs=[out_spec, out_spec],
            scratch_shapes=[
                pltpu.VMEM((2 * half, width), jnp.bfloat16),
                pltpu.VMEM((2 * half, 4 * columns), jnp.float32),
            ],
        ),
        compiler_params=pltpu.CompilerParams(vmem_limit_bytes=32 * 1024 * 1024),
        cost_estimate=pl.CostEstimate(
            flops=16 * half * part * columns,
            bytes_accessed=2 * (unit.size + 4 * part * columns),
            transcendentals=0,
        ),
        name="project",
    )(place, *([unit] * (segs + 1)), *(list(eigs) * segs))


def weigh(owns, mates, scales, mine, n_freq, out):
    slots = len(owns)
    rows, columns = owns[0].shape
    stride = n_freq + 1
    width = scales[0].shape[0]
    for k in range(slots):
        scale = scales[k][...].astype(jnp.float32).T
        own = owns[k][...].astype(jnp.float32).T
        mate = mates[k][...].astype(jnp.float32).T
        for h in range(2):
            coeffs = jnp.where(mine == h, own, mate)
            for at in range(0, rows, width):
                v = (h * rows + at) // width
                number = scale[v * stride + n_freq : v * stride + n_freq + 1, :]
                for f in range(n_freq):
                    one = scale[v * stride + f : v * stride + f + 1, :] * number
                    out[k, f * columns : (f + 1) * columns, h * rows + at : h * rows + at + width] = (
                        coeffs[:, at : at + width] * one
                    ).astype(jnp.bfloat16)


def chi_kernel(early, late, n_freq, factor, scalars, *refs):
    slots = early + late
    owns = refs[:slots]
    mates = refs[slots : 2 * slots]
    scales = refs[2 * slots : 3 * slots]
    rights_a = refs[3 * slots : 3 * slots + 4]
    rights_b = refs[3 * slots + 4 : -2]
    out, weighted = refs[-2:]
    columns = out.shape[0]

    @pl.when(pl.program_id(0) == 0)
    def _():
        weigh(owns, mates, scales, scalars[4], n_freq, weighted)

    core = scalars[2]
    same_y = scalars[1] == lax.rem(pl.program_id(0), 2)
    shift = lax.bitwise_xor(scalars[0], scalars[3] + pl.program_id(0) // 2)
    left, right = [], []
    for r in range(slots):
        left.append(weighted[lax.bitwise_xor(shift, r)])
        for h in range(2):
            if r < early:
                pair = [rights_a[2 * h + c][0, r] for c in range(2)]
            else:
                own, other, mate, both = [rights_b[8 * (r - early) + 4 * h + q][0] for q in range(4)]
                own = jnp.where(same_y, own, other)
                mate = jnp.where(same_y, mate, both)
                pair = [jnp.where(core == c, own, mate) for c in range(2)]
            right.append(jnp.concatenate(pair, axis=1))
    chi = jnp.dot(
        jnp.concatenate(left, axis=1),
        jnp.concatenate(right, axis=0),
        preferred_element_type=jnp.float32,
    )
    for f in range(n_freq):
        out[:, f, :] = chi[f * columns : (f + 1) * columns, :] * factor


def make_chi(owns, mates, units, right_a, rights_b, scalars, n_freq, factor):
    members, early, rows, columns = right_a.shape
    tiles = members // 4
    late = len(rights_b)
    slots = early + late
    width = units[0].shape[0]
    last = units[0].shape[1] // LANES - 1
    flops = 4 * slots * rows * n_freq * columns * tiles * 2 * columns

    def near(h, i, scalars):
        return (lax.bitwise_xor(scalars[0], h * 2 + i // 2), 0, 0)

    return pl.pallas_call(
        functools.partial(chi_kernel, early, late, n_freq, factor),
        out_shape=jax.ShapeDtypeStruct((columns, n_freq, tiles * 2 * columns), jnp.float32),
        grid_spec=pltpu.PrefetchScalarGridSpec(
            num_scalar_prefetch=1,
            grid=(tiles,),
            in_specs=[pl.BlockSpec((rows, columns), lambda i, scalars: (0, 0))] * (2 * slots)
            + [pl.BlockSpec((width, LANES), lambda i, scalars: (0, last))] * slots
            + [
                pl.BlockSpec(
                    (1, early, rows, columns),
                    functools.partial(
                        lambda h, c, i, scalars: (h * tiles * 2 + i * 2 + c, 0, 0, 0), h, c
                    ),
                )
                for h in range(2)
                for c in range(2)
            ]
            + [
                pl.BlockSpec((1, rows, columns), functools.partial(near, h))
                for r in range(late)
                for h in range(2)
                for q in range(4)
            ],
            out_specs=pl.BlockSpec((columns, n_freq, 2 * columns), lambda i, scalars: (0, 0, i)),
            scratch_shapes=[pltpu.VMEM((slots, n_freq * columns, 2 * rows), jnp.bfloat16)],
        ),
        compiler_params=pltpu.CompilerParams(vmem_limit_bytes=32 * 1024 * 1024),
        cost_estimate=pl.CostEstimate(
            flops=flops,
            bytes_accessed=2 * (early + late) * members * rows * columns
            + 4 * columns * n_freq * tiles * 2 * columns,
            transcendentals=0,
        ),
        name="chi",
    )(scalars, *owns, *mates, *units, *([right_a] * 4), *[a for four in rights_b for a in four * 2])


def fast(shape, unit, eigenvectors, part, val_count, cond_count, n_freq, factor):
    nz, ny, nc, nx = shape
    z, y, c, x = [lax.axis_index(name).astype(jnp.int32) for name in AXES]
    columns = eigenvectors.shape[1]
    places = [(i, j, k, t) for i in range(nz) for j in range(ny) for k in range(nc) for t in range(nx)]
    number = {place: at for at, place in enumerate(places)}

    def send(array, target):
        pairs = [(number[place], target(*place)) for place in places]
        return lax.ppermute(
            array, AXES, [(source, number[to]) for source, to in pairs if to is not None]
        )

    def along_z(array, moves):
        moves = dict(moves)
        return send(array, lambda i, j, k, t: (moves[i], j, k, t) if i in moves else None)

    here = y * nc + c
    eigs = []
    for k in range(ny * nc):
        at = lax.bitwise_xor(here, k) * part
        rows = lax.dynamic_slice_in_dim(eigenvectors, at, part, 0)
        eigs.append(
            send(rows, functools.partial(lambda q, i, j, k, t: (i, j ^ (q // 2), k ^ (q % 2), t), k))
            if k
            else rows
        )

    inner = (z == 1) | (z == 2)
    near = along_z(unit, [(0, 1), (1, 0), (2, 3), (3, 2)])
    middle = along_z(unit, [(1, 2), (2, 1)])
    across = along_z(near, [(1, 2), (2, 1)])
    outward = along_z(middle, [(1, 0), (2, 3)])
    far = along_z(across, [(1, 0), (2, 3)])
    units = [unit, near, jnp.where(inner, across, outward), jnp.where(inner, middle, far)]

    place = x[None]

    def coefficients(unit, ready=None):
        keep, away = project(unit, eigs, place, val_count, cond_count)
        sums = keep + send(away, lambda i, j, k, t: (i, j, 1 - k, t))
        if ready is not None:
            sums, _ = lax.optimization_barrier((sums, ready))
        total = sums[0, 0] + send(sums[0, 1], lambda i, j, k, t: (i, j, k, 1 - t))
        total = total + send(sums[1, 0], lambda i, j, k, t: (i, 1 - j, k, t))
        total = total + send(sums[1, 1], lambda i, j, k, t: (i, 1 - j, k, 1 - t))
        return total.astype(jnp.bfloat16)

    def mate(own):
        return send(own, lambda i, j, k, t: (i, j, k, 1 - t))

    def share(own, m):
        return send(own, lambda i, j, k, t: ((2 * t + i % 2) ^ m, j, k, i // 2))

    def spread(own):
        shares = [share(own, m) for m in range(nz)]
        shares, paired = lax.optimization_barrier((shares, mate(own)))
        held = jnp.stack(shares)
        other = send(held, lambda i, j, k, t: (i, 1 - j, k, t))
        across_core = lambda i, j, k, t: (i, j, 1 - k, t)
        return (held, other, send(held, across_core), send(other, across_core)), paired

    owns = [coefficients(units[k]) for k in range(2)]
    share_a = share(jnp.stack(owns), 0)
    right_a = lax.all_gather(share_a, ("z", "y", "c"), axis=0)
    mates = [mate(own) for own in owns]
    owns.append(coefficients(units[2], far))
    units[3], _ = lax.optimization_barrier((units[3], (share_a, mates)))
    owns.append(coefficients(units[3]))
    rights_b = []
    for own in owns[2:]:
        four, paired = spread(own)
        rights_b.append(four)
        mates.append(paired)
    scalars = jnp.stack([z, y, c, 2 * x, x])
    return make_chi(owns, mates, units, right_a, rights_b, scalars, n_freq, factor)


def plain(shape, unit, eigenvectors, part, val_count, cond_count, n_freq, factor):
    nz, ny, nc, nx = shape
    z = lax.axis_index("z").astype(jnp.int32)
    x = lax.axis_index("x").astype(jnp.int32)
    group = ny * nc
    n_parts = group * nx
    segs = cond_count // val_count
    seg = part // segs
    columns = eigenvectors.shape[1]
    zfold = nz // nx
    eigs = lax.all_to_all(
        eigenvectors.reshape(group, part, columns), ("y", "c"), 0, 0, tiled=True
    )
    every = lax.all_gather(unit, "z", axis=0)

    def coefficients(unit):
        cond = unit[:, :part].reshape(1, n_parts, cond_count, segs, seg)
        val = unit[:, part : part + seg].reshape(n_parts, segs, val_count, seg)
        val = val.transpose(2, 0, 1, 3)[:, :, None]
        density = (cond.astype(jnp.float32) * val.astype(jnp.float32)).astype(jnp.bfloat16)
        sums = jnp.einsum(
            "pg,qgs->qps", density.reshape(-1, part), eigs, preferred_element_type=jnp.float32
        )
        sums = sums.reshape(n_parts, -1, columns)
        sums = lax.all_to_all(sums, ("y", "c", "x"), 0, 0, tiled=True)
        return jnp.sum(sums, axis=0).astype(jnp.bfloat16)

    own = jnp.stack([coefficients(every[k]) for k in range(nz)])
    lefts = lax.all_gather(own, "x", axis=0)
    perm = []
    for s in range(nz):
        for q in range(group):
            for t in range(nx):
                target = ((s % zfold + zfold * t) * group + q) * nx + s // zfold
                perm.append(((s * group + q) * nx + t, target))
    share = lax.ppermute(own, AXES, perm)
    right = lax.all_gather(share, ("z", "y", "c"), axis=0)
    rows = own.shape[1]
    total = 0.0
    for k in range(nz):
        scale = every[k][:, part + seg : part + seg + val_count * (n_freq + 1)].astype(jnp.float32)
        scale = scale.reshape(n_parts * cond_count, val_count, n_freq + 1).transpose(1, 0, 2)
        scale = scale.reshape(nx, rows, n_freq + 1)
        scale = scale[..., :n_freq] * scale[..., n_freq:]
        weighted = (lefts[:, k, :, :, None].astype(jnp.float32) * scale[:, :, None, :]).astype(
            jnp.bfloat16
        )
        weighted = weighted.reshape(nx * rows, columns * n_freq)
        piece = right[:, k].reshape(nx, zfold * group, rows, columns)
        piece = piece.transpose(0, 2, 1, 3).reshape(nx * rows, zfold * group * columns)
        total = total + lax.dot_general(
            weighted, piece, (((0,), (0,)), ((), ())), preferred_element_type=jnp.float32
        )
    return (total * factor).reshape(columns, n_freq, zfold * group * columns)


def local(
    shape,
    val_orbitals,
    cond_orbitals,
    val_energy,
    cond_energy,
    val_slot,
    cond_slot,
    eigenvectors,
    frequencies,
):
    nz, ny, nc, nx = shape
    val_count, n_grid = val_orbitals.shape
    cond_count = cond_orbitals.shape[0]
    n_parts = ny * nc * nx
    part = n_grid // n_parts
    seg = part * val_count // cond_count
    columns = eigenvectors.shape[1]
    factor = -1.0 / math.sqrt(val_slot.shape[0] * nz * n_parts)
    packed = pack(
        val_orbitals,
        cond_orbitals,
        val_energy,
        cond_energy,
        val_slot,
        cond_slot,
        frequencies,
        nx,
        ny * nc,
    )
    unit = lax.all_to_all(packed, ("y", "c", "x"), 0, 0, tiled=True)
    unit = unit.reshape(n_parts * cond_count, part + seg + LANES)
    on_tiles = columns % LANES == 0 and seg % LANES == 0
    run = fast if on_tiles and nx == 2 and nz == 4 and val_count == 4 else plain
    return run(
        shape, unit, eigenvectors, part, val_count, cond_count, frequencies.shape[0], factor
    )


def solution(mesh):
    n_pair = mesh.shape["pair"]
    n_proj = mesh.shape["proj"]
    shape = (n_pair // 4, 2, 2, n_proj)
    grid = Mesh(mesh.devices.reshape(shape), AXES)
    return jax.shard_map(
        functools.partial(local, shape),
        mesh=grid,
        in_specs=(
            P(AXES, None),
            P(AXES, None),
            P(AXES),
            P(AXES),
            P(AXES),
            P(AXES),
            P("x", ("z", "y", "c")),
            P(),
        ),
        out_specs=P(("z", "y", "c"), None, "x"),
        check_vma=False,
    )
```

```python
import functools
import math

import jax
import jax.numpy as jnp
from jax import lax
from jax.experimental import pallas as pl
from jax.experimental.pallas import tpu as pltpu
from jax.sharding import Mesh
from jax.sharding import PartitionSpec as P

LANES = 128
AXES = ("z", "y", "c", "x")


def pack_kernel(nx, part, seg, val_energy, cond_energy, val_slot, cond_slot, frequencies, *refs):
    conds = refs[:nx]
    vals = refs[nx : 2 * nx]
    out, extra = refs[2 * nx :]
    val_count = val_energy.shape[0]
    cond_count = cond_energy.shape[0]
    n_freq = frequencies.shape[0]
    stride = n_freq + 1

    @pl.when(pl.program_id(0) == 0)
    def _():
        row = lax.broadcasted_iota(jnp.int32, (cond_count, LANES), 0)
        lane = lax.broadcasted_iota(jnp.int32, (cond_count, LANES), 1)
        cond_level = jnp.zeros((cond_count, LANES), jnp.float32)
        for c in range(cond_count):
            cond_level = jnp.where(row == c, cond_energy[c], cond_level)
        val_level = jnp.zeros((cond_count, LANES), jnp.float32)
        freq = jnp.zeros((cond_count, LANES), jnp.float32)
        is_count = lane < 0
        for v in range(val_count):
            for f in range(stride):
                here = lane == v * stride + f
                val_level = jnp.where(here, val_energy[v], val_level)
                if f < n_freq:
                    freq = jnp.where(here, frequencies[f], freq)
                else:
                    is_count = is_count | here
        gap = cond_level - val_level
        weight = 4.0 * gap / (gap * gap + freq * freq)

        def add(p, number):
            here = (row == cond_slot[p]) & (lane == val_slot[p] * stride + n_freq)
            return number + jnp.where(here, 1.0, 0.0)

        number = lax.fori_loop(0, val_slot.shape[0], add, jnp.zeros((cond_count, LANES), jnp.float32))
        used = lane < val_count * stride
        extra[...] = jnp.where(used, jnp.where(is_count, number, weight), 0.0).astype(jnp.bfloat16)

    for t in range(nx):
        out[t, :, :part] = conds[t][...]
        val = vals[t][...].astype(jnp.float32)
        pieces = [val[:, k * seg : (k + 1) * seg] for k in range(part // seg)]
        out[t, :, part : part + seg] = jnp.concatenate(pieces, axis=0).astype(jnp.bfloat16)
        out[t, :, part + seg :] = extra[...]


def pack(val_orbitals, cond_orbitals, val_energy, cond_energy, val_slot, cond_slot, frequencies, nx, group):
    val_count, n_grid = val_orbitals.shape
    cond_count = cond_orbitals.shape[0]
    n_freq = frequencies.shape[0]
    n_parts = group * nx
    part = n_grid // n_parts
    segs = cond_count // val_count
    seg = part // segs
    width = part + seg + LANES
    if seg % LANES == 0:
        smem = pl.BlockSpec(memory_space=pltpu.SMEM)
        piece = lambda rows: [
            pl.BlockSpec((rows, part), functools.partial(lambda t, i: (0, t * group + i), t))
            for t in range(nx)
        ]
        return pl.pallas_call(
            functools.partial(pack_kernel, nx, part, seg),
            out_shape=jax.ShapeDtypeStruct((n_parts, cond_count, width), jnp.bfloat16),
            grid=(group,),
            in_specs=[smem] * 5 + piece(cond_count) + piece(val_count),
            out_specs=pl.BlockSpec((nx, cond_count, width), lambda i: (i, 0, 0)),
            scratch_shapes=[pltpu.VMEM((cond_count, LANES), jnp.bfloat16)],
            name="pack",
        )(
            val_energy,
            cond_energy,
            val_slot,
            cond_slot,
            frequencies,
            *([cond_orbitals] * nx),
            *([val_orbitals] * nx),
        )
    gap = cond_energy[:, None] - val_energy[None, :]
    weights = (
        4.0 * gap[:, :, None] / (gap[:, :, None] ** 2 + frequencies[None, None, :] ** 2)
    ).astype(jnp.bfloat16)
    chosen = (cond_slot[:, None, None] == jnp.arange(cond_count, dtype=jnp.int32)[None, :, None]) & (
        val_slot[:, None, None] == jnp.arange(val_count, dtype=jnp.int32)[None, None, :]
    )
    counts = jnp.sum(chosen.astype(jnp.float32), axis=0).astype(jnp.bfloat16)
    extra = jnp.concatenate([weights, counts[:, :, None]], axis=2).reshape(
        cond_count, val_count * (n_freq + 1)
    )
    extra = jnp.pad(extra, ((0, 0), (0, LANES - extra.shape[1])))
    cond_parts = cond_orbitals.reshape(cond_count, nx, group, part).transpose(2, 1, 0, 3)
    val_parts = val_orbitals.reshape(val_count, nx, group, segs, seg).transpose(2, 1, 3, 0, 4)
    return jnp.concatenate(
        [
            cond_parts.reshape(n_parts, cond_count, part),
            val_parts.reshape(n_parts, cond_count, seg),
            jnp.broadcast_to(extra, (n_parts,) + extra.shape),
        ],
        axis=2,
    )


def project_kernel(segs, val_count, cond_count, place, *refs):
    conds = refs[:segs]
    val = refs[segs]
    eigs = refs[segs + 1 : 5 * segs + 1]
    keep, send, density, total = refs[5 * segs + 1 :]
    rows = val.shape[0]
    blocks = rows // cond_count
    columns = keep.shape[-1]
    half = keep.shape[-2]
    turn = place[0] * 2

    for k in range(segs):

        @pl.loop(0, blocks)
        def _(j):
            at = pl.ds(pl.multiple_of(j * cond_count, cond_count), cond_count)
            c = conds[k][at, :].astype(jnp.float32)
            vals = val[at, :].astype(jnp.float32)
            for v in range(val_count):
                row = k * val_count + v
                product = (c * vals[row : row + 1, :]).astype(jnp.bfloat16)
                start = lax.bitwise_xor(v, turn) * rows + j * cond_count
                density[pl.ds(pl.multiple_of(start, cond_count), cond_count), :] = product

        eig = jnp.concatenate([eigs[4 * k + q][...] for q in range(4)], axis=1)
        sums = jnp.dot(density[...], eig, preferred_element_type=jnp.float32)
        if k == 0:

            @pl.when(pl.program_id(0) == 0)
            def _():
                total[...] = sums

            @pl.when(pl.program_id(0) > 0)
            def _():
                total[...] += sums
        else:
            total[...] += sums

    @pl.when(pl.program_id(0) == pl.num_programs(0) - 1)
    def _():
        for q in range(4):
            out = send if q % 2 else keep
            for h in range(2):
                out[q // 2, h] = total[h * half : (h + 1) * half, q * columns : (q + 1) * columns]


def project(unit, eigs, place, val_count, cond_count):
    part, columns = eigs[0].shape
    segs = cond_count // val_count
    seg = part // segs
    rows = unit.shape[0]
    half = rows * val_count // 2
    width = math.gcd(seg, 384)
    steps = seg // width
    in_specs = (
        [
            pl.BlockSpec((rows, width), functools.partial(lambda k, i, place: (0, k * steps + i), k))
            for k in range(segs)
        ]
        + [pl.BlockSpec((rows, width), lambda i, place: (0, segs * steps + i))]
        + [
            pl.BlockSpec((width, columns), functools.partial(lambda k, i, place: (k * steps + i, 0), k))
            for k in range(segs)
            for q in range(4)
        ]
    )
    shape = (2, 2, half, columns)
    out = jax.ShapeDtypeStruct(shape, jnp.float32)
    out_spec = pl.BlockSpec(shape, lambda i, place: (0, 0, 0, 0))
    return pl.pallas_call(
        functools.partial(project_kernel, segs, val_count, cond_count),
        out_shape=[out, out],
        grid_spec=pltpu.PrefetchScalarGridSpec(
            num_scalar_prefetch=1,
            grid=(steps,),
            in_specs=in_specs,
            out_specs=[out_spec, out_spec],
            scratch_shapes=[
                pltpu.VMEM((2 * half, width), jnp.bfloat16),
                pltpu.VMEM((2 * half, 4 * columns), jnp.float32),
            ],
        ),
        compiler_params=pltpu.CompilerParams(vmem_limit_bytes=32 * 1024 * 1024),
        cost_estimate=pl.CostEstimate(
            flops=16 * half * part * columns,
            bytes_accessed=2 * (unit.size + 4 * part * columns),
            transcendentals=0,
        ),
        name="project",
    )(place, *([unit] * (segs + 1)), *(list(eigs) * segs))


def weigh(owns, mates, scales, mine, n_freq, out):
    slots = len(owns)
    rows, columns = owns[0].shape
    stride = n_freq + 1
    width = scales[0].shape[0]
    for k in range(slots):
        scale = scales[k][...].astype(jnp.float32).T
        own = owns[k][...].astype(jnp.float32).T
        mate = mates[k][...].astype(jnp.float32).T
        for h in range(2):
            coeffs = jnp.where(mine == h, own, mate)
            for at in range(0, rows, width):
                v = (h * rows + at) // width
                number = scale[v * stride + n_freq : v * stride + n_freq + 1, :]
                for f in range(n_freq):
                    one = scale[v * stride + f : v * stride + f + 1, :] * number
                    out[k, f * columns : (f + 1) * columns, h * rows + at : h * rows + at + width] = (
                        coeffs[:, at : at + width] * one
                    ).astype(jnp.bfloat16)


def chi_kernel(early, late, n_freq, factor, scalars, *refs):
    slots = early + late
    owns = refs[:slots]
    mates = refs[slots : 2 * slots]
    scales = refs[2 * slots : 3 * slots]
    rights_a = refs[3 * slots : 3 * slots + 4]
    rights_b = refs[3 * slots + 4 : -2]
    out, weighted = refs[-2:]
    columns = out.shape[0]

    @pl.when(pl.program_id(0) == 0)
    def _():
        weigh(owns, mates, scales, scalars[4], n_freq, weighted)

    core = scalars[2]
    same_y = scalars[1] == lax.rem(pl.program_id(0), 2)
    shift = lax.bitwise_xor(scalars[0], scalars[3] + pl.program_id(0) // 2)
    left, right = [], []
    for r in range(slots):
        left.append(weighted[lax.bitwise_xor(shift, r)])
        for h in range(2):
            if r < early:
                pair = [rights_a[2 * h + c][0, r] for c in range(2)]
            else:
                own, other, mate, both = [rights_b[8 * (r - early) + 4 * h + q][0] for q in range(4)]
                own = jnp.where(same_y, own, other)
                mate = jnp.where(same_y, mate, both)
                pair = [jnp.where(core == c, own, mate) for c in range(2)]
            right.append(jnp.concatenate(pair, axis=1))
    chi = jnp.dot(
        jnp.concatenate(left, axis=1),
        jnp.concatenate(right, axis=0),
        preferred_element_type=jnp.float32,
    )
    for f in range(n_freq):
        out[:, f, :] = chi[f * columns : (f + 1) * columns, :] * factor


def make_chi(owns, mates, units, right_a, rights_b, scalars, n_freq, factor):
    members, early, rows, columns = right_a.shape
    tiles = members // 4
    late = len(rights_b)
    slots = early + late
    width = units[0].shape[0]
    last = units[0].shape[1] // LANES - 1
    flops = 4 * slots * rows * n_freq * columns * tiles * 2 * columns

    def near(h, i, scalars):
        return (lax.bitwise_xor(scalars[0], h * 2 + i // 2), 0, 0)

    return pl.pallas_call(
        functools.partial(chi_kernel, early, late, n_freq, factor),
        out_shape=jax.ShapeDtypeStruct((columns, n_freq, tiles * 2 * columns), jnp.float32),
        grid_spec=pltpu.PrefetchScalarGridSpec(
            num_scalar_prefetch=1,
            grid=(tiles,),
            in_specs=[pl.BlockSpec((rows, columns), lambda i, scalars: (0, 0))] * (2 * slots)
            + [pl.BlockSpec((width, LANES), lambda i, scalars: (0, last))] * slots
            + [
                pl.BlockSpec(
                    (1, early, rows, columns),
                    functools.partial(
                        lambda h, c, i, scalars: (h * tiles * 2 + i * 2 + c, 0, 0, 0), h, c
                    ),
                )
                for h in range(2)
                for c in range(2)
            ]
            + [
                pl.BlockSpec((1, rows, columns), functools.partial(near, h))
                for r in range(late)
                for h in range(2)
                for q in range(4)
            ],
            out_specs=pl.BlockSpec((columns, n_freq, 2 * columns), lambda i, scalars: (0, 0, i)),
            scratch_shapes=[pltpu.VMEM((slots, n_freq * columns, 2 * rows), jnp.bfloat16)],
        ),
        compiler_params=pltpu.CompilerParams(vmem_limit_bytes=32 * 1024 * 1024),
        cost_estimate=pl.CostEstimate(
            flops=flops,
            bytes_accessed=2 * (early + late) * members * rows * columns
            + 4 * columns * n_freq * tiles * 2 * columns,
            transcendentals=0,
        ),
        name="chi",
    )(scalars, *owns, *mates, *units, *([right_a] * 4), *[a for four in rights_b for a in four * 2])


def fast(shape, unit, eigenvectors, part, val_count, cond_count, n_freq, factor):
    nz, ny, nc, nx = shape
    z, y, c, x = [lax.axis_index(name).astype(jnp.int32) for name in AXES]
    columns = eigenvectors.shape[1]
    places = [(i, j, k, t) for i in range(nz) for j in range(ny) for k in range(nc) for t in range(nx)]
    number = {place: at for at, place in enumerate(places)}

    def send(array, target):
        pairs = [(number[place], target(*place)) for place in places]
        return lax.ppermute(
            array, AXES, [(source, number[to]) for source, to in pairs if to is not None]
        )

    def along_z(array, moves):
        moves = dict(moves)
        return send(array, lambda i, j, k, t: (moves[i], j, k, t) if i in moves else None)

    here = y * nc + c
    eigs = []
    for k in range(ny * nc):
        at = lax.bitwise_xor(here, k) * part
        rows = lax.dynamic_slice_in_dim(eigenvectors, at, part, 0)
        eigs.append(
            send(rows, functools.partial(lambda q, i, j, k, t: (i, j ^ (q // 2), k ^ (q % 2), t), k))
            if k
            else rows
        )

    inner = (z == 1) | (z == 2)
    near = along_z(unit, [(0, 1), (1, 0), (2, 3), (3, 2)])
    middle = along_z(unit, [(1, 2), (2, 1)])
    across = along_z(near, [(1, 2), (2, 1)])
    outward = along_z(middle, [(1, 0), (2, 3)])
    far = along_z(across, [(1, 0), (2, 3)])
    units = [unit, near, jnp.where(inner, across, outward)]

    place = x[None]

    def coefficients(unit, ready=None):
        keep, away = project(unit, eigs, place, val_count, cond_count)
        sums = keep + send(away, lambda i, j, k, t: (i, j, 1 - k, t))
        if ready is not None:
            sums, _ = lax.optimization_barrier((sums, ready))
        total = sums[0, 0] + send(sums[0, 1], lambda i, j, k, t: (i, j, k, 1 - t))
        total = total + send(sums[1, 0], lambda i, j, k, t: (i, 1 - j, k, t))
        total = total + send(sums[1, 1], lambda i, j, k, t: (i, 1 - j, k, 1 - t))
        return total.astype(jnp.bfloat16)

    def mate(own):
        return send(own, lambda i, j, k, t: (i, j, k, 1 - t))

    def share(own, m):
        return send(own, lambda i, j, k, t: ((2 * t + i % 2) ^ m, j, k, i // 2))

    def spread(own):
        shares = [share(own, m) for m in range(nz)]
        shares, paired = lax.optimization_barrier((shares, mate(own)))
        held = jnp.stack(shares)
        other = send(held, lambda i, j, k, t: (i, 1 - j, k, t))
        across_core = lambda i, j, k, t: (i, j, 1 - k, t)
        return (held, other, send(held, across_core), send(other, across_core)), paired

    owns = [coefficients(units[0], (across, outward))] + [coefficients(units[k]) for k in (1, 2)]
    own_a = jnp.stack(owns)
    share_a, mate_a, far = lax.optimization_barrier((share(own_a, 0), mate(own_a), far))
    right_a = lax.all_gather(share_a, ("z", "y", "c"), axis=0)
    units.append(jnp.where(inner, middle, far))
    own_b = coefficients(units[3])
    four, mate_b = spread(own_b)
    owns.append(own_b)
    mates = [mate_a[k] for k in range(3)] + [mate_b]
    rights_b = [four]
    scalars = jnp.stack([z, y, c, 2 * x, x])
    return make_chi(owns, mates, units, right_a, rights_b, scalars, n_freq, factor)


def plain(shape, unit, eigenvectors, part, val_count, cond_count, n_freq, factor):
    nz, ny, nc, nx = shape
    z = lax.axis_index("z").astype(jnp.int32)
    x = lax.axis_index("x").astype(jnp.int32)
    group = ny * nc
    n_parts = group * nx
    segs = cond_count // val_count
    seg = part // segs
    columns = eigenvectors.shape[1]
    zfold = nz // nx
    eigs = lax.all_to_all(
        eigenvectors.reshape(group, part, columns), ("y", "c"), 0, 0, tiled=True
    )
    every = lax.all_gather(unit, "z", axis=0)

    def coefficients(unit):
        cond = unit[:, :part].reshape(1, n_parts, cond_count, segs, seg)
        val = unit[:, part : part + seg].reshape(n_parts, segs, val_count, seg)
        val = val.transpose(2, 0, 1, 3)[:, :, None]
        density = (cond.astype(jnp.float32) * val.astype(jnp.float32)).astype(jnp.bfloat16)
        sums = jnp.einsum(
            "pg,qgs->qps", density.reshape(-1, part), eigs, preferred_element_type=jnp.float32
        )
        sums = sums.reshape(n_parts, -1, columns)
        sums = lax.all_to_all(sums, ("y", "c", "x"), 0, 0, tiled=True)
        return jnp.sum(sums, axis=0).astype(jnp.bfloat16)

    own = jnp.stack([coefficients(every[k]) for k in range(nz)])
    lefts = lax.all_gather(own, "x", axis=0)
    perm = []
    for s in range(nz):
        for q in range(group):
            for t in range(nx):
                target = ((s % zfold + zfold * t) * group + q) * nx + s // zfold
                perm.append(((s * group + q) * nx + t, target))
    share = lax.ppermute(own, AXES, perm)
    right = lax.all_gather(share, ("z", "y", "c"), axis=0)
    rows = own.shape[1]
    total = 0.0
    for k in range(nz):
        scale = every[k][:, part + seg : part + seg + val_count * (n_freq + 1)].astype(jnp.float32)
        scale = scale.reshape(n_parts * cond_count, val_count, n_freq + 1).transpose(1, 0, 2)
        scale = scale.reshape(nx, rows, n_freq + 1)
        scale = scale[..., :n_freq] * scale[..., n_freq:]
        weighted = (lefts[:, k, :, :, None].astype(jnp.float32) * scale[:, :, None, :]).astype(
            jnp.bfloat16
        )
        weighted = weighted.reshape(nx * rows, columns * n_freq)
        piece = right[:, k].reshape(nx, zfold * group, rows, columns)
        piece = piece.transpose(0, 2, 1, 3).reshape(nx * rows, zfold * group * columns)
        total = total + lax.dot_general(
            weighted, piece, (((0,), (0,)), ((), ())), preferred_element_type=jnp.float32
        )
    return (total * factor).reshape(columns, n_freq, zfold * group * columns)


def local(
    shape,
    val_orbitals,
    cond_orbitals,
    val_energy,
    cond_energy,
    val_slot,
    cond_slot,
    eigenvectors,
    frequencies,
):
    nz, ny, nc, nx = shape
    val_count, n_grid = val_orbitals.shape
    cond_count = cond_orbitals.shape[0]
    n_parts = ny * nc * nx
    part = n_grid // n_parts
    seg = part * val_count // cond_count
    columns = eigenvectors.shape[1]
    factor = -1.0 / math.sqrt(val_slot.shape[0] * nz * n_parts)
    packed = pack(
        val_orbitals,
        cond_orbitals,
        val_energy,
        cond_energy,
        val_slot,
        cond_slot,
        frequencies,
        nx,
        ny * nc,
    )
    unit = lax.all_to_all(packed, ("y", "c", "x"), 0, 0, tiled=True)
    unit = unit.reshape(n_parts * cond_count, part + seg + LANES)
    on_tiles = columns % LANES == 0 and seg % LANES == 0
    run = fast if on_tiles and nx == 2 and nz == 4 and val_count == 4 else plain
    return run(
        shape, unit, eigenvectors, part, val_count, cond_count, frequencies.shape[0], factor
    )


def solution(mesh):
    n_pair = mesh.shape["pair"]
    n_proj = mesh.shape["proj"]
    shape = (n_pair // 4, 2, 2, n_proj)
    grid = Mesh(mesh.devices.reshape(shape), AXES)
    return jax.shard_map(
        functools.partial(local, shape),
        mesh=grid,
        in_specs=(
            P(AXES, None),
            P(AXES, None),
            P(AXES),
            P(AXES),
            P(AXES),
            P(AXES),
            P("x", ("z", "y", "c")),
            P(),
        ),
        out_specs=P(("z", "y", "c"), None, "x"),
        check_vma=False,
    )
```

```python
import functools
import math

import jax
import jax.numpy as jnp
from jax import lax
from jax.experimental import pallas as pl
from jax.experimental.pallas import tpu as pltpu
from jax.sharding import Mesh
from jax.sharding import PartitionSpec as P

LANES = 128
AXES = ("z", "y", "c", "x")


def pack_kernel(nx, part, seg, val_energy, cond_energy, val_slot, cond_slot, frequencies, *refs):
    conds = refs[:nx]
    vals = refs[nx : 2 * nx]
    out, extra = refs[2 * nx :]
    val_count = val_energy.shape[0]
    cond_count = cond_energy.shape[0]
    n_freq = frequencies.shape[0]
    stride = n_freq + 1

    @pl.when(pl.program_id(0) == 0)
    def _():
        row = lax.broadcasted_iota(jnp.int32, (cond_count, LANES), 0)
        lane = lax.broadcasted_iota(jnp.int32, (cond_count, LANES), 1)
        cond_level = jnp.zeros((cond_count, LANES), jnp.float32)
        for c in range(cond_count):
            cond_level = jnp.where(row == c, cond_energy[c], cond_level)
        val_level = jnp.zeros((cond_count, LANES), jnp.float32)
        freq = jnp.zeros((cond_count, LANES), jnp.float32)
        is_count = lane < 0
        for v in range(val_count):
            for f in range(stride):
                here = lane == v * stride + f
                val_level = jnp.where(here, val_energy[v], val_level)
                if f < n_freq:
                    freq = jnp.where(here, frequencies[f], freq)
                else:
                    is_count = is_count | here
        gap = cond_level - val_level
        weight = 4.0 * gap / (gap * gap + freq * freq)

        def add(p, number):
            here = (row == cond_slot[p]) & (lane == val_slot[p] * stride + n_freq)
            return number + jnp.where(here, 1.0, 0.0)

        number = lax.fori_loop(0, val_slot.shape[0], add, jnp.zeros((cond_count, LANES), jnp.float32))
        used = lane < val_count * stride
        extra[...] = jnp.where(used, jnp.where(is_count, number, weight), 0.0).astype(jnp.bfloat16)

    for t in range(nx):
        out[t, :, :part] = conds[t][...]
        val = vals[t][...].astype(jnp.float32)
        pieces = [val[:, k * seg : (k + 1) * seg] for k in range(part // seg)]
        out[t, :, part : part + seg] = jnp.concatenate(pieces, axis=0).astype(jnp.bfloat16)
        out[t, :, part + seg :] = extra[...]


def pack(val_orbitals, cond_orbitals, val_energy, cond_energy, val_slot, cond_slot, frequencies, nx, group):
    val_count, n_grid = val_orbitals.shape
    cond_count = cond_orbitals.shape[0]
    n_freq = frequencies.shape[0]
    n_parts = group * nx
    part = n_grid // n_parts
    segs = cond_count // val_count
    seg = part // segs
    width = part + seg + LANES
    if seg % LANES == 0:
        smem = pl.BlockSpec(memory_space=pltpu.SMEM)
        piece = lambda rows: [
            pl.BlockSpec((rows, part), functools.partial(lambda t, i: (0, t * group + i), t))
            for t in range(nx)
        ]
        return pl.pallas_call(
            functools.partial(pack_kernel, nx, part, seg),
            out_shape=jax.ShapeDtypeStruct((n_parts, cond_count, width), jnp.bfloat16),
            grid=(group,),
            in_specs=[smem] * 5 + piece(cond_count) + piece(val_count),
            out_specs=pl.BlockSpec((nx, cond_count, width), lambda i: (i, 0, 0)),
            scratch_shapes=[pltpu.VMEM((cond_count, LANES), jnp.bfloat16)],
            name="pack",
        )(
            val_energy,
            cond_energy,
            val_slot,
            cond_slot,
            frequencies,
            *([cond_orbitals] * nx),
            *([val_orbitals] * nx),
        )
    gap = cond_energy[:, None] - val_energy[None, :]
    weights = (
        4.0 * gap[:, :, None] / (gap[:, :, None] ** 2 + frequencies[None, None, :] ** 2)
    ).astype(jnp.bfloat16)
    chosen = (cond_slot[:, None, None] == jnp.arange(cond_count, dtype=jnp.int32)[None, :, None]) & (
        val_slot[:, None, None] == jnp.arange(val_count, dtype=jnp.int32)[None, None, :]
    )
    counts = jnp.sum(chosen.astype(jnp.float32), axis=0).astype(jnp.bfloat16)
    extra = jnp.concatenate([weights, counts[:, :, None]], axis=2).reshape(
        cond_count, val_count * (n_freq + 1)
    )
    extra = jnp.pad(extra, ((0, 0), (0, LANES - extra.shape[1])))
    cond_parts = cond_orbitals.reshape(cond_count, nx, group, part).transpose(2, 1, 0, 3)
    val_parts = val_orbitals.reshape(val_count, nx, group, segs, seg).transpose(2, 1, 3, 0, 4)
    return jnp.concatenate(
        [
            cond_parts.reshape(n_parts, cond_count, part),
            val_parts.reshape(n_parts, cond_count, seg),
            jnp.broadcast_to(extra, (n_parts,) + extra.shape),
        ],
        axis=2,
    )


def project_kernel(segs, val_count, cond_count, place, *refs):
    conds = refs[:segs]
    val = refs[segs]
    eigs = refs[segs + 1 : 5 * segs + 1]
    keep, send, density, total = refs[5 * segs + 1 :]
    rows = val.shape[0]
    blocks = rows // cond_count
    columns = keep.shape[-1]
    half = keep.shape[-2]
    turn = place[0] * 2

    for k in range(segs):

        @pl.loop(0, blocks)
        def _(j):
            at = pl.ds(pl.multiple_of(j * cond_count, cond_count), cond_count)
            c = conds[k][at, :].astype(jnp.float32)
            vals = val[at, :].astype(jnp.float32)
            for v in range(val_count):
                row = k * val_count + v
                product = (c * vals[row : row + 1, :]).astype(jnp.bfloat16)
                start = lax.bitwise_xor(v, turn) * rows + j * cond_count
                density[pl.ds(pl.multiple_of(start, cond_count), cond_count), :] = product

        eig = jnp.concatenate([eigs[4 * k + q][...] for q in range(4)], axis=1)
        sums = jnp.dot(density[...], eig, preferred_element_type=jnp.float32)
        if k == 0:

            @pl.when(pl.program_id(0) == 0)
            def _():
                total[...] = sums

            @pl.when(pl.program_id(0) > 0)
            def _():
                total[...] += sums
        else:
            total[...] += sums

    @pl.when(pl.program_id(0) == pl.num_programs(0) - 1)
    def _():
        for q in range(4):
            out = send if q % 2 else keep
            for h in range(2):
                out[q // 2, h] = total[h * half : (h + 1) * half, q * columns : (q + 1) * columns]


def project(unit, eigs, place, val_count, cond_count):
    part, columns = eigs[0].shape
    segs = cond_count // val_count
    seg = part // segs
    rows = unit.shape[0]
    half = rows * val_count // 2
    width = math.gcd(seg, 384)
    steps = seg // width
    in_specs = (
        [
            pl.BlockSpec((rows, width), functools.partial(lambda k, i, place: (0, k * steps + i), k))
            for k in range(segs)
        ]
        + [pl.BlockSpec((rows, width), lambda i, place: (0, segs * steps + i))]
        + [
            pl.BlockSpec((width, columns), functools.partial(lambda k, i, place: (k * steps + i, 0), k))
            for k in range(segs)
            for q in range(4)
        ]
    )
    shape = (2, 2, half, columns)
    out = jax.ShapeDtypeStruct(shape, jnp.float32)
    out_spec = pl.BlockSpec(shape, lambda i, place: (0, 0, 0, 0))
    return pl.pallas_call(
        functools.partial(project_kernel, segs, val_count, cond_count),
        out_shape=[out, out],
        grid_spec=pltpu.PrefetchScalarGridSpec(
            num_scalar_prefetch=1,
            grid=(steps,),
            in_specs=in_specs,
            out_specs=[out_spec, out_spec],
            scratch_shapes=[
                pltpu.VMEM((2 * half, width), jnp.bfloat16),
                pltpu.VMEM((2 * half, 4 * columns), jnp.float32),
            ],
        ),
        compiler_params=pltpu.CompilerParams(vmem_limit_bytes=32 * 1024 * 1024),
        cost_estimate=pl.CostEstimate(
            flops=16 * half * part * columns,
            bytes_accessed=2 * (unit.size + 4 * part * columns),
            transcendentals=0,
        ),
        name="project",
    )(place, *([unit] * (segs + 1)), *(list(eigs) * segs))


def weigh(owns, mates, scales, mine, n_freq, out):
    slots = len(owns)
    rows, columns = owns[0].shape
    stride = n_freq + 1
    width = scales[0].shape[0]
    for k in range(slots):
        scale = scales[k][...].astype(jnp.float32).T
        own = owns[k][...].astype(jnp.float32).T
        mate = mates[k][...].astype(jnp.float32).T
        for h in range(2):
            coeffs = jnp.where(mine == h, own, mate)
            for at in range(0, rows, width):
                v = (h * rows + at) // width
                number = scale[v * stride + n_freq : v * stride + n_freq + 1, :]
                for f in range(n_freq):
                    one = scale[v * stride + f : v * stride + f + 1, :] * number
                    out[k, f * columns : (f + 1) * columns, h * rows + at : h * rows + at + width] = (
                        coeffs[:, at : at + width] * one
                    ).astype(jnp.bfloat16)


def chi_kernel(early, late, n_freq, factor, scalars, *refs):
    slots = early + late
    owns = refs[:slots]
    mates = refs[slots : 2 * slots]
    scales = refs[2 * slots : 3 * slots]
    rights_a = refs[3 * slots : 3 * slots + 4]
    rights_b = refs[3 * slots + 4 : -2]
    out, weighted = refs[-2:]
    columns = out.shape[0]

    @pl.when(pl.program_id(0) == 0)
    def _():
        weigh(owns, mates, scales, scalars[4], n_freq, weighted)

    core = scalars[2]
    same_y = scalars[1] == lax.rem(pl.program_id(0), 2)
    shift = lax.bitwise_xor(scalars[0], scalars[3] + pl.program_id(0) // 2)
    left, right = [], []
    for r in range(slots):
        left.append(weighted[lax.bitwise_xor(shift, r)])
        for h in range(2):
            if r < early:
                pair = [rights_a[2 * h + c][0, r] for c in range(2)]
            else:
                own, other, mate, both = [rights_b[8 * (r - early) + 4 * h + q][0] for q in range(4)]
                own = jnp.where(same_y, own, other)
                mate = jnp.where(same_y, mate, both)
                pair = [jnp.where(core == c, own, mate) for c in range(2)]
            right.append(jnp.concatenate(pair, axis=1))
    chi = jnp.dot(
        jnp.concatenate(left, axis=1),
        jnp.concatenate(right, axis=0),
        preferred_element_type=jnp.float32,
    )
    for f in range(n_freq):
        out[:, f, :] = chi[f * columns : (f + 1) * columns, :] * factor


def make_chi(owns, mates, units, right_a, rights_b, scalars, n_freq, factor):
    members, early, rows, columns = right_a.shape
    tiles = members // 4
    late = len(rights_b)
    slots = early + late
    width = units[0].shape[0]
    last = units[0].shape[1] // LANES - 1
    flops = 4 * slots * rows * n_freq * columns * tiles * 2 * columns

    def near(h, i, scalars):
        return (lax.bitwise_xor(scalars[0], h * 2 + i // 2), 0, 0)

    return pl.pallas_call(
        functools.partial(chi_kernel, early, late, n_freq, factor),
        out_shape=jax.ShapeDtypeStruct((columns, n_freq, tiles * 2 * columns), jnp.float32),
        grid_spec=pltpu.PrefetchScalarGridSpec(
            num_scalar_prefetch=1,
            grid=(tiles,),
            in_specs=[pl.BlockSpec((rows, columns), lambda i, scalars: (0, 0))] * (2 * slots)
            + [pl.BlockSpec((width, LANES), lambda i, scalars: (0, last))] * slots
            + [
                pl.BlockSpec(
                    (1, early, rows, columns),
                    functools.partial(
                        lambda h, c, i, scalars: (h * tiles * 2 + i * 2 + c, 0, 0, 0), h, c
                    ),
                )
                for h in range(2)
                for c in range(2)
            ]
            + [
                pl.BlockSpec((1, rows, columns), functools.partial(near, h))
                for r in range(late)
                for h in range(2)
                for q in range(4)
            ],
            out_specs=pl.BlockSpec((columns, n_freq, 2 * columns), lambda i, scalars: (0, 0, i)),
            scratch_shapes=[pltpu.VMEM((slots, n_freq * columns, 2 * rows), jnp.bfloat16)],
        ),
        compiler_params=pltpu.CompilerParams(vmem_limit_bytes=32 * 1024 * 1024),
        cost_estimate=pl.CostEstimate(
            flops=flops,
            bytes_accessed=2 * (early + late) * members * rows * columns
            + 4 * columns * n_freq * tiles * 2 * columns,
            transcendentals=0,
        ),
        name="chi",
    )(scalars, *owns, *mates, *units, *([right_a] * 4), *[a for four in rights_b for a in four * 2])


def fast(shape, unit, eigenvectors, part, val_count, cond_count, n_freq, factor):
    nz, ny, nc, nx = shape
    z, y, c, x = [lax.axis_index(name).astype(jnp.int32) for name in AXES]
    columns = eigenvectors.shape[1]
    places = [(i, j, k, t) for i in range(nz) for j in range(ny) for k in range(nc) for t in range(nx)]
    number = {place: at for at, place in enumerate(places)}

    def send(array, target):
        pairs = [(number[place], target(*place)) for place in places]
        return lax.ppermute(
            array, AXES, [(source, number[to]) for source, to in pairs if to is not None]
        )

    def along_z(array, moves):
        moves = dict(moves)
        return send(array, lambda i, j, k, t: (moves[i], j, k, t) if i in moves else None)

    here = y * nc + c
    eigs = []
    for k in range(ny * nc):
        at = lax.bitwise_xor(here, k) * part
        rows = lax.dynamic_slice_in_dim(eigenvectors, at, part, 0)
        eigs.append(
            send(rows, functools.partial(lambda q, i, j, k, t: (i, j ^ (q // 2), k ^ (q % 2), t), k))
            if k
            else rows
        )

    inner = (z == 1) | (z == 2)
    near = along_z(unit, [(0, 1), (1, 0), (2, 3), (3, 2)])
    middle = along_z(unit, [(1, 2), (2, 1)])
    across = along_z(near, [(1, 2), (2, 1)])
    outward = along_z(middle, [(1, 0), (2, 3)])
    far = along_z(across, [(1, 0), (2, 3)])
    units = [unit, near, jnp.where(inner, across, outward)]

    place = x[None]

    def coefficients(unit, ready=None):
        keep, away = project(unit, eigs, place, val_count, cond_count)
        sums = keep + send(away, lambda i, j, k, t: (i, j, 1 - k, t))
        if ready is not None:
            sums, _ = lax.optimization_barrier((sums, ready))
        total = sums[0, 0] + send(sums[0, 1], lambda i, j, k, t: (i, j, k, 1 - t))
        total = total + send(sums[1, 0], lambda i, j, k, t: (i, 1 - j, k, t))
        total = total + send(sums[1, 1], lambda i, j, k, t: (i, 1 - j, k, 1 - t))
        return total.astype(jnp.bfloat16)

    def mate(own):
        return send(own, lambda i, j, k, t: (i, j, k, 1 - t))

    def share(own, m):
        return send(own, lambda i, j, k, t: ((2 * t + i % 2) ^ m, j, k, i // 2))

    def spread(own):
        shares = [share(own, m) for m in range(nz)]
        shares, paired = lax.optimization_barrier((shares, mate(own)))
        held = jnp.stack(shares)
        other = send(held, lambda i, j, k, t: (i, 1 - j, k, t))
        across_core = lambda i, j, k, t: (i, j, 1 - k, t)
        return (held, other, send(held, across_core), send(other, across_core)), paired

    owns = [coefficients(units[0], (across, outward)), coefficients(units[1])]
    owns.append(coefficients(units[2], far))
    own_a = jnp.stack(owns)
    share_a = share(own_a, 0)
    right_a = lax.all_gather(share_a, ("z", "y", "c"), axis=0)
    units.append(jnp.where(inner, middle, far))
    mate_a = mate(own_a)
    own_b = coefficients(units[3], (share_a, mate_a))
    four, mate_b = spread(own_b)
    owns.append(own_b)
    mates = [mate_a[k] for k in range(3)] + [mate_b]
    rights_b = [four]
    scalars = jnp.stack([z, y, c, 2 * x, x])
    return make_chi(owns, mates, units, right_a, rights_b, scalars, n_freq, factor)


def plain(shape, unit, eigenvectors, part, val_count, cond_count, n_freq, factor):
    nz, ny, nc, nx = shape
    z = lax.axis_index("z").astype(jnp.int32)
    x = lax.axis_index("x").astype(jnp.int32)
    group = ny * nc
    n_parts = group * nx
    segs = cond_count // val_count
    seg = part // segs
    columns = eigenvectors.shape[1]
    zfold = nz // nx
    eigs = lax.all_to_all(
        eigenvectors.reshape(group, part, columns), ("y", "c"), 0, 0, tiled=True
    )
    every = lax.all_gather(unit, "z", axis=0)

    def coefficients(unit):
        cond = unit[:, :part].reshape(1, n_parts, cond_count, segs, seg)
        val = unit[:, part : part + seg].reshape(n_parts, segs, val_count, seg)
        val = val.transpose(2, 0, 1, 3)[:, :, None]
        density = (cond.astype(jnp.float32) * val.astype(jnp.float32)).astype(jnp.bfloat16)
        sums = jnp.einsum(
            "pg,qgs->qps", density.reshape(-1, part), eigs, preferred_element_type=jnp.float32
        )
        sums = sums.reshape(n_parts, -1, columns)
        sums = lax.all_to_all(sums, ("y", "c", "x"), 0, 0, tiled=True)
        return jnp.sum(sums, axis=0).astype(jnp.bfloat16)

    own = jnp.stack([coefficients(every[k]) for k in range(nz)])
    lefts = lax.all_gather(own, "x", axis=0)
    perm = []
    for s in range(nz):
        for q in range(group):
            for t in range(nx):
                target = ((s % zfold + zfold * t) * group + q) * nx + s // zfold
                perm.append(((s * group + q) * nx + t, target))
    share = lax.ppermute(own, AXES, perm)
    right = lax.all_gather(share, ("z", "y", "c"), axis=0)
    rows = own.shape[1]
    total = 0.0
    for k in range(nz):
        scale = every[k][:, part + seg : part + seg + val_count * (n_freq + 1)].astype(jnp.float32)
        scale = scale.reshape(n_parts * cond_count, val_count, n_freq + 1).transpose(1, 0, 2)
        scale = scale.reshape(nx, rows, n_freq + 1)
        scale = scale[..., :n_freq] * scale[..., n_freq:]
        weighted = (lefts[:, k, :, :, None].astype(jnp.float32) * scale[:, :, None, :]).astype(
            jnp.bfloat16
        )
        weighted = weighted.reshape(nx * rows, columns * n_freq)
        piece = right[:, k].reshape(nx, zfold * group, rows, columns)
        piece = piece.transpose(0, 2, 1, 3).reshape(nx * rows, zfold * group * columns)
        total = total + lax.dot_general(
            weighted, piece, (((0,), (0,)), ((), ())), preferred_element_type=jnp.float32
        )
    return (total * factor).reshape(columns, n_freq, zfold * group * columns)


def local(
    shape,
    val_orbitals,
    cond_orbitals,
    val_energy,
    cond_energy,
    val_slot,
    cond_slot,
    eigenvectors,
    frequencies,
):
    nz, ny, nc, nx = shape
    val_count, n_grid = val_orbitals.shape
    cond_count = cond_orbitals.shape[0]
    n_parts = ny * nc * nx
    part = n_grid // n_parts
    seg = part * val_count // cond_count
    columns = eigenvectors.shape[1]
    factor = -1.0 / math.sqrt(val_slot.shape[0] * nz * n_parts)
    packed = pack(
        val_orbitals,
        cond_orbitals,
        val_energy,
        cond_energy,
        val_slot,
        cond_slot,
        frequencies,
        nx,
        ny * nc,
    )
    unit = lax.all_to_all(packed, ("y", "c", "x"), 0, 0, tiled=True)
    unit = unit.reshape(n_parts * cond_count, part + seg + LANES)
    on_tiles = columns % LANES == 0 and seg % LANES == 0
    run = fast if on_tiles and nx == 2 and nz == 4 and val_count == 4 else plain
    return run(
        shape, unit, eigenvectors, part, val_count, cond_count, frequencies.shape[0], factor
    )


def solution(mesh):
    n_pair = mesh.shape["pair"]
    n_proj = mesh.shape["proj"]
    shape = (n_pair // 4, 2, 2, n_proj)
    grid = Mesh(mesh.devices.reshape(shape), AXES)
    return jax.shard_map(
        functools.partial(local, shape),
        mesh=grid,
        in_specs=(
            P(AXES, None),
            P(AXES, None),
            P(AXES),
            P(AXES),
            P(AXES),
            P(AXES),
            P("x", ("z", "y", "c")),
            P(),
        ),
        out_specs=P(("z", "y", "c"), None, "x"),
        check_vma=False,
    )
```

```python
import functools
import math

import jax
import jax.numpy as jnp
from jax import lax
from jax.experimental import pallas as pl
from jax.experimental.pallas import tpu as pltpu
from jax.sharding import Mesh
from jax.sharding import PartitionSpec as P

LANES = 128
AXES = ("z", "y", "c", "x")


def pack_kernel(nx, part, seg, val_energy, cond_energy, val_slot, cond_slot, frequencies, *refs):
    conds = refs[:nx]
    vals = refs[nx : 2 * nx]
    out, extra = refs[2 * nx :]
    val_count = val_energy.shape[0]
    cond_count = cond_energy.shape[0]
    n_freq = frequencies.shape[0]
    stride = n_freq + 1

    @pl.when(pl.program_id(0) == 0)
    def _():
        row = lax.broadcasted_iota(jnp.int32, (cond_count, LANES), 0)
        lane = lax.broadcasted_iota(jnp.int32, (cond_count, LANES), 1)
        cond_level = jnp.zeros((cond_count, LANES), jnp.float32)
        for c in range(cond_count):
            cond_level = jnp.where(row == c, cond_energy[c], cond_level)
        val_level = jnp.zeros((cond_count, LANES), jnp.float32)
        freq = jnp.zeros((cond_count, LANES), jnp.float32)
        is_count = lane < 0
        for v in range(val_count):
            for f in range(stride):
                here = lane == v * stride + f
                val_level = jnp.where(here, val_energy[v], val_level)
                if f < n_freq:
                    freq = jnp.where(here, frequencies[f], freq)
                else:
                    is_count = is_count | here
        gap = cond_level - val_level
        weight = 4.0 * gap / (gap * gap + freq * freq)

        def add(p, number):
            here = (row == cond_slot[p]) & (lane == val_slot[p] * stride + n_freq)
            return number + jnp.where(here, 1.0, 0.0)

        number = lax.fori_loop(0, val_slot.shape[0], add, jnp.zeros((cond_count, LANES), jnp.float32))
        used = lane < val_count * stride
        extra[...] = jnp.where(used, jnp.where(is_count, number, weight), 0.0).astype(jnp.bfloat16)

    for t in range(nx):
        out[t, :, :part] = conds[t][...]
        val = vals[t][...].astype(jnp.float32)
        pieces = [val[:, k * seg : (k + 1) * seg] for k in range(part // seg)]
        out[t, :, part : part + seg] = jnp.concatenate(pieces, axis=0).astype(jnp.bfloat16)
        out[t, :, part + seg :] = extra[...]


def pack(val_orbitals, cond_orbitals, val_energy, cond_energy, val_slot, cond_slot, frequencies, nx, group):
    val_count, n_grid = val_orbitals.shape
    cond_count = cond_orbitals.shape[0]
    n_freq = frequencies.shape[0]
    n_parts = group * nx
    part = n_grid // n_parts
    segs = cond_count // val_count
    seg = part // segs
    width = part + seg + LANES
    if seg % LANES == 0:
        smem = pl.BlockSpec(memory_space=pltpu.SMEM)
        piece = lambda rows: [
            pl.BlockSpec((rows, part), functools.partial(lambda t, i: (0, t * group + i), t))
            for t in range(nx)
        ]
        return pl.pallas_call(
            functools.partial(pack_kernel, nx, part, seg),
            out_shape=jax.ShapeDtypeStruct((n_parts, cond_count, width), jnp.bfloat16),
            grid=(group,),
            in_specs=[smem] * 5 + piece(cond_count) + piece(val_count),
            out_specs=pl.BlockSpec((nx, cond_count, width), lambda i: (i, 0, 0)),
            scratch_shapes=[pltpu.VMEM((cond_count, LANES), jnp.bfloat16)],
            name="pack",
        )(
            val_energy,
            cond_energy,
            val_slot,
            cond_slot,
            frequencies,
            *([cond_orbitals] * nx),
            *([val_orbitals] * nx),
        )
    gap = cond_energy[:, None] - val_energy[None, :]
    weights = (
        4.0 * gap[:, :, None] / (gap[:, :, None] ** 2 + frequencies[None, None, :] ** 2)
    ).astype(jnp.bfloat16)
    chosen = (cond_slot[:, None, None] == jnp.arange(cond_count, dtype=jnp.int32)[None, :, None]) & (
        val_slot[:, None, None] == jnp.arange(val_count, dtype=jnp.int32)[None, None, :]
    )
    counts = jnp.sum(chosen.astype(jnp.float32), axis=0).astype(jnp.bfloat16)
    extra = jnp.concatenate([weights, counts[:, :, None]], axis=2).reshape(
        cond_count, val_count * (n_freq + 1)
    )
    extra = jnp.pad(extra, ((0, 0), (0, LANES - extra.shape[1])))
    cond_parts = cond_orbitals.reshape(cond_count, nx, group, part).transpose(2, 1, 0, 3)
    val_parts = val_orbitals.reshape(val_count, nx, group, segs, seg).transpose(2, 1, 3, 0, 4)
    return jnp.concatenate(
        [
            cond_parts.reshape(n_parts, cond_count, part),
            val_parts.reshape(n_parts, cond_count, seg),
            jnp.broadcast_to(extra, (n_parts,) + extra.shape),
        ],
        axis=2,
    )


def project_kernel(segs, val_count, cond_count, place, *refs):
    conds = refs[:segs]
    val = refs[segs]
    eigs = refs[segs + 1 : 5 * segs + 1]
    keep, send, density, total = refs[5 * segs + 1 :]
    rows = val.shape[0]
    blocks = rows // cond_count
    columns = keep.shape[-1]
    half = keep.shape[-2]
    turn = place[0] * 2

    for k in range(segs):

        @pl.loop(0, blocks)
        def _(j):
            at = pl.ds(pl.multiple_of(j * cond_count, cond_count), cond_count)
            c = conds[k][at, :].astype(jnp.float32)
            vals = val[at, :].astype(jnp.float32)
            for v in range(val_count):
                row = k * val_count + v
                product = (c * vals[row : row + 1, :]).astype(jnp.bfloat16)
                start = lax.bitwise_xor(v, turn) * rows + j * cond_count
                density[pl.ds(pl.multiple_of(start, cond_count), cond_count), :] = product

        eig = jnp.concatenate([eigs[4 * k + q][...] for q in range(4)], axis=1)
        sums = jnp.dot(density[...], eig, preferred_element_type=jnp.float32)
        if k == 0:

            @pl.when(pl.program_id(0) == 0)
            def _():
                total[...] = sums

            @pl.when(pl.program_id(0) > 0)
            def _():
                total[...] += sums
        else:
            total[...] += sums

    @pl.when(pl.program_id(0) == pl.num_programs(0) - 1)
    def _():
        for q in range(4):
            out = send if q % 2 else keep
            for h in range(2):
                out[q // 2, h] = total[h * half : (h + 1) * half, q * columns : (q + 1) * columns]


def project(unit, eigs, place, val_count, cond_count):
    part, columns = eigs[0].shape
    segs = cond_count // val_count
    seg = part // segs
    rows = unit.shape[0]
    half = rows * val_count // 2
    width = math.gcd(seg, 384)
    steps = seg // width
    in_specs = (
        [
            pl.BlockSpec((rows, width), functools.partial(lambda k, i, place: (0, k * steps + i), k))
            for k in range(segs)
        ]
        + [pl.BlockSpec((rows, width), lambda i, place: (0, segs * steps + i))]
        + [
            pl.BlockSpec((width, columns), functools.partial(lambda k, i, place: (k * steps + i, 0), k))
            for k in range(segs)
            for q in range(4)
        ]
    )
    shape = (2, 2, half, columns)
    out = jax.ShapeDtypeStruct(shape, jnp.float32)
    out_spec = pl.BlockSpec(shape, lambda i, place: (0, 0, 0, 0))
    return pl.pallas_call(
        functools.partial(project_kernel, segs, val_count, cond_count),
        out_shape=[out, out],
        grid_spec=pltpu.PrefetchScalarGridSpec(
            num_scalar_prefetch=1,
            grid=(steps,),
            in_specs=in_specs,
            out_specs=[out_spec, out_spec],
            scratch_shapes=[
                pltpu.VMEM((2 * half, width), jnp.bfloat16),
                pltpu.VMEM((2 * half, 4 * columns), jnp.float32),
            ],
        ),
        compiler_params=pltpu.CompilerParams(vmem_limit_bytes=32 * 1024 * 1024),
        cost_estimate=pl.CostEstimate(
            flops=16 * half * part * columns,
            bytes_accessed=2 * (unit.size + 4 * part * columns),
            transcendentals=0,
        ),
        name="project",
    )(place, *([unit] * (segs + 1)), *(list(eigs) * segs))


def weigh(owns, mates, scales, mine, n_freq, out):
    slots = len(owns)
    rows, columns = owns[0].shape
    stride = n_freq + 1
    width = scales[0].shape[0]
    for k in range(slots):
        scale = scales[k][...].astype(jnp.float32).T
        own = owns[k][...].astype(jnp.float32).T
        mate = mates[k][...].astype(jnp.float32).T
        for h in range(2):
            coeffs = jnp.where(mine == h, own, mate)
            for at in range(0, rows, width):
                v = (h * rows + at) // width
                number = scale[v * stride + n_freq : v * stride + n_freq + 1, :]
                for f in range(n_freq):
                    one = scale[v * stride + f : v * stride + f + 1, :] * number
                    out[k, f * columns : (f + 1) * columns, h * rows + at : h * rows + at + width] = (
                        coeffs[:, at : at + width] * one
                    ).astype(jnp.bfloat16)


def chi_kernel(early, late, n_freq, factor, scalars, *refs):
    slots = early + late
    owns = refs[:slots]
    mates = refs[slots : 2 * slots]
    scales = refs[2 * slots : 3 * slots]
    rights_a = refs[3 * slots : 3 * slots + 4]
    rights_b = refs[3 * slots + 4 : -2]
    out, weighted = refs[-2:]
    columns = out.shape[0]

    @pl.when(pl.program_id(0) == 0)
    def _():
        weigh(owns, mates, scales, scalars[4], n_freq, weighted)

    core = scalars[2]
    same_y = scalars[1] == lax.rem(pl.program_id(0), 2)
    shift = lax.bitwise_xor(scalars[0], scalars[3] + pl.program_id(0) // 2)
    left, right = [], []
    for r in range(slots):
        left.append(weighted[lax.bitwise_xor(shift, r)])
        for h in range(2):
            if r < early:
                pair = [rights_a[2 * h + c][0, r] for c in range(2)]
            else:
                own, other, mate, both = [rights_b[8 * (r - early) + 4 * h + q][0] for q in range(4)]
                own = jnp.where(same_y, own, other)
                mate = jnp.where(same_y, mate, both)
                pair = [jnp.where(core == c, own, mate) for c in range(2)]
            right.append(jnp.concatenate(pair, axis=1))
    chi = jnp.dot(
        jnp.concatenate(left, axis=1),
        jnp.concatenate(right, axis=0),
        preferred_element_type=jnp.float32,
    )
    for f in range(n_freq):
        out[:, f, :] = chi[f * columns : (f + 1) * columns, :] * factor


def make_chi(owns, mates, units, right_a, rights_b, scalars, n_freq, factor):
    members, early, rows, columns = right_a.shape
    tiles = members // 4
    late = len(rights_b)
    slots = early + late
    width = units[0].shape[0]
    last = units[0].shape[1] // LANES - 1
    flops = 4 * slots * rows * n_freq * columns * tiles * 2 * columns

    def near(h, i, scalars):
        return (lax.bitwise_xor(scalars[0], h * 2 + i // 2), 0, 0)

    return pl.pallas_call(
        functools.partial(chi_kernel, early, late, n_freq, factor),
        out_shape=jax.ShapeDtypeStruct((columns, n_freq, tiles * 2 * columns), jnp.float32),
        grid_spec=pltpu.PrefetchScalarGridSpec(
            num_scalar_prefetch=1,
            grid=(tiles,),
            in_specs=[pl.BlockSpec((rows, columns), lambda i, scalars: (0, 0))] * (2 * slots)
            + [pl.BlockSpec((width, LANES), lambda i, scalars: (0, last))] * slots
            + [
                pl.BlockSpec(
                    (1, early, rows, columns),
                    functools.partial(
                        lambda h, c, i, scalars: (h * tiles * 2 + i * 2 + c, 0, 0, 0), h, c
                    ),
                )
                for h in range(2)
                for c in range(2)
            ]
            + [
                pl.BlockSpec((1, rows, columns), functools.partial(near, h))
                for r in range(late)
                for h in range(2)
                for q in range(4)
            ],
            out_specs=pl.BlockSpec((columns, n_freq, 2 * columns), lambda i, scalars: (0, 0, i)),
            scratch_shapes=[pltpu.VMEM((slots, n_freq * columns, 2 * rows), jnp.bfloat16)],
        ),
        compiler_params=pltpu.CompilerParams(vmem_limit_bytes=32 * 1024 * 1024),
        cost_estimate=pl.CostEstimate(
            flops=flops,
            bytes_accessed=2 * (early + late) * members * rows * columns
            + 4 * columns * n_freq * tiles * 2 * columns,
            transcendentals=0,
        ),
        name="chi",
    )(scalars, *owns, *mates, *units, *([right_a] * 4), *[a for four in rights_b for a in four * 2])


def fast(shape, unit, eigenvectors, part, val_count, cond_count, n_freq, factor):
    nz, ny, nc, nx = shape
    z, y, c, x = [lax.axis_index(name).astype(jnp.int32) for name in AXES]
    columns = eigenvectors.shape[1]
    places = [(i, j, k, t) for i in range(nz) for j in range(ny) for k in range(nc) for t in range(nx)]
    number = {place: at for at, place in enumerate(places)}

    def send(array, target):
        pairs = [(number[place], target(*place)) for place in places]
        return lax.ppermute(
            array, AXES, [(source, number[to]) for source, to in pairs if to is not None]
        )

    def along_z(array, moves):
        moves = dict(moves)
        return send(array, lambda i, j, k, t: (moves[i], j, k, t) if i in moves else None)

    here = y * nc + c
    eigs = [
        lax.dynamic_slice_in_dim(eigenvectors, lax.bitwise_xor(here, k) * part, part, 0)
        for k in range(ny * nc)
    ]
    unit, eigs = lax.optimization_barrier((unit, eigs))
    for q in range(1, ny * nc):
        eigs[q] = send(
            eigs[q], functools.partial(lambda q, i, j, k, t: (i, j ^ (q // 2), k ^ (q % 2), t), q)
        )

    inner = (z == 1) | (z == 2)
    near = along_z(unit, [(0, 1), (1, 0), (2, 3), (3, 2)])
    middle = along_z(unit, [(1, 2), (2, 1)])
    across = along_z(near, [(1, 2), (2, 1)])
    outward = along_z(middle, [(1, 0), (2, 3)])
    far = along_z(across, [(1, 0), (2, 3)])
    units = [unit, near, jnp.where(inner, across, outward)]

    place = x[None]

    def coefficients(unit, ready=None, settled=None):
        keep, away = project(unit, eigs, place, val_count, cond_count)
        sums = keep + send(away, lambda i, j, k, t: (i, j, 1 - k, t))
        if ready is not None:
            sums, _ = lax.optimization_barrier((sums, ready))
        total = sums[0, 0] + send(sums[0, 1], lambda i, j, k, t: (i, j, k, 1 - t))
        total = total + send(sums[1, 0], lambda i, j, k, t: (i, 1 - j, k, t))
        total = total + send(sums[1, 1], lambda i, j, k, t: (i, 1 - j, k, 1 - t))
        if settled is not None:
            total, _ = lax.optimization_barrier((total, settled))
        return total.astype(jnp.bfloat16)

    def mate(own):
        return send(own, lambda i, j, k, t: (i, j, k, 1 - t))

    def share(own, m):
        return send(own, lambda i, j, k, t: ((2 * t + i % 2) ^ m, j, k, i // 2))

    owns = [coefficients(units[0], (across, outward)), coefficients(units[1])]
    mate_a = mate(jnp.stack(owns))
    owns.append(coefficients(units[2], None, (far, mate_a)))
    right_a = lax.all_gather(share(jnp.stack(owns), 0), ("z", "y", "c"), axis=0)
    units.append(jnp.where(inner, middle, far))
    own_b = coefficients(units[3])
    shares = [share(own_b, m) for m in range(nz)]
    mate_b = mate(jnp.stack([owns[2], own_b]))
    shares, mate_b = lax.optimization_barrier((shares, mate_b))
    held = jnp.stack(shares)
    other = send(held, lambda i, j, k, t: (i, 1 - j, k, t))
    across_core = lambda i, j, k, t: (i, j, 1 - k, t)
    rights_b = [(held, other, send(held, across_core), send(other, across_core))]
    owns.append(own_b)
    mates = [mate_a[0], mate_a[1], mate_b[0], mate_b[1]]
    scalars = jnp.stack([z, y, c, 2 * x, x])
    return make_chi(owns, mates, units, right_a, rights_b, scalars, n_freq, factor)


def plain(shape, unit, eigenvectors, part, val_count, cond_count, n_freq, factor):
    nz, ny, nc, nx = shape
    z = lax.axis_index("z").astype(jnp.int32)
    x = lax.axis_index("x").astype(jnp.int32)
    group = ny * nc
    n_parts = group * nx
    segs = cond_count // val_count
    seg = part // segs
    columns = eigenvectors.shape[1]
    zfold = nz // nx
    eigs = lax.all_to_all(
        eigenvectors.reshape(group, part, columns), ("y", "c"), 0, 0, tiled=True
    )
    every = lax.all_gather(unit, "z", axis=0)

    def coefficients(unit):
        cond = unit[:, :part].reshape(1, n_parts, cond_count, segs, seg)
        val = unit[:, part : part + seg].reshape(n_parts, segs, val_count, seg)
        val = val.transpose(2, 0, 1, 3)[:, :, None]
        density = (cond.astype(jnp.float32) * val.astype(jnp.float32)).astype(jnp.bfloat16)
        sums = jnp.einsum(
            "pg,qgs->qps", density.reshape(-1, part), eigs, preferred_element_type=jnp.float32
        )
        sums = sums.reshape(n_parts, -1, columns)
        sums = lax.all_to_all(sums, ("y", "c", "x"), 0, 0, tiled=True)
        return jnp.sum(sums, axis=0).astype(jnp.bfloat16)

    own = jnp.stack([coefficients(every[k]) for k in range(nz)])
    lefts = lax.all_gather(own, "x", axis=0)
    perm = []
    for s in range(nz):
        for q in range(group):
            for t in range(nx):
                target = ((s % zfold + zfold * t) * group + q) * nx + s // zfold
                perm.append(((s * group + q) * nx + t, target))
    share = lax.ppermute(own, AXES, perm)
    right = lax.all_gather(share, ("z", "y", "c"), axis=0)
    rows = own.shape[1]
    total = 0.0
    for k in range(nz):
        scale = every[k][:, part + seg : part + seg + val_count * (n_freq + 1)].astype(jnp.float32)
        scale = scale.reshape(n_parts * cond_count, val_count, n_freq + 1).transpose(1, 0, 2)
        scale = scale.reshape(nx, rows, n_freq + 1)
        scale = scale[..., :n_freq] * scale[..., n_freq:]
        weighted = (lefts[:, k, :, :, None].astype(jnp.float32) * scale[:, :, None, :]).astype(
            jnp.bfloat16
        )
        weighted = weighted.reshape(nx * rows, columns * n_freq)
        piece = right[:, k].reshape(nx, zfold * group, rows, columns)
        piece = piece.transpose(0, 2, 1, 3).reshape(nx * rows, zfold * group * columns)
        total = total + lax.dot_general(
            weighted, piece, (((0,), (0,)), ((), ())), preferred_element_type=jnp.float32
        )
    return (total * factor).reshape(columns, n_freq, zfold * group * columns)


def local(
    shape,
    val_orbitals,
    cond_orbitals,
    val_energy,
    cond_energy,
    val_slot,
    cond_slot,
    eigenvectors,
    frequencies,
):
    nz, ny, nc, nx = shape
    val_count, n_grid = val_orbitals.shape
    cond_count = cond_orbitals.shape[0]
    n_parts = ny * nc * nx
    part = n_grid // n_parts
    seg = part * val_count // cond_count
    columns = eigenvectors.shape[1]
    factor = -1.0 / math.sqrt(val_slot.shape[0] * nz * n_parts)
    packed = pack(
        val_orbitals,
        cond_orbitals,
        val_energy,
        cond_energy,
        val_slot,
        cond_slot,
        frequencies,
        nx,
        ny * nc,
    )
    unit = lax.all_to_all(packed, ("y", "c", "x"), 0, 0, tiled=True)
    unit = unit.reshape(n_parts * cond_count, part + seg + LANES)
    on_tiles = columns % LANES == 0 and seg % LANES == 0
    run = fast if on_tiles and nx == 2 and nz == 4 and val_count == 4 else plain
    return run(
        shape, unit, eigenvectors, part, val_count, cond_count, frequencies.shape[0], factor
    )


def solution(mesh):
    n_pair = mesh.shape["pair"]
    n_proj = mesh.shape["proj"]
    shape = (n_pair // 4, 2, 2, n_proj)
    grid = Mesh(mesh.devices.reshape(shape), AXES)
    return jax.shard_map(
        functools.partial(local, shape),
        mesh=grid,
        in_specs=(
            P(AXES, None),
            P(AXES, None),
            P(AXES),
            P(AXES),
            P(AXES),
            P(AXES),
            P("x", ("z", "y", "c")),
            P(),
        ),
        out_specs=P(("z", "y", "c"), None, "x"),
        check_vma=False,
    )
```

```python
import functools
import math

import jax
import jax.numpy as jnp
from jax import lax
from jax.experimental import pallas as pl
from jax.experimental.pallas import tpu as pltpu
from jax.sharding import Mesh
from jax.sharding import PartitionSpec as P

LANES = 128
AXES = ("z", "y", "c", "x")


def pack_kernel(nx, part, seg, val_energy, cond_energy, val_slot, cond_slot, frequencies, *refs):
    conds = refs[:nx]
    vals = refs[nx : 2 * nx]
    out, extra = refs[2 * nx :]
    val_count = val_energy.shape[0]
    cond_count = cond_energy.shape[0]
    n_freq = frequencies.shape[0]
    stride = n_freq + 1

    @pl.when(pl.program_id(0) == 0)
    def _():
        row = lax.broadcasted_iota(jnp.int32, (cond_count, LANES), 0)
        lane = lax.broadcasted_iota(jnp.int32, (cond_count, LANES), 1)
        cond_level = jnp.zeros((cond_count, LANES), jnp.float32)
        for c in range(cond_count):
            cond_level = jnp.where(row == c, cond_energy[c], cond_level)
        val_level = jnp.zeros((cond_count, LANES), jnp.float32)
        freq = jnp.zeros((cond_count, LANES), jnp.float32)
        is_count = lane < 0
        for v in range(val_count):
            for f in range(stride):
                here = lane == v * stride + f
                val_level = jnp.where(here, val_energy[v], val_level)
                if f < n_freq:
                    freq = jnp.where(here, frequencies[f], freq)
                else:
                    is_count = is_count | here
        gap = cond_level - val_level
        weight = 4.0 * gap / (gap * gap + freq * freq)

        def add(p, number):
            here = (row == cond_slot[p]) & (lane == val_slot[p] * stride + n_freq)
            return number + jnp.where(here, 1.0, 0.0)

        number = lax.fori_loop(0, val_slot.shape[0], add, jnp.zeros((cond_count, LANES), jnp.float32))
        used = lane < val_count * stride
        extra[...] = jnp.where(used, jnp.where(is_count, number, weight), 0.0).astype(jnp.bfloat16)

    for t in range(nx):
        out[t, :, :part] = conds[t][...]
        val = vals[t][...].astype(jnp.float32)
        pieces = [val[:, k * seg : (k + 1) * seg] for k in range(part // seg)]
        out[t, :, part : part + seg] = jnp.concatenate(pieces, axis=0).astype(jnp.bfloat16)
        out[t, :, part + seg :] = extra[...]


def pack(val_orbitals, cond_orbitals, val_energy, cond_energy, val_slot, cond_slot, frequencies, nx, group):
    val_count, n_grid = val_orbitals.shape
    cond_count = cond_orbitals.shape[0]
    n_freq = frequencies.shape[0]
    n_parts = group * nx
    part = n_grid // n_parts
    segs = cond_count // val_count
    seg = part // segs
    width = part + seg + LANES
    if seg % LANES == 0:
        smem = pl.BlockSpec(memory_space=pltpu.SMEM)
        piece = lambda rows: [
            pl.BlockSpec((rows, part), functools.partial(lambda t, i: (0, t * group + i), t))
            for t in range(nx)
        ]
        return pl.pallas_call(
            functools.partial(pack_kernel, nx, part, seg),
            out_shape=jax.ShapeDtypeStruct((n_parts, cond_count, width), jnp.bfloat16),
            grid=(group,),
            in_specs=[smem] * 5 + piece(cond_count) + piece(val_count),
            out_specs=pl.BlockSpec((nx, cond_count, width), lambda i: (i, 0, 0)),
            scratch_shapes=[pltpu.VMEM((cond_count, LANES), jnp.bfloat16)],
            name="pack",
        )(
            val_energy,
            cond_energy,
            val_slot,
            cond_slot,
            frequencies,
            *([cond_orbitals] * nx),
            *([val_orbitals] * nx),
        )
    gap = cond_energy[:, None] - val_energy[None, :]
    weights = (
        4.0 * gap[:, :, None] / (gap[:, :, None] ** 2 + frequencies[None, None, :] ** 2)
    ).astype(jnp.bfloat16)
    chosen = (cond_slot[:, None, None] == jnp.arange(cond_count, dtype=jnp.int32)[None, :, None]) & (
        val_slot[:, None, None] == jnp.arange(val_count, dtype=jnp.int32)[None, None, :]
    )
    counts = jnp.sum(chosen.astype(jnp.float32), axis=0).astype(jnp.bfloat16)
    extra = jnp.concatenate([weights, counts[:, :, None]], axis=2).reshape(
        cond_count, val_count * (n_freq + 1)
    )
    extra = jnp.pad(extra, ((0, 0), (0, LANES - extra.shape[1])))
    cond_parts = cond_orbitals.reshape(cond_count, nx, group, part).transpose(2, 1, 0, 3)
    val_parts = val_orbitals.reshape(val_count, nx, group, segs, seg).transpose(2, 1, 3, 0, 4)
    return jnp.concatenate(
        [
            cond_parts.reshape(n_parts, cond_count, part),
            val_parts.reshape(n_parts, cond_count, seg),
            jnp.broadcast_to(extra, (n_parts,) + extra.shape),
        ],
        axis=2,
    )


def project_kernel(segs, val_count, cond_count, place, *refs):
    conds = refs[:segs]
    val = refs[segs]
    eigs = refs[segs + 1 : 5 * segs + 1]
    keep, send, density, total = refs[5 * segs + 1 :]
    rows = val.shape[0]
    blocks = rows // cond_count
    columns = keep.shape[-1]
    half = keep.shape[-2]
    turn = place[0] * 2

    for k in range(segs):

        @pl.loop(0, blocks)
        def _(j):
            at = pl.ds(pl.multiple_of(j * cond_count, cond_count), cond_count)
            c = conds[k][at, :].astype(jnp.float32)
            vals = val[at, :].astype(jnp.float32)
            for v in range(val_count):
                row = k * val_count + v
                product = (c * vals[row : row + 1, :]).astype(jnp.bfloat16)
                start = lax.bitwise_xor(v, turn) * rows + j * cond_count
                density[pl.ds(pl.multiple_of(start, cond_count), cond_count), :] = product

        eig = jnp.concatenate([eigs[4 * k + q][...] for q in range(4)], axis=1)
        sums = jnp.dot(density[...], eig, preferred_element_type=jnp.float32)
        if k == 0:

            @pl.when(pl.program_id(0) == 0)
            def _():
                total[...] = sums

            @pl.when(pl.program_id(0) > 0)
            def _():
                total[...] += sums
        else:
            total[...] += sums

    @pl.when(pl.program_id(0) == pl.num_programs(0) - 1)
    def _():
        for q in range(4):
            out = send if q % 2 else keep
            for h in range(2):
                out[q // 2, h] = total[h * half : (h + 1) * half, q * columns : (q + 1) * columns]


def project(unit, eigs, place, val_count, cond_count):
    part, columns = eigs[0].shape
    segs = cond_count // val_count
    seg = part // segs
    rows = unit.shape[0]
    half = rows * val_count // 2
    width = math.gcd(seg, 384)
    steps = seg // width
    in_specs = (
        [
            pl.BlockSpec((rows, width), functools.partial(lambda k, i, place: (0, k * steps + i), k))
            for k in range(segs)
        ]
        + [pl.BlockSpec((rows, width), lambda i, place: (0, segs * steps + i))]
        + [
            pl.BlockSpec((width, columns), functools.partial(lambda k, i, place: (k * steps + i, 0), k))
            for k in range(segs)
            for q in range(4)
        ]
    )
    shape = (2, 2, half, columns)
    out = jax.ShapeDtypeStruct(shape, jnp.float32)
    out_spec = pl.BlockSpec(shape, lambda i, place: (0, 0, 0, 0))
    return pl.pallas_call(
        functools.partial(project_kernel, segs, val_count, cond_count),
        out_shape=[out, out],
        grid_spec=pltpu.PrefetchScalarGridSpec(
            num_scalar_prefetch=1,
            grid=(steps,),
            in_specs=in_specs,
            out_specs=[out_spec, out_spec],
            scratch_shapes=[
                pltpu.VMEM((2 * half, width), jnp.bfloat16),
                pltpu.VMEM((2 * half, 4 * columns), jnp.float32),
            ],
        ),
        compiler_params=pltpu.CompilerParams(vmem_limit_bytes=32 * 1024 * 1024),
        cost_estimate=pl.CostEstimate(
            flops=16 * half * part * columns,
            bytes_accessed=2 * (unit.size + 4 * part * columns),
            transcendentals=0,
        ),
        name="project",
    )(place, *([unit] * (segs + 1)), *(list(eigs) * segs))


def weigh(owns, mates, scales, mine, n_freq, out):
    slots = len(owns)
    rows, columns = owns[0].shape
    stride = n_freq + 1
    width = scales[0].shape[0]
    for k in range(slots):
        scale = scales[k][...].astype(jnp.float32).T
        own = owns[k][...].astype(jnp.float32).T
        mate = mates[k][...].astype(jnp.float32).T
        for h in range(2):
            coeffs = jnp.where(mine == h, own, mate)
            for at in range(0, rows, width):
                v = (h * rows + at) // width
                number = scale[v * stride + n_freq : v * stride + n_freq + 1, :]
                for f in range(n_freq):
                    one = scale[v * stride + f : v * stride + f + 1, :] * number
                    out[k, f * columns : (f + 1) * columns, h * rows + at : h * rows + at + width] = (
                        coeffs[:, at : at + width] * one
                    ).astype(jnp.bfloat16)


def chi_kernel(early, late, n_freq, factor, scalars, *refs):
    slots = early + late
    owns = refs[:slots]
    mates = refs[slots : 2 * slots]
    scales = refs[2 * slots : 3 * slots]
    rights_a = refs[3 * slots : 3 * slots + 4]
    rights_b = refs[3 * slots + 4 : 3 * slots + 12]
    out, weighted = refs[3 * slots + 12 :]
    columns = out.shape[0]

    @pl.when(pl.program_id(0) == 0)
    def _():
        weigh(owns, mates, scales, scalars[4], n_freq, weighted)

    core = scalars[2]
    same_y = scalars[1] == lax.rem(pl.program_id(0), 2)
    shift = lax.bitwise_xor(scalars[0], scalars[3] + pl.program_id(0) // 2)
    left, right = [], []
    for r in range(slots):
        left.append(weighted[lax.bitwise_xor(shift, r)])
        for h in range(2):
            if r < early:
                pair = [rights_a[2 * h + c][0, r] for c in range(2)]
            else:
                own, other, mate, both = [rights_b[4 * h + q][0, r - early] for q in range(4)]
                own = jnp.where(same_y, own, other)
                mate = jnp.where(same_y, mate, both)
                pair = [jnp.where(core == c, own, mate) for c in range(2)]
            right.append(jnp.concatenate(pair, axis=1))
    chi = jnp.dot(
        jnp.concatenate(left, axis=1),
        jnp.concatenate(right, axis=0),
        preferred_element_type=jnp.float32,
    )
    for f in range(n_freq):
        out[:, f, :] = chi[f * columns : (f + 1) * columns, :] * factor


def make_chi(owns, mates, units, right_a, rights_b, scalars, n_freq, factor):
    members, early, rows, columns = right_a.shape
    tiles = members // 4
    late = rights_b[0].shape[1]
    slots = early + late
    width = units[0].shape[0]
    last = units[0].shape[1] // LANES - 1
    flops = 4 * slots * rows * n_freq * columns * tiles * 2 * columns

    def near(h, i, scalars):
        return (lax.bitwise_xor(scalars[0], h * 2 + i // 2), 0, 0, 0)

    return pl.pallas_call(
        functools.partial(chi_kernel, early, late, n_freq, factor),
        out_shape=jax.ShapeDtypeStruct((columns, n_freq, tiles * 2 * columns), jnp.float32),
        grid_spec=pltpu.PrefetchScalarGridSpec(
            num_scalar_prefetch=1,
            grid=(tiles,),
            in_specs=[pl.BlockSpec((rows, columns), lambda i, scalars: (0, 0))] * (2 * slots)
            + [pl.BlockSpec((width, LANES), lambda i, scalars: (0, last))] * slots
            + [
                pl.BlockSpec(
                    (1, early, rows, columns),
                    functools.partial(
                        lambda h, c, i, scalars: (h * tiles * 2 + i * 2 + c, 0, 0, 0), h, c
                    ),
                )
                for h in range(2)
                for c in range(2)
            ]
            + [
                pl.BlockSpec((1, late, rows, columns), functools.partial(near, h))
                for h in range(2)
                for q in range(4)
            ],
            out_specs=pl.BlockSpec((columns, n_freq, 2 * columns), lambda i, scalars: (0, 0, i)),
            scratch_shapes=[pltpu.VMEM((slots, n_freq * columns, 2 * rows), jnp.bfloat16)],
        ),
        compiler_params=pltpu.CompilerParams(vmem_limit_bytes=32 * 1024 * 1024),
        cost_estimate=pl.CostEstimate(
            flops=flops,
            bytes_accessed=2 * (early + late) * members * rows * columns
            + 4 * columns * n_freq * tiles * 2 * columns,
            transcendentals=0,
        ),
        name="chi",
    )(scalars, *owns, *mates, *units, *([right_a] * 4), *(list(rights_b) * 2))


def fast(shape, unit, eigenvectors, part, val_count, cond_count, n_freq, factor):
    nz, ny, nc, nx = shape
    z, y, c, x = [lax.axis_index(name).astype(jnp.int32) for name in AXES]
    columns = eigenvectors.shape[1]
    places = [(i, j, k, t) for i in range(nz) for j in range(ny) for k in range(nc) for t in range(nx)]
    number = {place: at for at, place in enumerate(places)}

    def send(array, target):
        pairs = [(number[place], target(*place)) for place in places]
        return lax.ppermute(
            array, AXES, [(source, number[to]) for source, to in pairs if to is not None]
        )

    def along_z(array, moves):
        moves = dict(moves)
        return send(array, lambda i, j, k, t: (moves[i], j, k, t) if i in moves else None)

    here = y * nc + c
    eigs = [
        lax.dynamic_slice_in_dim(eigenvectors, lax.bitwise_xor(here, k) * part, part, 0)
        for k in range(ny * nc)
    ]
    unit, eigs = lax.optimization_barrier((unit, eigs))
    for q in range(1, ny * nc):
        eigs[q] = send(
            eigs[q], functools.partial(lambda q, i, j, k, t: (i, j ^ (q // 2), k ^ (q % 2), t), q)
        )

    inner = (z == 1) | (z == 2)
    near = along_z(unit, [(0, 1), (1, 0), (2, 3), (3, 2)])
    middle = along_z(unit, [(1, 2), (2, 1)])
    across = along_z(near, [(1, 2), (2, 1)])
    outward = along_z(middle, [(1, 0), (2, 3)])
    far = along_z(across, [(1, 0), (2, 3)])
    units = [unit, near, jnp.where(inner, across, outward)]

    place = x[None]

    def coefficients(unit, ready=None, settled=None):
        keep, away = project(unit, eigs, place, val_count, cond_count)
        sums = keep + send(away, lambda i, j, k, t: (i, j, 1 - k, t))
        if ready is not None:
            sums, _ = lax.optimization_barrier((sums, ready))
        total = sums[0, 0] + send(sums[0, 1], lambda i, j, k, t: (i, j, k, 1 - t))
        total = total + send(sums[1, 0], lambda i, j, k, t: (i, 1 - j, k, t))
        total = total + send(sums[1, 1], lambda i, j, k, t: (i, 1 - j, k, 1 - t))
        if settled is not None:
            total, _ = lax.optimization_barrier((total, settled))
        return total.astype(jnp.bfloat16)

    def mate(own):
        return send(own, lambda i, j, k, t: (i, j, k, 1 - t))

    def share(own, m):
        return send(own, lambda i, j, k, t: ((2 * t + i % 2) ^ m, j, k, i // 2))

    owns = [coefficients(units[0], (across, outward)), coefficients(units[1])]
    own_a = jnp.stack(owns)
    share_a = share(own_a, 0)
    mate_a = mate(own_a)
    right_a = lax.all_gather(share_a, ("z", "y", "c"), axis=0)
    owns.append(coefficients(units[2], None, (far, mate_a, share_a)))
    units.append(jnp.where(inner, middle, far))
    owns.append(coefficients(units[3], owns[2]))
    own_b = jnp.stack(owns[2:])
    shares = [share(own_b, m) for m in range(nz)]
    shares, mate_b, right_a = lax.optimization_barrier((shares, mate(own_b), right_a))
    held = jnp.stack(shares)
    other = send(held, lambda i, j, k, t: (i, 1 - j, k, t))
    across_core = lambda i, j, k, t: (i, j, 1 - k, t)
    rights_b = [held, other, send(held, across_core), send(other, across_core)]
    mates = [mate_a[0], mate_a[1], mate_b[0], mate_b[1]]
    scalars = jnp.stack([z, y, c, 2 * x, x])
    return make_chi(owns, mates, units, right_a, rights_b, scalars, n_freq, factor)


def plain(shape, unit, eigenvectors, part, val_count, cond_count, n_freq, factor):
    nz, ny, nc, nx = shape
    z = lax.axis_index("z").astype(jnp.int32)
    x = lax.axis_index("x").astype(jnp.int32)
    group = ny * nc
    n_parts = group * nx
    segs = cond_count // val_count
    seg = part // segs
    columns = eigenvectors.shape[1]
    zfold = nz // nx
    eigs = lax.all_to_all(
        eigenvectors.reshape(group, part, columns), ("y", "c"), 0, 0, tiled=True
    )
    every = lax.all_gather(unit, "z", axis=0)

    def coefficients(unit):
        cond = unit[:, :part].reshape(1, n_parts, cond_count, segs, seg)
        val = unit[:, part : part + seg].reshape(n_parts, segs, val_count, seg)
        val = val.transpose(2, 0, 1, 3)[:, :, None]
        density = (cond.astype(jnp.float32) * val.astype(jnp.float32)).astype(jnp.bfloat16)
        sums = jnp.einsum(
            "pg,qgs->qps", density.reshape(-1, part), eigs, preferred_element_type=jnp.float32
        )
        sums = sums.reshape(n_parts, -1, columns)
        sums = lax.all_to_all(sums, ("y", "c", "x"), 0, 0, tiled=True)
        return jnp.sum(sums, axis=0).astype(jnp.bfloat16)

    own = jnp.stack([coefficients(every[k]) for k in range(nz)])
    lefts = lax.all_gather(own, "x", axis=0)
    perm = []
    for s in range(nz):
        for q in range(group):
            for t in range(nx):
                target = ((s % zfold + zfold * t) * group + q) * nx + s // zfold
                perm.append(((s * group + q) * nx + t, target))
    share = lax.ppermute(own, AXES, perm)
    right = lax.all_gather(share, ("z", "y", "c"), axis=0)
    rows = own.shape[1]
    total = 0.0
    for k in range(nz):
        scale = every[k][:, part + seg : part + seg + val_count * (n_freq + 1)].astype(jnp.float32)
        scale = scale.reshape(n_parts * cond_count, val_count, n_freq + 1).transpose(1, 0, 2)
        scale = scale.reshape(nx, rows, n_freq + 1)
        scale = scale[..., :n_freq] * scale[..., n_freq:]
        weighted = (lefts[:, k, :, :, None].astype(jnp.float32) * scale[:, :, None, :]).astype(
            jnp.bfloat16
        )
        weighted = weighted.reshape(nx * rows, columns * n_freq)
        piece = right[:, k].reshape(nx, zfold * group, rows, columns)
        piece = piece.transpose(0, 2, 1, 3).reshape(nx * rows, zfold * group * columns)
        total = total + lax.dot_general(
            weighted, piece, (((0,), (0,)), ((), ())), preferred_element_type=jnp.float32
        )
    return (total * factor).reshape(columns, n_freq, zfold * group * columns)


def local(
    shape,
    val_orbitals,
    cond_orbitals,
    val_energy,
    cond_energy,
    val_slot,
    cond_slot,
    eigenvectors,
    frequencies,
):
    nz, ny, nc, nx = shape
    val_count, n_grid = val_orbitals.shape
    cond_count = cond_orbitals.shape[0]
    n_parts = ny * nc * nx
    part = n_grid // n_parts
    seg = part * val_count // cond_count
    columns = eigenvectors.shape[1]
    factor = -1.0 / math.sqrt(val_slot.shape[0] * nz * n_parts)
    packed = pack(
        val_orbitals,
        cond_orbitals,
        val_energy,
        cond_energy,
        val_slot,
        cond_slot,
        frequencies,
        nx,
        ny * nc,
    )
    unit = lax.all_to_all(packed, ("y", "c", "x"), 0, 0, tiled=True)
    unit = unit.reshape(n_parts * cond_count, part + seg + LANES)
    on_tiles = columns % LANES == 0 and seg % LANES == 0
    run = fast if on_tiles and nx == 2 and nz == 4 and val_count == 4 else plain
    return run(
        shape, unit, eigenvectors, part, val_count, cond_count, frequencies.shape[0], factor
    )


def solution(mesh):
    n_pair = mesh.shape["pair"]
    n_proj = mesh.shape["proj"]
    shape = (n_pair // 4, 2, 2, n_proj)
    grid = Mesh(mesh.devices.reshape(shape), AXES)
    return jax.shard_map(
        functools.partial(local, shape),
        mesh=grid,
        in_specs=(
            P(AXES, None),
            P(AXES, None),
            P(AXES),
            P(AXES),
            P(AXES),
            P(AXES),
            P("x", ("z", "y", "c")),
            P(),
        ),
        out_specs=P(("z", "y", "c"), None, "x"),
        check_vma=False,
    )
```

```python
import functools
import math

import jax
import jax.numpy as jnp
from jax import lax
from jax.experimental import pallas as pl
from jax.experimental.pallas import tpu as pltpu
from jax.sharding import Mesh
from jax.sharding import PartitionSpec as P

LANES = 128
AXES = ("z", "y", "c", "x")


def pack_kernel(nx, part, seg, val_energy, cond_energy, val_slot, cond_slot, frequencies, *refs):
    conds = refs[:nx]
    vals = refs[nx : 2 * nx]
    out, extra = refs[2 * nx :]
    val_count = val_energy.shape[0]
    cond_count = cond_energy.shape[0]
    n_freq = frequencies.shape[0]
    stride = n_freq + 1

    @pl.when(pl.program_id(0) == 0)
    def _():
        row = lax.broadcasted_iota(jnp.int32, (cond_count, LANES), 0)
        lane = lax.broadcasted_iota(jnp.int32, (cond_count, LANES), 1)
        cond_level = jnp.zeros((cond_count, LANES), jnp.float32)
        for c in range(cond_count):
            cond_level = jnp.where(row == c, cond_energy[c], cond_level)
        val_level = jnp.zeros((cond_count, LANES), jnp.float32)
        freq = jnp.zeros((cond_count, LANES), jnp.float32)
        is_count = lane < 0
        for v in range(val_count):
            for f in range(stride):
                here = lane == v * stride + f
                val_level = jnp.where(here, val_energy[v], val_level)
                if f < n_freq:
                    freq = jnp.where(here, frequencies[f], freq)
                else:
                    is_count = is_count | here
        gap = cond_level - val_level
        weight = 4.0 * gap / (gap * gap + freq * freq)

        def add(p, number):
            here = (row == cond_slot[p]) & (lane == val_slot[p] * stride + n_freq)
            return number + jnp.where(here, 1.0, 0.0)

        number = lax.fori_loop(0, val_slot.shape[0], add, jnp.zeros((cond_count, LANES), jnp.float32))
        used = lane < val_count * stride
        extra[...] = jnp.where(used, jnp.where(is_count, number, weight), 0.0).astype(jnp.bfloat16)

    for t in range(nx):
        out[t, :, :part] = conds[t][...]
        val = vals[t][...].astype(jnp.float32)
        pieces = [val[:, k * seg : (k + 1) * seg] for k in range(part // seg)]
        out[t, :, part : part + seg] = jnp.concatenate(pieces, axis=0).astype(jnp.bfloat16)
        out[t, :, part + seg :] = extra[...]


def pack(val_orbitals, cond_orbitals, val_energy, cond_energy, val_slot, cond_slot, frequencies, nx, group):
    val_count, n_grid = val_orbitals.shape
    cond_count = cond_orbitals.shape[0]
    n_freq = frequencies.shape[0]
    n_parts = group * nx
    part = n_grid // n_parts
    segs = cond_count // val_count
    seg = part // segs
    width = part + seg + LANES
    if seg % LANES == 0:
        smem = pl.BlockSpec(memory_space=pltpu.SMEM)
        piece = lambda rows: [
            pl.BlockSpec((rows, part), functools.partial(lambda t, i: (0, t * group + i), t))
            for t in range(nx)
        ]
        return pl.pallas_call(
            functools.partial(pack_kernel, nx, part, seg),
            out_shape=jax.ShapeDtypeStruct((n_parts, cond_count, width), jnp.bfloat16),
            grid=(group,),
            in_specs=[smem] * 5 + piece(cond_count) + piece(val_count),
            out_specs=pl.BlockSpec((nx, cond_count, width), lambda i: (i, 0, 0)),
            scratch_shapes=[pltpu.VMEM((cond_count, LANES), jnp.bfloat16)],
            name="pack",
        )(
            val_energy,
            cond_energy,
            val_slot,
            cond_slot,
            frequencies,
            *([cond_orbitals] * nx),
            *([val_orbitals] * nx),
        )
    gap = cond_energy[:, None] - val_energy[None, :]
    weights = (
        4.0 * gap[:, :, None] / (gap[:, :, None] ** 2 + frequencies[None, None, :] ** 2)
    ).astype(jnp.bfloat16)
    chosen = (cond_slot[:, None, None] == jnp.arange(cond_count, dtype=jnp.int32)[None, :, None]) & (
        val_slot[:, None, None] == jnp.arange(val_count, dtype=jnp.int32)[None, None, :]
    )
    counts = jnp.sum(chosen.astype(jnp.float32), axis=0).astype(jnp.bfloat16)
    extra = jnp.concatenate([weights, counts[:, :, None]], axis=2).reshape(
        cond_count, val_count * (n_freq + 1)
    )
    extra = jnp.pad(extra, ((0, 0), (0, LANES - extra.shape[1])))
    cond_parts = cond_orbitals.reshape(cond_count, nx, group, part).transpose(2, 1, 0, 3)
    val_parts = val_orbitals.reshape(val_count, nx, group, segs, seg).transpose(2, 1, 3, 0, 4)
    return jnp.concatenate(
        [
            cond_parts.reshape(n_parts, cond_count, part),
            val_parts.reshape(n_parts, cond_count, seg),
            jnp.broadcast_to(extra, (n_parts,) + extra.shape),
        ],
        axis=2,
    )


def project_kernel(segs, val_count, cond_count, place, *refs):
    conds = refs[:segs]
    val = refs[segs]
    eigs = refs[segs + 1 : 5 * segs + 1]
    keep, send, density, total = refs[5 * segs + 1 :]
    rows = val.shape[0]
    blocks = rows // cond_count
    columns = keep.shape[-1]
    half = keep.shape[-2]
    turn = place[0] * 2

    for k in range(segs):

        @pl.loop(0, blocks)
        def _(j):
            at = pl.ds(pl.multiple_of(j * cond_count, cond_count), cond_count)
            c = conds[k][at, :].astype(jnp.float32)
            vals = val[at, :].astype(jnp.float32)
            for v in range(val_count):
                row = k * val_count + v
                product = (c * vals[row : row + 1, :]).astype(jnp.bfloat16)
                start = lax.bitwise_xor(v, turn) * rows + j * cond_count
                density[pl.ds(pl.multiple_of(start, cond_count), cond_count), :] = product

        eig = jnp.concatenate([eigs[4 * k + q][...] for q in range(4)], axis=1)
        sums = jnp.dot(density[...], eig, preferred_element_type=jnp.float32)
        if k == 0:

            @pl.when(pl.program_id(0) == 0)
            def _():
                total[...] = sums

            @pl.when(pl.program_id(0) > 0)
            def _():
                total[...] += sums
        else:
            total[...] += sums

    @pl.when(pl.program_id(0) == pl.num_programs(0) - 1)
    def _():
        for q in range(4):
            out = send if q % 2 else keep
            for h in range(2):
                out[q // 2, h] = total[h * half : (h + 1) * half, q * columns : (q + 1) * columns]


def project(unit, eigs, place, val_count, cond_count):
    part, columns = eigs[0].shape
    segs = cond_count // val_count
    seg = part // segs
    rows = unit.shape[0]
    half = rows * val_count // 2
    width = math.gcd(seg, 384)
    steps = seg // width
    in_specs = (
        [
            pl.BlockSpec((rows, width), functools.partial(lambda k, i, place: (0, k * steps + i), k))
            for k in range(segs)
        ]
        + [pl.BlockSpec((rows, width), lambda i, place: (0, segs * steps + i))]
        + [
            pl.BlockSpec((width, columns), functools.partial(lambda k, i, place: (k * steps + i, 0), k))
            for k in range(segs)
            for q in range(4)
        ]
    )
    shape = (2, 2, half, columns)
    out = jax.ShapeDtypeStruct(shape, jnp.float32)
    out_spec = pl.BlockSpec(shape, lambda i, place: (0, 0, 0, 0))
    return pl.pallas_call(
        functools.partial(project_kernel, segs, val_count, cond_count),
        out_shape=[out, out],
        grid_spec=pltpu.PrefetchScalarGridSpec(
            num_scalar_prefetch=1,
            grid=(steps,),
            in_specs=in_specs,
            out_specs=[out_spec, out_spec],
            scratch_shapes=[
                pltpu.VMEM((2 * half, width), jnp.bfloat16),
                pltpu.VMEM((2 * half, 4 * columns), jnp.float32),
            ],
        ),
        compiler_params=pltpu.CompilerParams(vmem_limit_bytes=32 * 1024 * 1024),
        cost_estimate=pl.CostEstimate(
            flops=16 * half * part * columns,
            bytes_accessed=2 * (unit.size + 4 * part * columns),
            transcendentals=0,
        ),
        name="project",
    )(place, *([unit] * (segs + 1)), *(list(eigs) * segs))


def weigh(owns, mates, scales, mine, n_freq, out):
    slots = len(owns)
    rows, columns = owns[0].shape
    stride = n_freq + 1
    width = scales[0].shape[0]
    for k in range(slots):
        scale = scales[k][...].astype(jnp.float32).T
        own = owns[k][...].astype(jnp.float32).T
        mate = mates[k][...].astype(jnp.float32).T
        for h in range(2):
            coeffs = jnp.where(mine == h, own, mate)
            for at in range(0, rows, width):
                v = (h * rows + at) // width
                number = scale[v * stride + n_freq : v * stride + n_freq + 1, :]
                for f in range(n_freq):
                    one = scale[v * stride + f : v * stride + f + 1, :] * number
                    out[k, f * columns : (f + 1) * columns, h * rows + at : h * rows + at + width] = (
                        coeffs[:, at : at + width] * one
                    ).astype(jnp.bfloat16)


def chi_kernel(early, late, n_freq, factor, scalars, *refs):
    slots = early + late
    owns = refs[:slots]
    mates = refs[slots : 2 * slots]
    scales = refs[2 * slots : 3 * slots]
    rights_a = refs[3 * slots : 3 * slots + 4]
    rights_b = refs[3 * slots + 4 : 3 * slots + 12]
    out, weighted = refs[3 * slots + 12 :]
    columns = out.shape[0]

    @pl.when(pl.program_id(0) == 0)
    def _():
        weigh(owns, mates, scales, scalars[4], n_freq, weighted)

    core = scalars[2]
    same_y = scalars[1] == lax.rem(pl.program_id(0), 2)
    shift = lax.bitwise_xor(scalars[0], scalars[3] + pl.program_id(0) // 2)
    left, right = [], []
    for r in range(slots):
        left.append(weighted[lax.bitwise_xor(shift, r)])
        for h in range(2):
            if r < early:
                pair = [rights_a[2 * h + c][0, r] for c in range(2)]
            else:
                own, other, mate, both = [rights_b[4 * h + q][0, r - early] for q in range(4)]
                own = jnp.where(same_y, own, other)
                mate = jnp.where(same_y, mate, both)
                pair = [jnp.where(core == c, own, mate) for c in range(2)]
            right.append(jnp.concatenate(pair, axis=1))
    chi = jnp.dot(
        jnp.concatenate(left, axis=1),
        jnp.concatenate(right, axis=0),
        preferred_element_type=jnp.float32,
    )
    for f in range(n_freq):
        out[:, f, :] = chi[f * columns : (f + 1) * columns, :] * factor


def make_chi(owns, mates, units, right_a, rights_b, scalars, n_freq, factor):
    members, early, rows, columns = right_a.shape
    tiles = members // 4
    late = rights_b[0].shape[1]
    slots = early + late
    width = units[0].shape[0]
    last = units[0].shape[1] // LANES - 1
    flops = 4 * slots * rows * n_freq * columns * tiles * 2 * columns

    def near(h, i, scalars):
        return (lax.bitwise_xor(scalars[0], h * 2 + i // 2), 0, 0, 0)

    return pl.pallas_call(
        functools.partial(chi_kernel, early, late, n_freq, factor),
        out_shape=jax.ShapeDtypeStruct((columns, n_freq, tiles * 2 * columns), jnp.float32),
        grid_spec=pltpu.PrefetchScalarGridSpec(
            num_scalar_prefetch=1,
            grid=(tiles,),
            in_specs=[pl.BlockSpec((rows, columns), lambda i, scalars: (0, 0))] * (2 * slots)
            + [pl.BlockSpec((width, LANES), lambda i, scalars: (0, last))] * slots
            + [
                pl.BlockSpec(
                    (1, early, rows, columns),
                    functools.partial(
                        lambda h, c, i, scalars: (h * tiles * 2 + i * 2 + c, 0, 0, 0), h, c
                    ),
                )
                for h in range(2)
                for c in range(2)
            ]
            + [
                pl.BlockSpec((1, late, rows, columns), functools.partial(near, h))
                for h in range(2)
                for q in range(4)
            ],
            out_specs=pl.BlockSpec((columns, n_freq, 2 * columns), lambda i, scalars: (0, 0, i)),
            scratch_shapes=[pltpu.VMEM((slots, n_freq * columns, 2 * rows), jnp.bfloat16)],
        ),
        compiler_params=pltpu.CompilerParams(vmem_limit_bytes=32 * 1024 * 1024),
        cost_estimate=pl.CostEstimate(
            flops=flops,
            bytes_accessed=2 * (early + late) * members * rows * columns
            + 4 * columns * n_freq * tiles * 2 * columns,
            transcendentals=0,
        ),
        name="chi",
    )(scalars, *owns, *mates, *units, *([right_a] * 4), *(list(rights_b) * 2))


def fast(shape, unit, eigenvectors, part, val_count, cond_count, n_freq, factor):
    nz, ny, nc, nx = shape
    z, y, c, x = [lax.axis_index(name).astype(jnp.int32) for name in AXES]
    columns = eigenvectors.shape[1]
    places = [(i, j, k, t) for i in range(nz) for j in range(ny) for k in range(nc) for t in range(nx)]
    number = {place: at for at, place in enumerate(places)}

    def send(array, target):
        pairs = [(number[place], target(*place)) for place in places]
        return lax.ppermute(
            array, AXES, [(source, number[to]) for source, to in pairs if to is not None]
        )

    def along_z(array, moves):
        moves = dict(moves)
        return send(array, lambda i, j, k, t: (moves[i], j, k, t) if i in moves else None)

    here = y * nc + c
    eigs = [
        lax.dynamic_slice_in_dim(eigenvectors, lax.bitwise_xor(here, k) * part, part, 0)
        for k in range(ny * nc)
    ]
    unit, eigs = lax.optimization_barrier((unit, eigs))
    for q in range(1, ny * nc):
        eigs[q] = send(
            eigs[q], functools.partial(lambda q, i, j, k, t: (i, j ^ (q // 2), k ^ (q % 2), t), q)
        )

    inner = (z == 1) | (z == 2)
    near = along_z(unit, [(0, 1), (1, 0), (2, 3), (3, 2)])
    middle = along_z(unit, [(1, 2), (2, 1)])
    across = along_z(near, [(1, 2), (2, 1)])
    outward = along_z(middle, [(1, 0), (2, 3)])
    far = along_z(across, [(1, 0), (2, 3)])
    units = [unit, near, jnp.where(inner, across, outward)]

    place = x[None]

    def coefficients(unit, ready=None, settled=None):
        keep, away = project(unit, eigs, place, val_count, cond_count)
        sums = keep + send(away, lambda i, j, k, t: (i, j, 1 - k, t))
        if ready is not None:
            sums, _ = lax.optimization_barrier((sums, ready))
        total = sums[0, 0] + send(sums[0, 1], lambda i, j, k, t: (i, j, k, 1 - t))
        total = total + send(sums[1, 0], lambda i, j, k, t: (i, 1 - j, k, t))
        total = total + send(sums[1, 1], lambda i, j, k, t: (i, 1 - j, k, 1 - t))
        if settled is not None:
            total, _ = lax.optimization_barrier((total, settled))
        return total.astype(jnp.bfloat16)

    def mate(own):
        return send(own, lambda i, j, k, t: (i, j, k, 1 - t))

    def share(own, m):
        return send(own, lambda i, j, k, t: ((2 * t + i % 2) ^ m, j, k, i // 2))

    units[1], _ = lax.optimization_barrier((units[1], (across, outward)))
    owns = [coefficients(units[0]), coefficients(units[1])]
    own_a = jnp.stack(owns)
    share_a = share(own_a, 0)
    mate_a = mate(own_a)
    right_a = lax.all_gather(share_a, ("z", "y", "c"), axis=0)
    owns.append(coefficients(units[2], (far, mate_a, share_a)))
    units.append(jnp.where(inner, middle, far))
    owns.append(coefficients(units[3], owns[2]))
    own_b = jnp.stack(owns[2:])
    shares = [share(own_b, m) for m in range(nz)]
    shares, mate_b, right_a = lax.optimization_barrier((shares, mate(own_b), right_a))
    held = jnp.stack(shares)
    other = send(held, lambda i, j, k, t: (i, 1 - j, k, t))
    across_core = lambda i, j, k, t: (i, j, 1 - k, t)
    rights_b = [held, other, send(held, across_core), send(other, across_core)]
    mates = [mate_a[0], mate_a[1], mate_b[0], mate_b[1]]
    scalars = jnp.stack([z, y, c, 2 * x, x])
    return make_chi(owns, mates, units, right_a, rights_b, scalars, n_freq, factor)


def plain(shape, unit, eigenvectors, part, val_count, cond_count, n_freq, factor):
    nz, ny, nc, nx = shape
    z = lax.axis_index("z").astype(jnp.int32)
    x = lax.axis_index("x").astype(jnp.int32)
    group = ny * nc
    n_parts = group * nx
    segs = cond_count // val_count
    seg = part // segs
    columns = eigenvectors.shape[1]
    zfold = nz // nx
    eigs = lax.all_to_all(
        eigenvectors.reshape(group, part, columns), ("y", "c"), 0, 0, tiled=True
    )
    every = lax.all_gather(unit, "z", axis=0)

    def coefficients(unit):
        cond = unit[:, :part].reshape(1, n_parts, cond_count, segs, seg)
        val = unit[:, part : part + seg].reshape(n_parts, segs, val_count, seg)
        val = val.transpose(2, 0, 1, 3)[:, :, None]
        density = (cond.astype(jnp.float32) * val.astype(jnp.float32)).astype(jnp.bfloat16)
        sums = jnp.einsum(
            "pg,qgs->qps", density.reshape(-1, part), eigs, preferred_element_type=jnp.float32
        )
        sums = sums.reshape(n_parts, -1, columns)
        sums = lax.all_to_all(sums, ("y", "c", "x"), 0, 0, tiled=True)
        return jnp.sum(sums, axis=0).astype(jnp.bfloat16)

    own = jnp.stack([coefficients(every[k]) for k in range(nz)])
    lefts = lax.all_gather(own, "x", axis=0)
    perm = []
    for s in range(nz):
        for q in range(group):
            for t in range(nx):
                target = ((s % zfold + zfold * t) * group + q) * nx + s // zfold
                perm.append(((s * group + q) * nx + t, target))
    share = lax.ppermute(own, AXES, perm)
    right = lax.all_gather(share, ("z", "y", "c"), axis=0)
    rows = own.shape[1]
    total = 0.0
    for k in range(nz):
        scale = every[k][:, part + seg : part + seg + val_count * (n_freq + 1)].astype(jnp.float32)
        scale = scale.reshape(n_parts * cond_count, val_count, n_freq + 1).transpose(1, 0, 2)
        scale = scale.reshape(nx, rows, n_freq + 1)
        scale = scale[..., :n_freq] * scale[..., n_freq:]
        weighted = (lefts[:, k, :, :, None].astype(jnp.float32) * scale[:, :, None, :]).astype(
            jnp.bfloat16
        )
        weighted = weighted.reshape(nx * rows, columns * n_freq)
        piece = right[:, k].reshape(nx, zfold * group, rows, columns)
        piece = piece.transpose(0, 2, 1, 3).reshape(nx * rows, zfold * group * columns)
        total = total + lax.dot_general(
            weighted, piece, (((0,), (0,)), ((), ())), preferred_element_type=jnp.float32
        )
    return (total * factor).reshape(columns, n_freq, zfold * group * columns)


def local(
    shape,
    val_orbitals,
    cond_orbitals,
    val_energy,
    cond_energy,
    val_slot,
    cond_slot,
    eigenvectors,
    frequencies,
):
    nz, ny, nc, nx = shape
    val_count, n_grid = val_orbitals.shape
    cond_count = cond_orbitals.shape[0]
    n_parts = ny * nc * nx
    part = n_grid // n_parts
    seg = part * val_count // cond_count
    columns = eigenvectors.shape[1]
    factor = -1.0 / math.sqrt(val_slot.shape[0] * nz * n_parts)
    packed = pack(
        val_orbitals,
        cond_orbitals,
        val_energy,
        cond_energy,
        val_slot,
        cond_slot,
        frequencies,
        nx,
        ny * nc,
    )
    unit = lax.all_to_all(packed, ("y", "c", "x"), 0, 0, tiled=True)
    unit = unit.reshape(n_parts * cond_count, part + seg + LANES)
    on_tiles = columns % LANES == 0 and seg % LANES == 0
    run = fast if on_tiles and nx == 2 and nz == 4 and val_count == 4 else plain
    return run(
        shape, unit, eigenvectors, part, val_count, cond_count, frequencies.shape[0], factor
    )


def solution(mesh):
    n_pair = mesh.shape["pair"]
    n_proj = mesh.shape["proj"]
    shape = (n_pair // 4, 2, 2, n_proj)
    grid = Mesh(mesh.devices.reshape(shape), AXES)
    return jax.shard_map(
        functools.partial(local, shape),
        mesh=grid,
        in_specs=(
            P(AXES, None),
            P(AXES, None),
            P(AXES),
            P(AXES),
            P(AXES),
            P(AXES),
            P("x", ("z", "y", "c")),
            P(),
        ),
        out_specs=P(("z", "y", "c"), None, "x"),
        check_vma=False,
    )
```

```python
import functools
import math

import jax
import jax.numpy as jnp
from jax import lax
from jax.experimental import pallas as pl
from jax.experimental.pallas import tpu as pltpu
from jax.sharding import Mesh
from jax.sharding import PartitionSpec as P

LANES = 128
AXES = ("z", "y", "c", "x")


def pack_kernel(nx, part, seg, val_energy, cond_energy, val_slot, cond_slot, frequencies, *refs):
    conds = refs[:nx]
    vals = refs[nx : 2 * nx]
    out, extra = refs[2 * nx :]
    val_count = val_energy.shape[0]
    cond_count = cond_energy.shape[0]
    n_freq = frequencies.shape[0]
    stride = n_freq + 1

    @pl.when(pl.program_id(0) == 0)
    def _():
        row = lax.broadcasted_iota(jnp.int32, (cond_count, LANES), 0)
        lane = lax.broadcasted_iota(jnp.int32, (cond_count, LANES), 1)
        cond_level = jnp.zeros((cond_count, LANES), jnp.float32)
        for c in range(cond_count):
            cond_level = jnp.where(row == c, cond_energy[c], cond_level)
        val_level = jnp.zeros((cond_count, LANES), jnp.float32)
        freq = jnp.zeros((cond_count, LANES), jnp.float32)
        is_count = lane < 0
        for v in range(val_count):
            for f in range(stride):
                here = lane == v * stride + f
                val_level = jnp.where(here, val_energy[v], val_level)
                if f < n_freq:
                    freq = jnp.where(here, frequencies[f], freq)
                else:
                    is_count = is_count | here
        gap = cond_level - val_level
        weight = 4.0 * gap / (gap * gap + freq * freq)

        def add(p, number):
            here = (row == cond_slot[p]) & (lane == val_slot[p] * stride + n_freq)
            return number + jnp.where(here, 1.0, 0.0)

        number = lax.fori_loop(0, val_slot.shape[0], add, jnp.zeros((cond_count, LANES), jnp.float32))
        used = lane < val_count * stride
        extra[...] = jnp.where(used, jnp.where(is_count, number, weight), 0.0).astype(jnp.bfloat16)

    for t in range(nx):
        out[t, :, :part] = conds[t][...]
        val = vals[t][...].astype(jnp.float32)
        pieces = [val[:, k * seg : (k + 1) * seg] for k in range(part // seg)]
        out[t, :, part : part + seg] = jnp.concatenate(pieces, axis=0).astype(jnp.bfloat16)
        out[t, :, part + seg :] = extra[...]


def pack(val_orbitals, cond_orbitals, val_energy, cond_energy, val_slot, cond_slot, frequencies, nx, group):
    val_count, n_grid = val_orbitals.shape
    cond_count = cond_orbitals.shape[0]
    n_freq = frequencies.shape[0]
    n_parts = group * nx
    part = n_grid // n_parts
    segs = cond_count // val_count
    seg = part // segs
    width = part + seg + LANES
    if seg % LANES == 0:
        smem = pl.BlockSpec(memory_space=pltpu.SMEM)
        piece = lambda rows: [
            pl.BlockSpec((rows, part), functools.partial(lambda t, i: (0, t * group + i), t))
            for t in range(nx)
        ]
        return pl.pallas_call(
            functools.partial(pack_kernel, nx, part, seg),
            out_shape=jax.ShapeDtypeStruct((n_parts, cond_count, width), jnp.bfloat16),
            grid=(group,),
            in_specs=[smem] * 5 + piece(cond_count) + piece(val_count),
            out_specs=pl.BlockSpec((nx, cond_count, width), lambda i: (i, 0, 0)),
            scratch_shapes=[pltpu.VMEM((cond_count, LANES), jnp.bfloat16)],
            name="pack",
        )(
            val_energy,
            cond_energy,
            val_slot,
            cond_slot,
            frequencies,
            *([cond_orbitals] * nx),
            *([val_orbitals] * nx),
        )
    gap = cond_energy[:, None] - val_energy[None, :]
    weights = (
        4.0 * gap[:, :, None] / (gap[:, :, None] ** 2 + frequencies[None, None, :] ** 2)
    ).astype(jnp.bfloat16)
    chosen = (cond_slot[:, None, None] == jnp.arange(cond_count, dtype=jnp.int32)[None, :, None]) & (
        val_slot[:, None, None] == jnp.arange(val_count, dtype=jnp.int32)[None, None, :]
    )
    counts = jnp.sum(chosen.astype(jnp.float32), axis=0).astype(jnp.bfloat16)
    extra = jnp.concatenate([weights, counts[:, :, None]], axis=2).reshape(
        cond_count, val_count * (n_freq + 1)
    )
    extra = jnp.pad(extra, ((0, 0), (0, LANES - extra.shape[1])))
    cond_parts = cond_orbitals.reshape(cond_count, nx, group, part).transpose(2, 1, 0, 3)
    val_parts = val_orbitals.reshape(val_count, nx, group, segs, seg).transpose(2, 1, 3, 0, 4)
    return jnp.concatenate(
        [
            cond_parts.reshape(n_parts, cond_count, part),
            val_parts.reshape(n_parts, cond_count, seg),
            jnp.broadcast_to(extra, (n_parts,) + extra.shape),
        ],
        axis=2,
    )


def project_kernel(segs, val_count, cond_count, place, *refs):
    conds = refs[:segs]
    val = refs[segs]
    eigs = refs[segs + 1 : 5 * segs + 1]
    keep, send, density, total = refs[5 * segs + 1 :]
    rows = val.shape[0]
    blocks = rows // cond_count
    columns = keep.shape[-1]
    half = keep.shape[-2]
    turn = place[0] * 2

    for k in range(segs):

        @pl.loop(0, blocks)
        def _(j):
            at = pl.ds(pl.multiple_of(j * cond_count, cond_count), cond_count)
            c = conds[k][at, :].astype(jnp.float32)
            vals = val[at, :].astype(jnp.float32)
            for v in range(val_count):
                row = k * val_count + v
                product = (c * vals[row : row + 1, :]).astype(jnp.bfloat16)
                start = lax.bitwise_xor(v, turn) * rows + j * cond_count
                density[pl.ds(pl.multiple_of(start, cond_count), cond_count), :] = product

        eig = jnp.concatenate([eigs[4 * k + q][...] for q in range(4)], axis=1)
        sums = jnp.dot(density[...], eig, preferred_element_type=jnp.float32)
        if k == 0:

            @pl.when(pl.program_id(0) == 0)
            def _():
                total[...] = sums

            @pl.when(pl.program_id(0) > 0)
            def _():
                total[...] += sums
        else:
            total[...] += sums

    @pl.when(pl.program_id(0) == pl.num_programs(0) - 1)
    def _():
        for q in range(4):
            out = send if q % 2 else keep
            for h in range(2):
                out[q // 2, h] = total[h * half : (h + 1) * half, q * columns : (q + 1) * columns]


def project(unit, eigs, place, val_count, cond_count):
    part, columns = eigs[0].shape
    segs = cond_count // val_count
    seg = part // segs
    rows = unit.shape[0]
    half = rows * val_count // 2
    width = math.gcd(seg, 384)
    steps = seg // width
    in_specs = (
        [
            pl.BlockSpec((rows, width), functools.partial(lambda k, i, place: (0, k * steps + i), k))
            for k in range(segs)
        ]
        + [pl.BlockSpec((rows, width), lambda i, place: (0, segs * steps + i))]
        + [
            pl.BlockSpec((width, columns), functools.partial(lambda k, i, place: (k * steps + i, 0), k))
            for k in range(segs)
            for q in range(4)
        ]
    )
    shape = (2, 2, half, columns)
    out = jax.ShapeDtypeStruct(shape, jnp.float32)
    out_spec = pl.BlockSpec(shape, lambda i, place: (0, 0, 0, 0))
    return pl.pallas_call(
        functools.partial(project_kernel, segs, val_count, cond_count),
        out_shape=[out, out],
        grid_spec=pltpu.PrefetchScalarGridSpec(
            num_scalar_prefetch=1,
            grid=(steps,),
            in_specs=in_specs,
            out_specs=[out_spec, out_spec],
            scratch_shapes=[
                pltpu.VMEM((2 * half, width), jnp.bfloat16),
                pltpu.VMEM((2 * half, 4 * columns), jnp.float32),
            ],
        ),
        compiler_params=pltpu.CompilerParams(vmem_limit_bytes=32 * 1024 * 1024),
        cost_estimate=pl.CostEstimate(
            flops=16 * half * part * columns,
            bytes_accessed=2 * (unit.size + 4 * part * columns),
            transcendentals=0,
        ),
        name="project",
    )(place, *([unit] * (segs + 1)), *(list(eigs) * segs))


def weigh(owns, mates, scales, mine, n_freq, out):
    slots = len(owns)
    rows, columns = owns[0].shape
    stride = n_freq + 1
    width = scales[0].shape[0]
    for k in range(slots):
        scale = scales[k][...].astype(jnp.float32).T
        own = owns[k][...].astype(jnp.float32).T
        mate = mates[k][...].astype(jnp.float32).T
        for h in range(2):
            coeffs = jnp.where(mine == h, own, mate)
            for at in range(0, rows, width):
                v = (h * rows + at) // width
                number = scale[v * stride + n_freq : v * stride + n_freq + 1, :]
                for f in range(n_freq):
                    one = scale[v * stride + f : v * stride + f + 1, :] * number
                    out[k, f * columns : (f + 1) * columns, h * rows + at : h * rows + at + width] = (
                        coeffs[:, at : at + width] * one
                    ).astype(jnp.bfloat16)


def chi_kernel(early, late, n_freq, factor, scalars, *refs):
    slots = early + late
    owns = refs[:slots]
    mates = refs[slots : 2 * slots]
    scales = refs[2 * slots : 3 * slots]
    rights_a = refs[3 * slots : 3 * slots + 4]
    rights_b = refs[3 * slots + 4 : 3 * slots + 12]
    out, weighted = refs[3 * slots + 12 :]
    columns = out.shape[0]

    @pl.when(pl.program_id(0) == 0)
    def _():
        weigh(owns, mates, scales, scalars[4], n_freq, weighted)

    core = scalars[2]
    same_y = scalars[1] == lax.rem(pl.program_id(0), 2)
    shift = lax.bitwise_xor(scalars[0], scalars[3] + pl.program_id(0) // 2)
    left, right = [], []
    for r in range(slots):
        left.append(weighted[lax.bitwise_xor(shift, r)])
        for h in range(2):
            if r < early:
                pair = [rights_a[2 * h + c][0, r] for c in range(2)]
            else:
                own, other, mate, both = [rights_b[4 * h + q][0, r - early] for q in range(4)]
                own = jnp.where(same_y, own, other)
                mate = jnp.where(same_y, mate, both)
                pair = [jnp.where(core == c, own, mate) for c in range(2)]
            right.append(jnp.concatenate(pair, axis=1))
    chi = jnp.dot(
        jnp.concatenate(left, axis=1),
        jnp.concatenate(right, axis=0),
        preferred_element_type=jnp.float32,
    )
    for f in range(n_freq):
        out[:, f, :] = chi[f * columns : (f + 1) * columns, :] * factor


def make_chi(owns, mates, units, right_a, rights_b, scalars, n_freq, factor):
    members, early, rows, columns = right_a.shape
    tiles = members // 4
    late = rights_b[0].shape[1]
    slots = early + late
    width = units[0].shape[0]
    last = units[0].shape[1] // LANES - 1
    flops = 4 * slots * rows * n_freq * columns * tiles * 2 * columns

    def near(h, i, scalars):
        return (lax.bitwise_xor(scalars[0], h * 2 + i // 2), 0, 0, 0)

    return pl.pallas_call(
        functools.partial(chi_kernel, early, late, n_freq, factor),
        out_shape=jax.ShapeDtypeStruct((columns, n_freq, tiles * 2 * columns), jnp.float32),
        grid_spec=pltpu.PrefetchScalarGridSpec(
            num_scalar_prefetch=1,
            grid=(tiles,),
            in_specs=[pl.BlockSpec((rows, columns), lambda i, scalars: (0, 0))] * (2 * slots)
            + [pl.BlockSpec((width, LANES), lambda i, scalars: (0, last))] * slots
            + [
                pl.BlockSpec(
                    (1, early, rows, columns),
                    functools.partial(
                        lambda h, c, i, scalars: (h * tiles * 2 + i * 2 + c, 0, 0, 0), h, c
                    ),
                )
                for h in range(2)
                for c in range(2)
            ]
            + [
                pl.BlockSpec((1, late, rows, columns), functools.partial(near, h))
                for h in range(2)
                for q in range(4)
            ],
            out_specs=pl.BlockSpec((columns, n_freq, 2 * columns), lambda i, scalars: (0, 0, i)),
            scratch_shapes=[pltpu.VMEM((slots, n_freq * columns, 2 * rows), jnp.bfloat16)],
        ),
        compiler_params=pltpu.CompilerParams(vmem_limit_bytes=32 * 1024 * 1024),
        cost_estimate=pl.CostEstimate(
            flops=flops,
            bytes_accessed=2 * (early + late) * members * rows * columns
            + 4 * columns * n_freq * tiles * 2 * columns,
            transcendentals=0,
        ),
        name="chi",
    )(scalars, *owns, *mates, *units, *([right_a] * 4), *(list(rights_b) * 2))


def fast(shape, unit, eigenvectors, part, val_count, cond_count, n_freq, factor):
    nz, ny, nc, nx = shape
    z, y, c, x = [lax.axis_index(name).astype(jnp.int32) for name in AXES]
    columns = eigenvectors.shape[1]
    places = [(i, j, k, t) for i in range(nz) for j in range(ny) for k in range(nc) for t in range(nx)]
    number = {place: at for at, place in enumerate(places)}

    def send(array, target):
        pairs = [(number[place], target(*place)) for place in places]
        return lax.ppermute(
            array, AXES, [(source, number[to]) for source, to in pairs if to is not None]
        )

    def along_z(array, moves):
        moves = dict(moves)
        return send(array, lambda i, j, k, t: (moves[i], j, k, t) if i in moves else None)

    here = y * nc + c
    eigs = [
        lax.dynamic_slice_in_dim(eigenvectors, lax.bitwise_xor(here, k) * part, part, 0)
        for k in range(ny * nc)
    ]
    unit, eigs = lax.optimization_barrier((unit, eigs))
    for q in range(1, ny * nc):
        eigs[q] = send(
            eigs[q], functools.partial(lambda q, i, j, k, t: (i, j ^ (q // 2), k ^ (q % 2), t), q)
        )

    inner = (z == 1) | (z == 2)
    near = along_z(unit, [(0, 1), (1, 0), (2, 3), (3, 2)])
    middle = along_z(unit, [(1, 2), (2, 1)])
    across = along_z(near, [(1, 2), (2, 1)])
    outward = along_z(middle, [(1, 0), (2, 3)])
    far = along_z(across, [(1, 0), (2, 3)])
    units = [unit, near, jnp.where(inner, across, outward)]

    place = x[None]

    def coefficients(unit, ready=None, settled=None):
        keep, away = project(unit, eigs, place, val_count, cond_count)
        sums = keep + send(away, lambda i, j, k, t: (i, j, 1 - k, t))
        if ready is not None:
            sums, _ = lax.optimization_barrier((sums, ready))
        total = sums[0, 0] + send(sums[0, 1], lambda i, j, k, t: (i, j, k, 1 - t))
        total = total + send(sums[1, 0], lambda i, j, k, t: (i, 1 - j, k, t))
        total = total + send(sums[1, 1], lambda i, j, k, t: (i, 1 - j, k, 1 - t))
        if settled is not None:
            total, _ = lax.optimization_barrier((total, settled))
        return total.astype(jnp.bfloat16)

    def mate(own):
        return send(own, lambda i, j, k, t: (i, j, k, 1 - t))

    def share(own, m):
        return send(own, lambda i, j, k, t: ((2 * t + i % 2) ^ m, j, k, i // 2))

    owns = [coefficients(units[0], (across, outward)), coefficients(units[1])]
    own_a = jnp.stack(owns)
    mate_a = mate(own_a)
    own_a, far = lax.optimization_barrier((own_a, far))
    right_a = lax.all_gather(share(own_a, 0), ("z", "y", "c"), axis=0)
    owns.append(coefficients(units[2], mate_a))
    units.append(jnp.where(inner, middle, far))
    owns.append(coefficients(units[3], owns[2]))
    own_b = jnp.stack(owns[2:])
    shares = [share(own_b, m) for m in range(nz)]
    shares, mate_b, right_a = lax.optimization_barrier((shares, mate(own_b), right_a))
    held = jnp.stack(shares)
    other = send(held, lambda i, j, k, t: (i, 1 - j, k, t))
    across_core = lambda i, j, k, t: (i, j, 1 - k, t)
    rights_b = [held, other, send(held, across_core), send(other, across_core)]
    mates = [mate_a[0], mate_a[1], mate_b[0], mate_b[1]]
    scalars = jnp.stack([z, y, c, 2 * x, x])
    return make_chi(owns, mates, units, right_a, rights_b, scalars, n_freq, factor)


def plain(shape, unit, eigenvectors, part, val_count, cond_count, n_freq, factor):
    nz, ny, nc, nx = shape
    z = lax.axis_index("z").astype(jnp.int32)
    x = lax.axis_index("x").astype(jnp.int32)
    group = ny * nc
    n_parts = group * nx
    segs = cond_count // val_count
    seg = part // segs
    columns = eigenvectors.shape[1]
    zfold = nz // nx
    eigs = lax.all_to_all(
        eigenvectors.reshape(group, part, columns), ("y", "c"), 0, 0, tiled=True
    )
    every = lax.all_gather(unit, "z", axis=0)

    def coefficients(unit):
        cond = unit[:, :part].reshape(1, n_parts, cond_count, segs, seg)
        val = unit[:, part : part + seg].reshape(n_parts, segs, val_count, seg)
        val = val.transpose(2, 0, 1, 3)[:, :, None]
        density = (cond.astype(jnp.float32) * val.astype(jnp.float32)).astype(jnp.bfloat16)
        sums = jnp.einsum(
            "pg,qgs->qps", density.reshape(-1, part), eigs, preferred_element_type=jnp.float32
        )
        sums = sums.reshape(n_parts, -1, columns)
        sums = lax.all_to_all(sums, ("y", "c", "x"), 0, 0, tiled=True)
        return jnp.sum(sums, axis=0).astype(jnp.bfloat16)

    own = jnp.stack([coefficients(every[k]) for k in range(nz)])
    lefts = lax.all_gather(own, "x", axis=0)
    perm = []
    for s in range(nz):
        for q in range(group):
            for t in range(nx):
                target = ((s % zfold + zfold * t) * group + q) * nx + s // zfold
                perm.append(((s * group + q) * nx + t, target))
    share = lax.ppermute(own, AXES, perm)
    right = lax.all_gather(share, ("z", "y", "c"), axis=0)
    rows = own.shape[1]
    total = 0.0
    for k in range(nz):
        scale = every[k][:, part + seg : part + seg + val_count * (n_freq + 1)].astype(jnp.float32)
        scale = scale.reshape(n_parts * cond_count, val_count, n_freq + 1).transpose(1, 0, 2)
        scale = scale.reshape(nx, rows, n_freq + 1)
        scale = scale[..., :n_freq] * scale[..., n_freq:]
        weighted = (lefts[:, k, :, :, None].astype(jnp.float32) * scale[:, :, None, :]).astype(
            jnp.bfloat16
        )
        weighted = weighted.reshape(nx * rows, columns * n_freq)
        piece = right[:, k].reshape(nx, zfold * group, rows, columns)
        piece = piece.transpose(0, 2, 1, 3).reshape(nx * rows, zfold * group * columns)
        total = total + lax.dot_general(
            weighted, piece, (((0,), (0,)), ((), ())), preferred_element_type=jnp.float32
        )
    return (total * factor).reshape(columns, n_freq, zfold * group * columns)


def local(
    shape,
    val_orbitals,
    cond_orbitals,
    val_energy,
    cond_energy,
    val_slot,
    cond_slot,
    eigenvectors,
    frequencies,
):
    nz, ny, nc, nx = shape
    val_count, n_grid = val_orbitals.shape
    cond_count = cond_orbitals.shape[0]
    n_parts = ny * nc * nx
    part = n_grid // n_parts
    seg = part * val_count // cond_count
    columns = eigenvectors.shape[1]
    factor = -1.0 / math.sqrt(val_slot.shape[0] * nz * n_parts)
    packed = pack(
        val_orbitals,
        cond_orbitals,
        val_energy,
        cond_energy,
        val_slot,
        cond_slot,
        frequencies,
        nx,
        ny * nc,
    )
    unit = lax.all_to_all(packed, ("y", "c", "x"), 0, 0, tiled=True)
    unit = unit.reshape(n_parts * cond_count, part + seg + LANES)
    on_tiles = columns % LANES == 0 and seg % LANES == 0
    run = fast if on_tiles and nx == 2 and nz == 4 and val_count == 4 else plain
    return run(
        shape, unit, eigenvectors, part, val_count, cond_count, frequencies.shape[0], factor
    )


def solution(mesh):
    n_pair = mesh.shape["pair"]
    n_proj = mesh.shape["proj"]
    shape = (n_pair // 4, 2, 2, n_proj)
    grid = Mesh(mesh.devices.reshape(shape), AXES)
    return jax.shard_map(
        functools.partial(local, shape),
        mesh=grid,
        in_specs=(
            P(AXES, None),
            P(AXES, None),
            P(AXES),
            P(AXES),
            P(AXES),
            P(AXES),
            P("x", ("z", "y", "c")),
            P(),
        ),
        out_specs=P(("z", "y", "c"), None, "x"),
        check_vma=False,
    )
```

```python
import functools
import math

import jax
import jax.numpy as jnp
from jax import lax
from jax.experimental import pallas as pl
from jax.experimental.pallas import tpu as pltpu
from jax.sharding import Mesh
from jax.sharding import PartitionSpec as P

LANES = 128
AXES = ("z", "y", "c", "x")


def pack_kernel(nx, part, seg, val_energy, cond_energy, val_slot, cond_slot, frequencies, *refs):
    conds = refs[:nx]
    vals = refs[nx : 2 * nx]
    out, extra = refs[2 * nx :]
    val_count = val_energy.shape[0]
    cond_count = cond_energy.shape[0]
    n_freq = frequencies.shape[0]
    stride = n_freq + 1

    @pl.when(pl.program_id(0) == 0)
    def _():
        row = lax.broadcasted_iota(jnp.int32, (cond_count, LANES), 0)
        lane = lax.broadcasted_iota(jnp.int32, (cond_count, LANES), 1)
        cond_level = jnp.zeros((cond_count, LANES), jnp.float32)
        for c in range(cond_count):
            cond_level = jnp.where(row == c, cond_energy[c], cond_level)
        val_level = jnp.zeros((cond_count, LANES), jnp.float32)
        freq = jnp.zeros((cond_count, LANES), jnp.float32)
        is_count = lane < 0
        for v in range(val_count):
            for f in range(stride):
                here = lane == v * stride + f
                val_level = jnp.where(here, val_energy[v], val_level)
                if f < n_freq:
                    freq = jnp.where(here, frequencies[f], freq)
                else:
                    is_count = is_count | here
        gap = cond_level - val_level
        weight = 4.0 * gap / (gap * gap + freq * freq)

        def add(p, number):
            here = (row == cond_slot[p]) & (lane == val_slot[p] * stride + n_freq)
            return number + jnp.where(here, 1.0, 0.0)

        number = lax.fori_loop(0, val_slot.shape[0], add, jnp.zeros((cond_count, LANES), jnp.float32))
        used = lane < val_count * stride
        extra[...] = jnp.where(used, jnp.where(is_count, number, weight), 0.0).astype(jnp.bfloat16)

    for t in range(nx):
        out[t, :, :part] = conds[t][...]
        val = vals[t][...].astype(jnp.float32)
        pieces = [val[:, k * seg : (k + 1) * seg] for k in range(part // seg)]
        out[t, :, part : part + seg] = jnp.concatenate(pieces, axis=0).astype(jnp.bfloat16)
        out[t, :, part + seg :] = extra[...]


def pack(val_orbitals, cond_orbitals, val_energy, cond_energy, val_slot, cond_slot, frequencies, nx, group):
    val_count, n_grid = val_orbitals.shape
    cond_count = cond_orbitals.shape[0]
    n_freq = frequencies.shape[0]
    n_parts = group * nx
    part = n_grid // n_parts
    segs = cond_count // val_count
    seg = part // segs
    width = part + seg + LANES
    if seg % LANES == 0:
        smem = pl.BlockSpec(memory_space=pltpu.SMEM)
        piece = lambda rows: [
            pl.BlockSpec((rows, part), functools.partial(lambda t, i: (0, t * group + i), t))
            for t in range(nx)
        ]
        return pl.pallas_call(
            functools.partial(pack_kernel, nx, part, seg),
            out_shape=jax.ShapeDtypeStruct((n_parts, cond_count, width), jnp.bfloat16),
            grid=(group,),
            in_specs=[smem] * 5 + piece(cond_count) + piece(val_count),
            out_specs=pl.BlockSpec((nx, cond_count, width), lambda i: (i, 0, 0)),
            scratch_shapes=[pltpu.VMEM((cond_count, LANES), jnp.bfloat16)],
            name="pack",
        )(
            val_energy,
            cond_energy,
            val_slot,
            cond_slot,
            frequencies,
            *([cond_orbitals] * nx),
            *([val_orbitals] * nx),
        )
    gap = cond_energy[:, None] - val_energy[None, :]
    weights = (
        4.0 * gap[:, :, None] / (gap[:, :, None] ** 2 + frequencies[None, None, :] ** 2)
    ).astype(jnp.bfloat16)
    chosen = (cond_slot[:, None, None] == jnp.arange(cond_count, dtype=jnp.int32)[None, :, None]) & (
        val_slot[:, None, None] == jnp.arange(val_count, dtype=jnp.int32)[None, None, :]
    )
    counts = jnp.sum(chosen.astype(jnp.float32), axis=0).astype(jnp.bfloat16)
    extra = jnp.concatenate([weights, counts[:, :, None]], axis=2).reshape(
        cond_count, val_count * (n_freq + 1)
    )
    extra = jnp.pad(extra, ((0, 0), (0, LANES - extra.shape[1])))
    cond_parts = cond_orbitals.reshape(cond_count, nx, group, part).transpose(2, 1, 0, 3)
    val_parts = val_orbitals.reshape(val_count, nx, group, segs, seg).transpose(2, 1, 3, 0, 4)
    return jnp.concatenate(
        [
            cond_parts.reshape(n_parts, cond_count, part),
            val_parts.reshape(n_parts, cond_count, seg),
            jnp.broadcast_to(extra, (n_parts,) + extra.shape),
        ],
        axis=2,
    )


def project_kernel(segs, val_count, cond_count, place, *refs):
    conds = refs[:segs]
    val = refs[segs]
    eigs = refs[segs + 1 : 5 * segs + 1]
    keep, send, density, total = refs[5 * segs + 1 :]
    rows = val.shape[0]
    blocks = rows // cond_count
    columns = keep.shape[-1]
    half = keep.shape[-2]
    turn = place[0] * 2

    for k in range(segs):

        @pl.loop(0, blocks)
        def _(j):
            at = pl.ds(pl.multiple_of(j * cond_count, cond_count), cond_count)
            c = conds[k][at, :].astype(jnp.float32)
            vals = val[at, :].astype(jnp.float32)
            for v in range(val_count):
                row = k * val_count + v
                product = (c * vals[row : row + 1, :]).astype(jnp.bfloat16)
                start = lax.bitwise_xor(v, turn) * rows + j * cond_count
                density[pl.ds(pl.multiple_of(start, cond_count), cond_count), :] = product

        eig = jnp.concatenate([eigs[4 * k + q][...] for q in range(4)], axis=1)
        sums = jnp.dot(density[...], eig, preferred_element_type=jnp.float32)
        if k == 0:

            @pl.when(pl.program_id(0) == 0)
            def _():
                total[...] = sums

            @pl.when(pl.program_id(0) > 0)
            def _():
                total[...] += sums
        else:
            total[...] += sums

    @pl.when(pl.program_id(0) == pl.num_programs(0) - 1)
    def _():
        for q in range(4):
            out = send if q % 2 else keep
            for h in range(2):
                out[q // 2, h] = total[h * half : (h + 1) * half, q * columns : (q + 1) * columns]


def project(unit, eigs, place, val_count, cond_count):
    part, columns = eigs[0].shape
    segs = cond_count // val_count
    seg = part // segs
    rows = unit.shape[0]
    half = rows * val_count // 2
    width = math.gcd(seg, 384)
    steps = seg // width
    in_specs = (
        [
            pl.BlockSpec((rows, width), functools.partial(lambda k, i, place: (0, k * steps + i), k))
            for k in range(segs)
        ]
        + [pl.BlockSpec((rows, width), lambda i, place: (0, segs * steps + i))]
        + [
            pl.BlockSpec((width, columns), functools.partial(lambda k, i, place: (k * steps + i, 0), k))
            for k in range(segs)
            for q in range(4)
        ]
    )
    shape = (2, 2, half, columns)
    out = jax.ShapeDtypeStruct(shape, jnp.float32)
    out_spec = pl.BlockSpec(shape, lambda i, place: (0, 0, 0, 0))
    return pl.pallas_call(
        functools.partial(project_kernel, segs, val_count, cond_count),
        out_shape=[out, out],
        grid_spec=pltpu.PrefetchScalarGridSpec(
            num_scalar_prefetch=1,
            grid=(steps,),
            in_specs=in_specs,
            out_specs=[out_spec, out_spec],
            scratch_shapes=[
                pltpu.VMEM((2 * half, width), jnp.bfloat16),
                pltpu.VMEM((2 * half, 4 * columns), jnp.float32),
            ],
        ),
        compiler_params=pltpu.CompilerParams(vmem_limit_bytes=32 * 1024 * 1024),
        cost_estimate=pl.CostEstimate(
            flops=16 * half * part * columns,
            bytes_accessed=2 * (unit.size + 4 * part * columns),
            transcendentals=0,
        ),
        name="project",
    )(place, *([unit] * (segs + 1)), *(list(eigs) * segs))


def weigh(owns, mates, scales, mine, n_freq, out):
    slots = len(owns)
    rows, columns = owns[0].shape
    stride = n_freq + 1
    width = scales[0].shape[0]
    for k in range(slots):
        scale = scales[k][...].astype(jnp.float32).T
        own = owns[k][...].astype(jnp.float32).T
        mate = mates[k][...].astype(jnp.float32).T
        for h in range(2):
            coeffs = jnp.where(mine == h, own, mate)
            for at in range(0, rows, width):
                v = (h * rows + at) // width
                number = scale[v * stride + n_freq : v * stride + n_freq + 1, :]
                for f in range(n_freq):
                    one = scale[v * stride + f : v * stride + f + 1, :] * number
                    out[k, f * columns : (f + 1) * columns, h * rows + at : h * rows + at + width] = (
                        coeffs[:, at : at + width] * one
                    ).astype(jnp.bfloat16)


def chi_kernel(early, late, n_freq, factor, scalars, *refs):
    slots = early + late
    owns = refs[:slots]
    mates = refs[slots : 2 * slots]
    scales = refs[2 * slots : 3 * slots]
    rights_a = refs[3 * slots : 3 * slots + 4]
    rights_b = refs[3 * slots + 4 : 3 * slots + 12]
    out, weighted = refs[3 * slots + 12 :]
    columns = out.shape[0]

    @pl.when(pl.program_id(0) == 0)
    def _():
        weigh(owns, mates, scales, scalars[4], n_freq, weighted)

    core = scalars[2]
    same_y = scalars[1] == lax.rem(pl.program_id(0), 2)
    shift = lax.bitwise_xor(scalars[0], scalars[3] + pl.program_id(0) // 2)
    left, right = [], []
    for r in range(slots):
        left.append(weighted[lax.bitwise_xor(shift, r)])
        for h in range(2):
            if r < early:
                pair = [rights_a[2 * h + c][0, r] for c in range(2)]
            else:
                own, other, mate, both = [rights_b[4 * h + q][0, r - early] for q in range(4)]
                own = jnp.where(same_y, own, other)
                mate = jnp.where(same_y, mate, both)
                pair = [jnp.where(core == c, own, mate) for c in range(2)]
            right.append(jnp.concatenate(pair, axis=1))
    chi = jnp.dot(
        jnp.concatenate(left, axis=1),
        jnp.concatenate(right, axis=0),
        preferred_element_type=jnp.float32,
    )
    for f in range(n_freq):
        out[:, f, :] = chi[f * columns : (f + 1) * columns, :] * factor


def make_chi(owns, mates, units, right_a, rights_b, scalars, n_freq, factor):
    members, early, rows, columns = right_a.shape
    tiles = members // 4
    late = rights_b[0].shape[1]
    slots = early + late
    width = units[0].shape[0]
    last = units[0].shape[1] // LANES - 1
    flops = 4 * slots * rows * n_freq * columns * tiles * 2 * columns

    def near(h, i, scalars):
        return (lax.bitwise_xor(scalars[0], h * 2 + i // 2), 0, 0, 0)

    return pl.pallas_call(
        functools.partial(chi_kernel, early, late, n_freq, factor),
        out_shape=jax.ShapeDtypeStruct((columns, n_freq, tiles * 2 * columns), jnp.float32),
        grid_spec=pltpu.PrefetchScalarGridSpec(
            num_scalar_prefetch=1,
            grid=(tiles,),
            in_specs=[pl.BlockSpec((rows, columns), lambda i, scalars: (0, 0))] * (2 * slots)
            + [pl.BlockSpec((width, LANES), lambda i, scalars: (0, last))] * slots
            + [
                pl.BlockSpec(
                    (1, early, rows, columns),
                    functools.partial(
                        lambda h, c, i, scalars: (h * tiles * 2 + i * 2 + c, 0, 0, 0), h, c
                    ),
                )
                for h in range(2)
                for c in range(2)
            ]
            + [
                pl.BlockSpec((1, late, rows, columns), functools.partial(near, h))
                for h in range(2)
                for q in range(4)
            ],
            out_specs=pl.BlockSpec((columns, n_freq, 2 * columns), lambda i, scalars: (0, 0, i)),
            scratch_shapes=[pltpu.VMEM((slots, n_freq * columns, 2 * rows), jnp.bfloat16)],
        ),
        compiler_params=pltpu.CompilerParams(vmem_limit_bytes=32 * 1024 * 1024),
        cost_estimate=pl.CostEstimate(
            flops=flops,
            bytes_accessed=2 * (early + late) * members * rows * columns
            + 4 * columns * n_freq * tiles * 2 * columns,
            transcendentals=0,
        ),
        name="chi",
    )(scalars, *owns, *mates, *units, *([right_a] * 4), *(list(rights_b) * 2))


def fast(shape, unit, eigenvectors, part, val_count, cond_count, n_freq, factor):
    nz, ny, nc, nx = shape
    z, y, c, x = [lax.axis_index(name).astype(jnp.int32) for name in AXES]
    columns = eigenvectors.shape[1]
    places = [(i, j, k, t) for i in range(nz) for j in range(ny) for k in range(nc) for t in range(nx)]
    number = {place: at for at, place in enumerate(places)}

    def send(array, target):
        pairs = [(number[place], target(*place)) for place in places]
        return lax.ppermute(
            array, AXES, [(source, number[to]) for source, to in pairs if to is not None]
        )

    def along_z(array, moves):
        moves = dict(moves)
        return send(array, lambda i, j, k, t: (moves[i], j, k, t) if i in moves else None)

    here = y * nc + c
    eigs = [
        lax.dynamic_slice_in_dim(eigenvectors, lax.bitwise_xor(here, k) * part, part, 0)
        for k in range(ny * nc)
    ]
    unit, eigs = lax.optimization_barrier((unit, eigs))
    for q in range(1, ny * nc):
        eigs[q] = send(
            eigs[q], functools.partial(lambda q, i, j, k, t: (i, j ^ (q // 2), k ^ (q % 2), t), q)
        )

    inner = (z == 1) | (z == 2)
    near = along_z(unit, [(0, 1), (1, 0), (2, 3), (3, 2)])
    middle = along_z(unit, [(1, 2), (2, 1)])
    across = along_z(near, [(1, 2), (2, 1)])
    outward = along_z(middle, [(1, 0), (2, 3)])
    far = along_z(across, [(1, 0), (2, 3)])
    units = [unit, near, jnp.where(inner, across, outward)]

    place = x[None]

    def coefficients(unit, ready=None, settled=None):
        keep, away = project(unit, eigs, place, val_count, cond_count)
        sums = keep + send(away, lambda i, j, k, t: (i, j, 1 - k, t))
        if ready is not None:
            sums, _ = lax.optimization_barrier((sums, ready))
        total = sums[0, 0] + send(sums[0, 1], lambda i, j, k, t: (i, j, k, 1 - t))
        total = total + send(sums[1, 0], lambda i, j, k, t: (i, 1 - j, k, t))
        total = total + send(sums[1, 1], lambda i, j, k, t: (i, 1 - j, k, 1 - t))
        if settled is not None:
            total, _ = lax.optimization_barrier((total, settled))
        return total.astype(jnp.bfloat16)

    def mate(own):
        return send(own, lambda i, j, k, t: (i, j, k, 1 - t))

    def share(own, m):
        return send(own, lambda i, j, k, t: ((2 * t + i % 2) ^ m, j, k, i // 2))

    owns = [coefficients(units[0], (across, outward)), coefficients(units[1])]
    own_a = jnp.stack(owns)
    mate_a = mate(own_a)
    owns.append(coefficients(units[2]))
    own_a, far, mate_a, owns[2] = lax.optimization_barrier((own_a, far, mate_a, owns[2]))
    right_a = lax.all_gather(share(own_a, 0), ("z", "y", "c"), axis=0)
    units.append(jnp.where(inner, middle, far))
    owns.append(coefficients(units[3]))
    own_b = jnp.stack(owns[2:])
    shares = [share(own_b, m) for m in range(nz)]
    shares, mate_b, right_a = lax.optimization_barrier((shares, mate(own_b), right_a))
    held = jnp.stack(shares)
    other = send(held, lambda i, j, k, t: (i, 1 - j, k, t))
    across_core = lambda i, j, k, t: (i, j, 1 - k, t)
    rights_b = [held, other, send(held, across_core), send(other, across_core)]
    mates = [mate_a[0], mate_a[1], mate_b[0], mate_b[1]]
    scalars = jnp.stack([z, y, c, 2 * x, x])
    return make_chi(owns, mates, units, right_a, rights_b, scalars, n_freq, factor)


def plain(shape, unit, eigenvectors, part, val_count, cond_count, n_freq, factor):
    nz, ny, nc, nx = shape
    z = lax.axis_index("z").astype(jnp.int32)
    x = lax.axis_index("x").astype(jnp.int32)
    group = ny * nc
    n_parts = group * nx
    segs = cond_count // val_count
    seg = part // segs
    columns = eigenvectors.shape[1]
    zfold = nz // nx
    eigs = lax.all_to_all(
        eigenvectors.reshape(group, part, columns), ("y", "c"), 0, 0, tiled=True
    )
    every = lax.all_gather(unit, "z", axis=0)

    def coefficients(unit):
        cond = unit[:, :part].reshape(1, n_parts, cond_count, segs, seg)
        val = unit[:, part : part + seg].reshape(n_parts, segs, val_count, seg)
        val = val.transpose(2, 0, 1, 3)[:, :, None]
        density = (cond.astype(jnp.float32) * val.astype(jnp.float32)).astype(jnp.bfloat16)
        sums = jnp.einsum(
            "pg,qgs->qps", density.reshape(-1, part), eigs, preferred_element_type=jnp.float32
        )
        sums = sums.reshape(n_parts, -1, columns)
        sums = lax.all_to_all(sums, ("y", "c", "x"), 0, 0, tiled=True)
        return jnp.sum(sums, axis=0).astype(jnp.bfloat16)

    own = jnp.stack([coefficients(every[k]) for k in range(nz)])
    lefts = lax.all_gather(own, "x", axis=0)
    perm = []
    for s in range(nz):
        for q in range(group):
            for t in range(nx):
                target = ((s % zfold + zfold * t) * group + q) * nx + s // zfold
                perm.append(((s * group + q) * nx + t, target))
    share = lax.ppermute(own, AXES, perm)
    right = lax.all_gather(share, ("z", "y", "c"), axis=0)
    rows = own.shape[1]
    total = 0.0
    for k in range(nz):
        scale = every[k][:, part + seg : part + seg + val_count * (n_freq + 1)].astype(jnp.float32)
        scale = scale.reshape(n_parts * cond_count, val_count, n_freq + 1).transpose(1, 0, 2)
        scale = scale.reshape(nx, rows, n_freq + 1)
        scale = scale[..., :n_freq] * scale[..., n_freq:]
        weighted = (lefts[:, k, :, :, None].astype(jnp.float32) * scale[:, :, None, :]).astype(
            jnp.bfloat16
        )
        weighted = weighted.reshape(nx * rows, columns * n_freq)
        piece = right[:, k].reshape(nx, zfold * group, rows, columns)
        piece = piece.transpose(0, 2, 1, 3).reshape(nx * rows, zfold * group * columns)
        total = total + lax.dot_general(
            weighted, piece, (((0,), (0,)), ((), ())), preferred_element_type=jnp.float32
        )
    return (total * factor).reshape(columns, n_freq, zfold * group * columns)


def local(
    shape,
    val_orbitals,
    cond_orbitals,
    val_energy,
    cond_energy,
    val_slot,
    cond_slot,
    eigenvectors,
    frequencies,
):
    nz, ny, nc, nx = shape
    val_count, n_grid = val_orbitals.shape
    cond_count = cond_orbitals.shape[0]
    n_parts = ny * nc * nx
    part = n_grid // n_parts
    seg = part * val_count // cond_count
    columns = eigenvectors.shape[1]
    factor = -1.0 / math.sqrt(val_slot.shape[0] * nz * n_parts)
    packed = pack(
        val_orbitals,
        cond_orbitals,
        val_energy,
        cond_energy,
        val_slot,
        cond_slot,
        frequencies,
        nx,
        ny * nc,
    )
    unit = lax.all_to_all(packed, ("y", "c", "x"), 0, 0, tiled=True)
    unit = unit.reshape(n_parts * cond_count, part + seg + LANES)
    on_tiles = columns % LANES == 0 and seg % LANES == 0
    run = fast if on_tiles and nx == 2 and nz == 4 and val_count == 4 else plain
    return run(
        shape, unit, eigenvectors, part, val_count, cond_count, frequencies.shape[0], factor
    )


def solution(mesh):
    n_pair = mesh.shape["pair"]
    n_proj = mesh.shape["proj"]
    shape = (n_pair // 4, 2, 2, n_proj)
    grid = Mesh(mesh.devices.reshape(shape), AXES)
    return jax.shard_map(
        functools.partial(local, shape),
        mesh=grid,
        in_specs=(
            P(AXES, None),
            P(AXES, None),
            P(AXES),
            P(AXES),
            P(AXES),
            P(AXES),
            P("x", ("z", "y", "c")),
            P(),
        ),
        out_specs=P(("z", "y", "c"), None, "x"),
        check_vma=False,
    )
```

```python
import functools
import math

import jax
import jax.numpy as jnp
from jax import lax
from jax.experimental import pallas as pl
from jax.experimental.pallas import tpu as pltpu
from jax.sharding import Mesh
from jax.sharding import PartitionSpec as P

LANES = 128
AXES = ("z", "y", "c", "x")


def pack_kernel(nx, part, seg, val_energy, cond_energy, val_slot, cond_slot, frequencies, *refs):
    conds = refs[:nx]
    vals = refs[nx : 2 * nx]
    out, extra = refs[2 * nx :]
    val_count = val_energy.shape[0]
    cond_count = cond_energy.shape[0]
    n_freq = frequencies.shape[0]
    stride = n_freq + 1

    @pl.when(pl.program_id(0) == 0)
    def _():
        row = lax.broadcasted_iota(jnp.int32, (cond_count, LANES), 0)
        lane = lax.broadcasted_iota(jnp.int32, (cond_count, LANES), 1)
        cond_level = jnp.zeros((cond_count, LANES), jnp.float32)
        for c in range(cond_count):
            cond_level = jnp.where(row == c, cond_energy[c], cond_level)
        val_level = jnp.zeros((cond_count, LANES), jnp.float32)
        freq = jnp.zeros((cond_count, LANES), jnp.float32)
        is_count = lane < 0
        for v in range(val_count):
            for f in range(stride):
                here = lane == v * stride + f
                val_level = jnp.where(here, val_energy[v], val_level)
                if f < n_freq:
                    freq = jnp.where(here, frequencies[f], freq)
                else:
                    is_count = is_count | here
        gap = cond_level - val_level
        weight = 4.0 * gap / (gap * gap + freq * freq)

        def add(p, number):
            here = (row == cond_slot[p]) & (lane == val_slot[p] * stride + n_freq)
            return number + jnp.where(here, 1.0, 0.0)

        number = lax.fori_loop(0, val_slot.shape[0], add, jnp.zeros((cond_count, LANES), jnp.float32))
        used = lane < val_count * stride
        extra[...] = jnp.where(used, jnp.where(is_count, number, weight), 0.0).astype(jnp.bfloat16)

    for t in range(nx):
        out[t, :, :part] = conds[t][...]
        val = vals[t][...].astype(jnp.float32)
        pieces = [val[:, k * seg : (k + 1) * seg] for k in range(part // seg)]
        out[t, :, part : part + seg] = jnp.concatenate(pieces, axis=0).astype(jnp.bfloat16)
        out[t, :, part + seg :] = extra[...]


def pack(val_orbitals, cond_orbitals, val_energy, cond_energy, val_slot, cond_slot, frequencies, nx, group):
    val_count, n_grid = val_orbitals.shape
    cond_count = cond_orbitals.shape[0]
    n_freq = frequencies.shape[0]
    n_parts = group * nx
    part = n_grid // n_parts
    segs = cond_count // val_count
    seg = part // segs
    width = part + seg + LANES
    if seg % LANES == 0:
        smem = pl.BlockSpec(memory_space=pltpu.SMEM)
        piece = lambda rows: [
            pl.BlockSpec((rows, part), functools.partial(lambda t, i: (0, t * group + i), t))
            for t in range(nx)
        ]
        return pl.pallas_call(
            functools.partial(pack_kernel, nx, part, seg),
            out_shape=jax.ShapeDtypeStruct((n_parts, cond_count, width), jnp.bfloat16),
            grid=(group,),
            in_specs=[smem] * 5 + piece(cond_count) + piece(val_count),
            out_specs=pl.BlockSpec((nx, cond_count, width), lambda i: (i, 0, 0)),
            scratch_shapes=[pltpu.VMEM((cond_count, LANES), jnp.bfloat16)],
            name="pack",
        )(
            val_energy,
            cond_energy,
            val_slot,
            cond_slot,
            frequencies,
            *([cond_orbitals] * nx),
            *([val_orbitals] * nx),
        )
    gap = cond_energy[:, None] - val_energy[None, :]
    weights = (
        4.0 * gap[:, :, None] / (gap[:, :, None] ** 2 + frequencies[None, None, :] ** 2)
    ).astype(jnp.bfloat16)
    chosen = (cond_slot[:, None, None] == jnp.arange(cond_count, dtype=jnp.int32)[None, :, None]) & (
        val_slot[:, None, None] == jnp.arange(val_count, dtype=jnp.int32)[None, None, :]
    )
    counts = jnp.sum(chosen.astype(jnp.float32), axis=0).astype(jnp.bfloat16)
    extra = jnp.concatenate([weights, counts[:, :, None]], axis=2).reshape(
        cond_count, val_count * (n_freq + 1)
    )
    extra = jnp.pad(extra, ((0, 0), (0, LANES - extra.shape[1])))
    cond_parts = cond_orbitals.reshape(cond_count, nx, group, part).transpose(2, 1, 0, 3)
    val_parts = val_orbitals.reshape(val_count, nx, group, segs, seg).transpose(2, 1, 3, 0, 4)
    return jnp.concatenate(
        [
            cond_parts.reshape(n_parts, cond_count, part),
            val_parts.reshape(n_parts, cond_count, seg),
            jnp.broadcast_to(extra, (n_parts,) + extra.shape),
        ],
        axis=2,
    )


def project_kernel(segs, val_count, cond_count, place, *refs):
    conds = refs[:segs]
    val = refs[segs]
    eigs = refs[segs + 1 : 5 * segs + 1]
    keep, send, density, total = refs[5 * segs + 1 :]
    rows = val.shape[0]
    blocks = rows // cond_count
    columns = keep.shape[-1]
    half = keep.shape[-2]
    turn = place[0] * 2

    for k in range(segs):

        @pl.loop(0, blocks)
        def _(j):
            at = pl.ds(pl.multiple_of(j * cond_count, cond_count), cond_count)
            c = conds[k][at, :].astype(jnp.float32)
            vals = val[at, :].astype(jnp.float32)
            for v in range(val_count):
                row = k * val_count + v
                product = (c * vals[row : row + 1, :]).astype(jnp.bfloat16)
                start = lax.bitwise_xor(v, turn) * rows + j * cond_count
                density[pl.ds(pl.multiple_of(start, cond_count), cond_count), :] = product

        eig = jnp.concatenate([eigs[4 * k + q][...] for q in range(4)], axis=1)
        sums = jnp.dot(density[...], eig, preferred_element_type=jnp.float32)
        if k == 0:

            @pl.when(pl.program_id(0) == 0)
            def _():
                total[...] = sums

            @pl.when(pl.program_id(0) > 0)
            def _():
                total[...] += sums
        else:
            total[...] += sums

    @pl.when(pl.program_id(0) == pl.num_programs(0) - 1)
    def _():
        for q in range(4):
            out = send if q % 2 else keep
            for h in range(2):
                out[q // 2, h] = total[h * half : (h + 1) * half, q * columns : (q + 1) * columns]


def project(unit, eigs, place, val_count, cond_count):
    part, columns = eigs[0].shape
    segs = cond_count // val_count
    seg = part // segs
    rows = unit.shape[0]
    half = rows * val_count // 2
    width = math.gcd(seg, 384)
    steps = seg // width
    in_specs = (
        [
            pl.BlockSpec((rows, width), functools.partial(lambda k, i, place: (0, k * steps + i), k))
            for k in range(segs)
        ]
        + [pl.BlockSpec((rows, width), lambda i, place: (0, segs * steps + i))]
        + [
            pl.BlockSpec((width, columns), functools.partial(lambda k, i, place: (k * steps + i, 0), k))
            for k in range(segs)
            for q in range(4)
        ]
    )
    shape = (2, 2, half, columns)
    out = jax.ShapeDtypeStruct(shape, jnp.float32)
    out_spec = pl.BlockSpec(shape, lambda i, place: (0, 0, 0, 0))
    return pl.pallas_call(
        functools.partial(project_kernel, segs, val_count, cond_count),
        out_shape=[out, out],
        grid_spec=pltpu.PrefetchScalarGridSpec(
            num_scalar_prefetch=1,
            grid=(steps,),
            in_specs=in_specs,
            out_specs=[out_spec, out_spec],
            scratch_shapes=[
                pltpu.VMEM((2 * half, width), jnp.bfloat16),
                pltpu.VMEM((2 * half, 4 * columns), jnp.float32),
            ],
        ),
        compiler_params=pltpu.CompilerParams(vmem_limit_bytes=32 * 1024 * 1024),
        cost_estimate=pl.CostEstimate(
            flops=16 * half * part * columns,
            bytes_accessed=2 * (unit.size + 4 * part * columns),
            transcendentals=0,
        ),
        name="project",
    )(place, *([unit] * (segs + 1)), *(list(eigs) * segs))


def weigh(owns, mates, scales, mine, n_freq, out):
    slots = len(owns)
    rows, columns = owns[0].shape
    stride = n_freq + 1
    width = scales[0].shape[0]
    for k in range(slots):
        scale = scales[k][...].astype(jnp.float32).T
        own = owns[k][...].astype(jnp.float32).T
        mate = mates[k][...].astype(jnp.float32).T
        for h in range(2):
            coeffs = jnp.where(mine == h, own, mate)
            for at in range(0, rows, width):
                v = (h * rows + at) // width
                number = scale[v * stride + n_freq : v * stride + n_freq + 1, :]
                for f in range(n_freq):
                    one = scale[v * stride + f : v * stride + f + 1, :] * number
                    out[k, f * columns : (f + 1) * columns, h * rows + at : h * rows + at + width] = (
                        coeffs[:, at : at + width] * one
                    ).astype(jnp.bfloat16)


def chi_kernel(early, late, n_freq, factor, scalars, *refs):
    slots = early + late
    owns = refs[:slots]
    mates = refs[slots : 2 * slots]
    scales = refs[2 * slots : 3 * slots]
    rights_a = refs[3 * slots : 3 * slots + 4]
    rights_b = refs[3 * slots + 4 : -2]
    out, weighted = refs[-2:]
    columns = out.shape[0]

    @pl.when(pl.program_id(0) == 0)
    def _():
        weigh(owns, mates, scales, scalars[4], n_freq, weighted)

    core = scalars[2]
    same_y = scalars[1] == lax.rem(pl.program_id(0), 2)
    shift = lax.bitwise_xor(scalars[0], scalars[3] + pl.program_id(0) // 2)
    left, right = [], []
    for r in range(slots):
        left.append(weighted[lax.bitwise_xor(shift, r)])
        for h in range(2):
            if r < early:
                pair = [rights_a[2 * h + c][0, r] for c in range(2)]
            else:
                own, other, mate, both = [rights_b[8 * (r - early) + 4 * h + q][0] for q in range(4)]
                own = jnp.where(same_y, own, other)
                mate = jnp.where(same_y, mate, both)
                pair = [jnp.where(core == c, own, mate) for c in range(2)]
            right.append(jnp.concatenate(pair, axis=1))
    chi = jnp.dot(
        jnp.concatenate(left, axis=1),
        jnp.concatenate(right, axis=0),
        preferred_element_type=jnp.float32,
    )
    for f in range(n_freq):
        out[:, f, :] = chi[f * columns : (f + 1) * columns, :] * factor


def make_chi(owns, mates, units, right_a, rights_b, scalars, n_freq, factor):
    members, early, rows, columns = right_a.shape
    tiles = members // 4
    late = len(rights_b)
    slots = early + late
    width = units[0].shape[0]
    last = units[0].shape[1] // LANES - 1
    flops = 4 * slots * rows * n_freq * columns * tiles * 2 * columns

    def near(h, i, scalars):
        return (lax.bitwise_xor(scalars[0], h * 2 + i // 2), 0, 0)

    return pl.pallas_call(
        functools.partial(chi_kernel, early, late, n_freq, factor),
        out_shape=jax.ShapeDtypeStruct((columns, n_freq, tiles * 2 * columns), jnp.float32),
        grid_spec=pltpu.PrefetchScalarGridSpec(
            num_scalar_prefetch=1,
            grid=(tiles,),
            in_specs=[pl.BlockSpec((rows, columns), lambda i, scalars: (0, 0))] * (2 * slots)
            + [pl.BlockSpec((width, LANES), lambda i, scalars: (0, last))] * slots
            + [
                pl.BlockSpec(
                    (1, early, rows, columns),
                    functools.partial(
                        lambda h, c, i, scalars: (h * tiles * 2 + i * 2 + c, 0, 0, 0), h, c
                    ),
                )
                for h in range(2)
                for c in range(2)
            ]
            + [
                pl.BlockSpec((1, rows, columns), functools.partial(near, h))
                for r in range(late)
                for h in range(2)
                for q in range(4)
            ],
            out_specs=pl.BlockSpec((columns, n_freq, 2 * columns), lambda i, scalars: (0, 0, i)),
            scratch_shapes=[pltpu.VMEM((slots, n_freq * columns, 2 * rows), jnp.bfloat16)],
        ),
        compiler_params=pltpu.CompilerParams(vmem_limit_bytes=32 * 1024 * 1024),
        cost_estimate=pl.CostEstimate(
            flops=flops,
            bytes_accessed=2 * (early + late) * members * rows * columns
            + 4 * columns * n_freq * tiles * 2 * columns,
            transcendentals=0,
        ),
        name="chi",
    )(scalars, *owns, *mates, *units, *([right_a] * 4), *[a for four in rights_b for a in four * 2])


def fast(shape, unit, eigenvectors, part, val_count, cond_count, n_freq, factor):
    nz, ny, nc, nx = shape
    z, y, c, x = [lax.axis_index(name).astype(jnp.int32) for name in AXES]
    columns = eigenvectors.shape[1]
    places = [(i, j, k, t) for i in range(nz) for j in range(ny) for k in range(nc) for t in range(nx)]
    number = {place: at for at, place in enumerate(places)}

    def send(array, target):
        pairs = [(number[place], target(*place)) for place in places]
        return lax.ppermute(
            array, AXES, [(source, number[to]) for source, to in pairs if to is not None]
        )

    def along_z(array, moves):
        moves = dict(moves)
        return send(array, lambda i, j, k, t: (moves[i], j, k, t) if i in moves else None)

    here = y * nc + c
    eigs = [
        lax.dynamic_slice_in_dim(eigenvectors, lax.bitwise_xor(here, k) * part, part, 0)
        for k in range(ny * nc)
    ]
    unit, eigs = lax.optimization_barrier((unit, eigs))
    for q in range(1, ny * nc):
        eigs[q] = send(
            eigs[q], functools.partial(lambda q, i, j, k, t: (i, j ^ (q // 2), k ^ (q % 2), t), q)
        )

    inner = (z == 1) | (z == 2)
    near = along_z(unit, [(0, 1), (1, 0), (2, 3), (3, 2)])
    middle = along_z(unit, [(1, 2), (2, 1)])
    across = along_z(near, [(1, 2), (2, 1)])
    outward = along_z(middle, [(1, 0), (2, 3)])
    far = along_z(across, [(1, 0), (2, 3)])
    units = [unit, near, jnp.where(inner, across, outward)]

    place = x[None]

    def coefficients(unit, ready=None):
        keep, away = project(unit, eigs, place, val_count, cond_count)
        sums = keep + send(away, lambda i, j, k, t: (i, j, 1 - k, t))
        if ready is not None:
            sums, _ = lax.optimization_barrier((sums, ready))
        total = sums[0, 0] + send(sums[0, 1], lambda i, j, k, t: (i, j, k, 1 - t))
        total = total + send(sums[1, 0], lambda i, j, k, t: (i, 1 - j, k, t))
        total = total + send(sums[1, 1], lambda i, j, k, t: (i, 1 - j, k, 1 - t))
        return total.astype(jnp.bfloat16)

    def mate(own):
        return send(own, lambda i, j, k, t: (i, j, k, 1 - t))

    def share(own, m):
        return send(own, lambda i, j, k, t: ((2 * t + i % 2) ^ m, j, k, i // 2))

    def spread(own):
        shares = [share(own, m) for m in range(nz)]
        shares, paired = lax.optimization_barrier((shares, mate(own)))
        held = jnp.stack(shares)
        other = send(held, lambda i, j, k, t: (i, 1 - j, k, t))
        across_core = lambda i, j, k, t: (i, j, 1 - k, t)
        return (held, other, send(held, across_core), send(other, across_core)), paired

    owns = [coefficients(units[0], (across, outward))] + [coefficients(units[k]) for k in (1, 2)]
    own_a = jnp.stack(owns)
    share_a, mate_a, far = lax.optimization_barrier((share(own_a, 0), mate(own_a), far))
    right_a = lax.all_gather(share_a, ("z", "y", "c"), axis=0)
    units.append(jnp.where(inner, middle, far))
    own_b = coefficients(units[3])
    four, mate_b = spread(own_b)
    owns.append(own_b)
    mates = [mate_a[k] for k in range(3)] + [mate_b]
    rights_b = [four]
    scalars = jnp.stack([z, y, c, 2 * x, x])
    return make_chi(owns, mates, units, right_a, rights_b, scalars, n_freq, factor)


def plain(shape, unit, eigenvectors, part, val_count, cond_count, n_freq, factor):
    nz, ny, nc, nx = shape
    z = lax.axis_index("z").astype(jnp.int32)
    x = lax.axis_index("x").astype(jnp.int32)
    group = ny * nc
    n_parts = group * nx
    segs = cond_count // val_count
    seg = part // segs
    columns = eigenvectors.shape[1]
    zfold = nz // nx
    eigs = lax.all_to_all(
        eigenvectors.reshape(group, part, columns), ("y", "c"), 0, 0, tiled=True
    )
    every = lax.all_gather(unit, "z", axis=0)

    def coefficients(unit):
        cond = unit[:, :part].reshape(1, n_parts, cond_count, segs, seg)
        val = unit[:, part : part + seg].reshape(n_parts, segs, val_count, seg)
        val = val.transpose(2, 0, 1, 3)[:, :, None]
        density = (cond.astype(jnp.float32) * val.astype(jnp.float32)).astype(jnp.bfloat16)
        sums = jnp.einsum(
            "pg,qgs->qps", density.reshape(-1, part), eigs, preferred_element_type=jnp.float32
        )
        sums = sums.reshape(n_parts, -1, columns)
        sums = lax.all_to_all(sums, ("y", "c", "x"), 0, 0, tiled=True)
        return jnp.sum(sums, axis=0).astype(jnp.bfloat16)

    own = jnp.stack([coefficients(every[k]) for k in range(nz)])
    lefts = lax.all_gather(own, "x", axis=0)
    perm = []
    for s in range(nz):
        for q in range(group):
            for t in range(nx):
                target = ((s % zfold + zfold * t) * group + q) * nx + s // zfold
                perm.append(((s * group + q) * nx + t, target))
    share = lax.ppermute(own, AXES, perm)
    right = lax.all_gather(share, ("z", "y", "c"), axis=0)
    rows = own.shape[1]
    total = 0.0
    for k in range(nz):
        scale = every[k][:, part + seg : part + seg + val_count * (n_freq + 1)].astype(jnp.float32)
        scale = scale.reshape(n_parts * cond_count, val_count, n_freq + 1).transpose(1, 0, 2)
        scale = scale.reshape(nx, rows, n_freq + 1)
        scale = scale[..., :n_freq] * scale[..., n_freq:]
        weighted = (lefts[:, k, :, :, None].astype(jnp.float32) * scale[:, :, None, :]).astype(
            jnp.bfloat16
        )
        weighted = weighted.reshape(nx * rows, columns * n_freq)
        piece = right[:, k].reshape(nx, zfold * group, rows, columns)
        piece = piece.transpose(0, 2, 1, 3).reshape(nx * rows, zfold * group * columns)
        total = total + lax.dot_general(
            weighted, piece, (((0,), (0,)), ((), ())), preferred_element_type=jnp.float32
        )
    return (total * factor).reshape(columns, n_freq, zfold * group * columns)


def local(
    shape,
    val_orbitals,
    cond_orbitals,
    val_energy,
    cond_energy,
    val_slot,
    cond_slot,
    eigenvectors,
    frequencies,
):
    nz, ny, nc, nx = shape
    val_count, n_grid = val_orbitals.shape
    cond_count = cond_orbitals.shape[0]
    n_parts = ny * nc * nx
    part = n_grid // n_parts
    seg = part * val_count // cond_count
    columns = eigenvectors.shape[1]
    factor = -1.0 / math.sqrt(val_slot.shape[0] * nz * n_parts)
    packed = pack(
        val_orbitals,
        cond_orbitals,
        val_energy,
        cond_energy,
        val_slot,
        cond_slot,
        frequencies,
        nx,
        ny * nc,
    )
    unit = lax.all_to_all(packed, ("y", "c", "x"), 0, 0, tiled=True)
    unit = unit.reshape(n_parts * cond_count, part + seg + LANES)
    on_tiles = columns % LANES == 0 and seg % LANES == 0
    run = fast if on_tiles and nx == 2 and nz == 4 and val_count == 4 else plain
    return run(
        shape, unit, eigenvectors, part, val_count, cond_count, frequencies.shape[0], factor
    )


def solution(mesh):
    n_pair = mesh.shape["pair"]
    n_proj = mesh.shape["proj"]
    shape = (n_pair // 4, 2, 2, n_proj)
    grid = Mesh(mesh.devices.reshape(shape), AXES)
    return jax.shard_map(
        functools.partial(local, shape),
        mesh=grid,
        in_specs=(
            P(AXES, None),
            P(AXES, None),
            P(AXES),
            P(AXES),
            P(AXES),
            P(AXES),
            P("x", ("z", "y", "c")),
            P(),
        ),
        out_specs=P(("z", "y", "c"), None, "x"),
        check_vma=False,
    )
```
